32 devices in a mesh: members: 2 (over x), band: 16 (over z, y, core).
Axes of the slice: x: 2, y: 2, z: 4, core: 2. Of those that a mesh axis runs over, the one named last changes fastest.
Arguments:
- queries: bfloat16 [8192, 1024], P(('members', 'band')), parts along dimension 0, may hold values from -32 to 32
- keys: bfloat16 [8192, 1024], P(('members', 'band')), parts along dimension 0, may hold values from -16 to 16
- values: bfloat16 [8192, 1024], P(('members', 'band')), parts along dimension 0, may hold values from -6 to 6
- grad_out: bfloat16 [8192, 1024], P(('members', 'band')), parts along dimension 0, may hold values from -6 to 6
- windows: int32 [4096, 2], P('band'), may hold values from 0 to 4096, as said below
Outputs:
- attended: bfloat16 [8192, 1024], P(('members', 'band')), parts along dimension 0
- grad_queries: bfloat16 [8192, 1024], P(('members', 'band')), parts along dimension 0
- grad_keys: bfloat16 [8192, 1024], P(('members', 'band')), parts along dimension 0
- grad_values: bfloat16 [8192, 1024], P(('members', 'band')), parts along dimension 0
The draws below stay inside these ranges and needn't reach their ends.
There are 2 independent parts, one for each index of `members`. The reference program is written for one: setup_inputs(seed, part) draws one part's arguments, and reference() takes and returns one part's arrays. A program takes and returns all parts, laid end to end along the dimension named above; an argument that names none is the same for every part. Nothing has to cross between parts.
Inputs may be any that keep to these rules, and one draw needn't show every extreme that they name: `windows`: points are ordered by latitude rows of 1 to 100 points, growing from each pole toward the middle of the grid. A point's window runs from the first point of the row before its own to the last point of the row after its own (only its own row's side where it lies in the first or last row); so every window holds its own point, and no key lies more than 199 points before or after the point; both distances are reached.
All inputs are finite; a program needn't handle non-finite values.
Results may differ from the reference program's by a relative error of at most 0.018.
Values may be sent and summed in bfloat16 or wider, within the bound.
No kernel may reach another device: no remote copies, remote signals or barrier semaphores. Data moves between devices by JAX's collectives and lax.ppermute only.
A program may use at most 128 MiB of HBM per device.

```python
import jax
import jax.numpy as jnp
from jax import lax

D = 1024
HEADS = 16
HEAD_DIM = 64
P_DEV = 256
ROWMIN = 20
STEP = 4
TOKENS = 4096
ROWMAX = 100
HALO = 200


def pair_fields(key):
    part_keys = jax.random.split(key, 2)
    shape = (TOKENS, D)
    normal_q = jnp.clip(jax.random.normal(part_keys[0], shape, jnp.float32), -4.0, 4.0)
    normal_k = jnp.clip(jax.random.normal(part_keys[1], shape, jnp.float32), -4.0, 4.0)
    field_q = normal_q
    field_k = normal_k
    rows = jnp.arange(TOKENS, dtype=jnp.int32)
    marked = (rows % 61 == 0) & (rows < TOKENS - 1)
    marked_prev = jnp.roll(marked, 1)
    keys_new = jnp.where(marked[:, None], field_k, field_k)
    keys_new = jnp.where(marked_prev[:, None], keys_new, keys_new)
    queries_new = jnp.where(marked[:, None], field_q, field_q)
    return (queries_new, keys_new)


def draw_queries(key, part):
    fields = pair_fields(key)
    return fields[0].astype(jnp.bfloat16)


def draw_keys(key, part):
    fields = pair_fields(key)
    return fields[1].astype(jnp.bfloat16)


def draw_windows(key, part):
    key = jax.random.fold_in(key, 7)
    middle = TOKENS // 2
    count = middle // ROWMIN + 2
    jitter = jax.random.randint(key, (count,), 0, STEP + 1, dtype=jnp.int32)
    lengths = jnp.minimum(ROWMAX, ROWMIN + STEP * jnp.arange(count, dtype=jnp.int32) + jitter)
    starts = jnp.concatenate([jnp.zeros((1,), jnp.int32), jnp.cumsum(lengths).astype(jnp.int32)])[:count]
    north = jnp.minimum(starts, middle)
    south = TOKENS - north
    bounds = jnp.sort(jnp.concatenate([north, south, jnp.full((1,), TOKENS, jnp.int32)]))
    total = bounds.shape[0]
    points = jnp.arange(TOKENS, dtype=jnp.int32)
    after = jnp.searchsorted(bounds, points, side='right').astype(jnp.int32)
    row_start = bounds[after - 1]
    row_end = bounds[jnp.minimum(after, total - 1)]
    before_at = jnp.searchsorted(bounds, jnp.maximum(row_start - 1, 0), side='right').astype(jnp.int32)
    lower = jnp.where(row_start > 0, bounds[jnp.maximum(before_at - 1, 0)], 0)
    next_at = jnp.searchsorted(bounds, row_end, side='right').astype(jnp.int32)
    upper = jnp.where(row_end < TOKENS, bounds[jnp.minimum(next_at, total - 1)], TOKENS)
    return jnp.stack([lower, upper], axis=1).astype(jnp.int32)


def steps_of(stream_key, dims, cuts, smallest, top_value):
    factor_of, own = 1.0, jax.random.fold_in(stream_key, 6)
    for axis_at, blocks in cuts:
        draws = jnp.exp(jax.random.uniform(jax.random.fold_in(own, axis_at), (blocks,), jnp.float32, smallest / len(cuts), top_value / len(cuts)))
        factor_of = factor_of * jnp.repeat(draws, dims[axis_at] // blocks).reshape([-1 if axis == axis_at else 1 for axis in range(len(dims))])
    return factor_of


def centred(rng, extent, width, limit, shards=(), kind=jnp.bfloat16):
    loudness = steps_of(rng, extent, shards, -0.22, 0.18) if shards else 1.0
    result = jax.random.normal(rng, extent, jnp.float32) * width * loudness
    return jnp.minimum(jnp.maximum(result, -limit), limit).astype(kind)


def setup_inputs(seed: int = 0, part: int = 0) -> dict:
    arg_keys = jax.random.split(jax.random.key(seed), 6)
    part_splits = jax.random.split(jax.random.fold_in(arg_keys[5], part), 6)
    return {
        "queries": draw_queries(jax.random.fold_in(jax.random.fold_in(arg_keys[5], part), 71), part),
        "keys": draw_keys(jax.random.fold_in(jax.random.fold_in(arg_keys[5], part), 71), part),
        "values": centred(part_splits[2], (TOKENS, D), 1.0, 6.0, ((0, 16),)),
        "grad_out": centred(part_splits[3], (TOKENS, D), 1.0, 6.0, ((0, 16),)),
        "windows": draw_windows(jax.random.fold_in(arg_keys[5], 71), part),
    }


def core(qb, kb, vb, gb, lower, upper, key_first):
    rows = qb.shape[0]
    cols_n = kb.shape[0]
    scale = HEAD_DIM ** -0.5
    qh = qb.astype(jnp.float32).reshape(rows, HEADS, HEAD_DIM)
    kh = kb.astype(jnp.float32).reshape(cols_n, HEADS, HEAD_DIM)
    vh = vb.astype(jnp.float32).reshape(cols_n, HEADS, HEAD_DIM)
    gh = gb.astype(jnp.float32).reshape(rows, HEADS, HEAD_DIM)
    scores = jnp.einsum('rhe,che->hrc', qh, kh) * scale
    cols = key_first + jnp.arange(cols_n, dtype=jnp.int32)
    inside = (cols[None, :] >= lower[:, None]) & (cols[None, :] < upper[:, None])
    scores = jnp.where(inside[None], scores, -jnp.inf)
    top = jnp.max(scores, axis=-1, keepdims=True)
    lse = top + jnp.log(jnp.sum(jnp.exp(scores - top), axis=-1, keepdims=True))
    probs = jnp.exp(scores - lse)
    probs_low = probs.astype(jnp.bfloat16).astype(jnp.float32)
    attended = jnp.einsum('hrc,che->rhe', probs_low, vh).astype(jnp.bfloat16)
    delta = jnp.sum(gh * attended.astype(jnp.float32), axis=-1).T
    dprobs = jnp.einsum('rhe,che->hrc', gh, vh)
    dscores = (probs * (dprobs - delta[:, :, None])).astype(jnp.bfloat16).astype(jnp.float32)
    grad_q = (jnp.einsum('hrc,che->rhe', dscores, kh) * scale).astype(jnp.bfloat16)
    grad_k = jnp.einsum('hrc,rhe->che', dscores, qh) * scale
    grad_v = jnp.einsum('hrc,rhe->che', probs_low, gh)
    return (attended.reshape(rows, D), grad_q.reshape(rows, D),
            grad_k.reshape(cols_n, D), grad_v.reshape(cols_n, D))


def reference(queries, keys, values, grad_out, windows):
    border = jnp.zeros((HALO, D), jnp.bfloat16)
    keys_wide = jnp.concatenate([border, keys, border], axis=0)
    values_wide = jnp.concatenate([border, values, border], axis=0)
    blocks = TOKENS // P_DEV
    span = P_DEV + 2 * HALO

    def step(carry, index):
        key_acc, value_acc = carry
        first = index * P_DEV
        qb = lax.dynamic_slice_in_dim(queries, first, P_DEV, 0)
        gb = lax.dynamic_slice_in_dim(grad_out, first, P_DEV, 0)
        kb = lax.dynamic_slice_in_dim(keys_wide, first, span, 0)
        vb = lax.dynamic_slice_in_dim(values_wide, first, span, 0)
        wb = lax.dynamic_slice_in_dim(windows, first, P_DEV, 0)
        attended, grad_q, grad_k, grad_v = core(qb, kb, vb, gb, wb[:, 0], wb[:, 1], first - HALO)
        key_acc = lax.dynamic_update_slice_in_dim(
            key_acc, lax.dynamic_slice_in_dim(key_acc, first, span, 0) + grad_k, first, 0)
        value_acc = lax.dynamic_update_slice_in_dim(
            value_acc, lax.dynamic_slice_in_dim(value_acc, first, span, 0) + grad_v, first, 0)
        return (key_acc, value_acc), (attended, grad_q)

    zeros = jnp.zeros((TOKENS + 2 * HALO, D), jnp.float32)
    (key_acc, value_acc), (attended, grad_q) = lax.scan(
        step, (zeros, zeros), jnp.arange(blocks, dtype=jnp.int32))
    attended = attended.reshape(TOKENS, D)
    grad_q = grad_q.reshape(TOKENS, D)
    grad_k = key_acc[HALO:HALO + TOKENS].astype(jnp.bfloat16)
    grad_v = value_acc[HALO:HALO + TOKENS].astype(jnp.bfloat16)
    return (attended, grad_q, grad_k, grad_v)
```

```python
import functools
import math

import jax
import jax.numpy as jnp
from jax import lax
from jax.experimental import pallas as pl
from jax.experimental.pallas import tpu as pltpu
from jax.sharding import PartitionSpec as P

HEADS = 16
HEAD_DIM = 64
ROWMIN = 20
STEP = 4
PAIR = 2 * HEAD_DIM
PAIRS = HEADS // 2
SCALE = HEAD_DIM**-0.5
EXP2_SCALE = SCALE * math.log2(math.e)
OUTSIDE = -1e30
QG_CHUNKS = (0, 4, 8)
VMEM_BYTES = 40 * 2**20


def passed_along(value, steps):
    count = lax.axis_size("band")
    initial, last = (max(0, -steps), min(count, count - steps))
    return lax.ppermute(value, "band", [(source, source + steps) for source in range(initial, last)])


def reach_sizes(points, count):
    area_rows = points * count // STEP
    root_bound = min(((area_rows + 2 * 4**power) // (3 * 2**power) for power in range(3, 9)))
    grow_rows = root_bound - ROWMIN // STEP - 6
    row_longest = ROWMIN + STEP * (grow_rows - 1)
    rim_width = (2 * row_longest + 15) // 16 * 16
    return (rim_width, (rim_width + points - 1) // points)


def dot_nt(left, right):
    return lax.dot_general(
        left, right, (((1,), (1,)), ((), ())), preferred_element_type=jnp.float32
    )


def dot_nn(left, right):
    return jnp.dot(left, right, preferred_element_type=jnp.float32)


def head_masks():
    lanes = lax.broadcasted_iota(jnp.int32, (1, PAIR), 1)
    first = (lanes < HEAD_DIM).astype(jnp.float32).astype(jnp.bfloat16)
    return (first, (1.0 - first.astype(jnp.float32)).astype(jnp.bfloat16))


def own_kernel(firsts, lengths, points, *refs):
    count = len(firsts)
    win_ref, q_ref, g_ref, k_ref, v_ref = refs[:5]
    halo_refs = refs[5 : 5 + count - 1]
    att_ref, dq_ref, dk_ref, dv_ref = refs[5 + count - 1 : 9 + count - 1]
    stat_refs = refs[9 + count - 1 : 9 + 2 * (count - 1)]
    bias_ref = refs[-1]
    own = count // 2
    rows = [sum(lengths[:at]) for at in range(count)]

    @pl.when(pl.program_id(0) == 0)
    def _():
        lower = win_ref[0:1, :]
        upper = win_ref[1:2, :]
        for at in range(count):
            keys = firsts[at] + lax.broadcasted_iota(jnp.int32, (lengths[at], points), 0)
            inside = (keys >= lower) & (keys < upper)
            bias_ref[rows[at] : rows[at] + lengths[at], :] = jnp.where(inside, 0.0, OUTSIDE)

    q = q_ref[...]
    g = g_ref[...]
    ks, vs = [], []
    for at in range(count):
        if at == own:
            ks.append(k_ref[...])
            vs.append(v_ref[...])
        else:
            ref = halo_refs[at if at < own else at - 1]
            ks.append(ref[0])
            vs.append(ref[1])
    k_all = jnp.concatenate(ks, axis=0)
    v_all = jnp.concatenate(vs, axis=0)
    k_turned = k_all.T
    v_turned = v_all.T
    g_turned = g.T
    own_rows = slice(rows[own], rows[own] + points)
    att, dq, stats = [], [], []
    dk = dv = None
    for head, mask in enumerate(head_masks()):
        part = slice(head * HEAD_DIM, (head + 1) * HEAD_DIM)
        q_head = q * mask
        g_head = g * mask
        scores = dot_nt(k_all, q_head) + bias_ref[...]
        top = jnp.max(scores, axis=0, keepdims=True)
        probs = jnp.exp2((scores - top) * EXP2_SCALE)
        total = jnp.sum(probs, axis=0, keepdims=True)
        probs = probs * (1.0 / total)
        stats.append(top + jnp.log(total) * (1.0 / SCALE))
        probs_low = probs.astype(jnp.bfloat16)
        att_head = dot_nn(v_turned[part], probs_low).astype(jnp.bfloat16)
        delta = jnp.sum(
            g_turned[part].astype(jnp.float32) * att_head.astype(jnp.float32), axis=0, keepdims=True
        )
        stats.append(delta)
        dscores = (probs * (dot_nt(v_all, g_head) - delta)).astype(jnp.bfloat16)
        dq_head = (dot_nn(k_turned[part], dscores) * SCALE).astype(jnp.bfloat16)
        att.append(att_head)
        dq.append(dq_head)
        dk_head = dot_nn(dscores[own_rows], q_head)
        dv_head = dot_nn(probs_low[own_rows], g_head)
        dk = dk_head if dk is None else dk + dk_head
        dv = dv_head if dv is None else dv + dv_head
    att_ref[...] = jnp.concatenate(att, axis=0).T
    dq_ref[...] = jnp.concatenate(dq, axis=0).T
    dk_ref[...] = dk
    dv_ref[...] = dv
    stats = jnp.concatenate(stats, axis=0)
    for ref, at in zip(stat_refs, [at for at in range(count) if at != own]):
        ref[0] = stats[:, points - lengths[at] :] if at < own else stats[:, : lengths[at]]


def halo_kernel(firsts, lengths, points, *refs):
    count = len(firsts)
    win_ref, k_ref, v_ref, dk_part_ref, dv_part_ref = refs[:5]
    qg_refs = refs[5 : 5 + count]
    stat_refs = refs[5 + count : 5 + 2 * count]
    dk_ref, dv_ref = refs[-2 - count : -count]
    bias_refs = refs[-count:]
    lows = [first < 0 for first in firsts]
    starts = [0 if low else points - length for low, length in zip(lows, lengths)]

    @pl.when(pl.program_id(0) == 0)
    def _():
        for at in range(count):
            part = slice(starts[at], starts[at] + lengths[at])
            queries = firsts[at] + lax.broadcasted_iota(jnp.int32, (lengths[at], lengths[at]), 1)
            inside = (queries >= win_ref[part, 0:1]) & (queries < win_ref[part, 1:2])
            bias_refs[at][...] = jnp.where(inside, 0.0, OUTSIDE)

    dk_ref_sum = dk_part_ref[...]
    dv_ref_sum = dv_part_ref[...]
    for at in range(count):
        part = slice(starts[at], starts[at] + lengths[at])
        k = k_ref[part, :]
        v = v_ref[part, :]
        q = qg_refs[at][0]
        g = qg_refs[at][1]
        stats = stat_refs[at][0]
        dk = dv = None
        for head, mask in enumerate(head_masks()):
            q_head = q * mask
            g_head = g * mask
            lse = stats[2 * head : 2 * head + 1]
            delta = stats[2 * head + 1 : 2 * head + 2]
            scores = dot_nt(k, q_head) + bias_refs[at][...]
            probs = jnp.exp2((scores - lse) * EXP2_SCALE)
            dscores = (probs * (dot_nt(v, g_head) - delta)).astype(jnp.bfloat16)
            dk_head = dot_nn(dscores, q_head)
            dv_head = dot_nn(probs.astype(jnp.bfloat16), g_head)
            dk = dk_head if dk is None else dk + dk_head
            dv = dv_head if dv is None else dv + dv_head
        if lengths[at] < points:
            blank = jnp.zeros((points - lengths[at], PAIR), jnp.float32)
            order = (lambda x: [x, blank]) if lows[at] else (lambda x: [blank, x])
            dk = jnp.concatenate(order(dk), axis=0)
            dv = jnp.concatenate(order(dv), axis=0)
        dk_ref_sum = dk_ref_sum + dk
        dv_ref_sum = dv_ref_sum + dv
    dk_ref[...] = (dk_ref_sum * SCALE).astype(jnp.bfloat16)
    dv_ref[...] = dv_ref_sum.astype(jnp.bfloat16)


def compiler_params():
    return pltpu.CompilerParams(
        vmem_limit_bytes=VMEM_BYTES, dimension_semantics=("arbitrary",)
    )


def per_device(queries, keys, values, grad_out, windows):
    points, width = queries.shape
    rim_width, reach = reach_sizes(points, lax.axis_size("band"))
    offsets = [d for d in range(-reach, reach + 1) if d != 0]
    sizes = [min(points, rim_width - (abs(d) - 1) * points) for d in offsets]
    firsts = [(d + 1) * points - n if d < 0 else d * points for d, n in zip(offsets, sizes)]
    relative = windows - lax.axis_index("band") * points

    def edge(field, offset, size):
        return field[points - size :] if offset < 0 else field[:size]

    def fetch(fields, columns):
        return [
            passed_along(
                jnp.stack([edge(field, d, n)[:, columns] for field in fields]), -d
            )
            for d, n in zip(offsets, sizes)
        ]

    kv_halo = fetch([keys, values], slice(0, width))
    qg_halo = [
        fetch([queries, grad_out], slice(low * PAIR, high * PAIR))
        for low, high in zip(QG_CHUNKS[:-1], QG_CHUNKS[1:])
    ]

    pair_block = pl.BlockSpec((points, PAIR), lambda i: (0, i))
    own_count = len(offsets) + 1
    own_at = own_count // 2
    all_sizes = sizes[:own_at] + [points] + sizes[own_at:]
    all_firsts = firsts[:own_at] + [0] + firsts[own_at:]
    wide = sum(all_sizes)
    outs = pl.pallas_call(
        functools.partial(own_kernel, all_firsts, all_sizes, points),
        grid=(PAIRS,),
        in_specs=[pl.BlockSpec((2, points), lambda i: (0, 0))]
        + [pair_block] * 4
        + [pl.BlockSpec((2, n, PAIR), lambda i: (0, 0, i)) for n in sizes],
        out_specs=[pair_block] * 4 + [pl.BlockSpec((1, 4, n), lambda i: (i, 0, 0)) for n in sizes],
        out_shape=[
            jax.ShapeDtypeStruct((points, width), jnp.bfloat16),
            jax.ShapeDtypeStruct((points, width), jnp.bfloat16),
            jax.ShapeDtypeStruct((points, width), jnp.float32),
            jax.ShapeDtypeStruct((points, width), jnp.float32),
        ]
        + [jax.ShapeDtypeStruct((PAIRS, 4, n), jnp.float32) for n in sizes],
        scratch_shapes=[pltpu.VMEM((wide, points), jnp.float32)],
        compiler_params=compiler_params(),
        cost_estimate=pl.CostEstimate(
            flops=HEADS * 8 * points * wide * PAIR,
            bytes_accessed=2 * width * (6 * points + 2 * wide) + 8 * points * width,
            transcendentals=HEADS * points * wide,
        ),
        name="own_queries",
    )(relative.T, queries, grad_out, keys, values, *kv_halo)
    attended, grad_q, dk_part, dv_part = outs[:4]
    stats_halo = [passed_along(stat, -d) for stat, d in zip(outs[4:], offsets)]

    grads = None
    for chunk, (low, high) in enumerate(zip(QG_CHUNKS[:-1], QG_CHUNKS[1:])):
        from_low = functools.partial(lambda low, i: (0, i + low), low)
        block = pl.BlockSpec((points, PAIR), from_low)
        carried = [] if grads is None else list(grads)
        kernel = functools.partial(halo_kernel, firsts, sizes, points)
        args = [relative, keys, values, dk_part, dv_part, *qg_halo[chunk], *stats_halo]
        if carried:
            inner = kernel
            kernel = functools.partial(
                lambda inner, at, *refs: inner(*refs[:at], *refs[at + 2 :]), inner, len(args)
            )
        grads = pl.pallas_call(
            kernel,
            grid=(high - low,),
            in_specs=[pl.BlockSpec((points, 2), lambda i: (0, 0))]
            + [block] * 4
            + [pl.BlockSpec((2, n, PAIR), lambda i: (0, 0, i)) for n in sizes]
            + [
                pl.BlockSpec((1, 4, n), functools.partial(lambda low, i: (i + low, 0, 0), low))
                for n in sizes
            ]
            + [pl.BlockSpec(memory_space=pl.ANY)] * len(carried),
            out_specs=[block] * 2,
            out_shape=[jax.ShapeDtypeStruct((points, width), jnp.bfloat16)] * 2,
            input_output_aliases={len(args) + at: at for at in range(len(carried))},
            scratch_shapes=[pltpu.VMEM((n, n), jnp.float32) for n in sizes],
            compiler_params=compiler_params(),
            cost_estimate=pl.CostEstimate(
                flops=(high - low) * 2 * sum(8 * n * n * PAIR for n in sizes),
                bytes_accessed=(high - low) * PAIR * 20 * points,
                transcendentals=(high - low) * 2 * sum(n * n for n in sizes),
            ),
            name=f"halo_queries_{chunk}",
        )(*args, *carried)
    return (attended, grad_q, grads[0], grads[1])


def solution(mesh):
    spread = P(("members", "band"), None)
    return jax.shard_map(
        per_device,
        mesh=mesh,
        in_specs=(spread, spread, spread, spread, P("band", None)),
        out_specs=(spread, spread, spread, spread),
        check_vma=False,
    )
```

```python
import functools
import math

import jax
import jax.numpy as jnp
from jax import lax
from jax.experimental import pallas as pl
from jax.experimental.pallas import tpu as pltpu
from jax.sharding import PartitionSpec as P

HEADS = 16
HEAD_DIM = 64
ROWMIN = 20
STEP = 4
PAIR = 2 * HEAD_DIM
PAIRS = HEADS // 2
SCALE = HEAD_DIM**-0.5
EXP2_SCALE = SCALE * math.log2(math.e)
OUTSIDE = -1e30
KV_CHUNKS = (0, 4, 8)
QG_CHUNKS = (0, 4, 8)
VMEM_BYTES = 40 * 2**20


def reach_sizes(points, count):
    area_rows = points * count // STEP
    root_bound = min(((area_rows + 2 * 4**power) // (3 * 2**power) for power in range(3, 9)))
    grow_rows = root_bound - ROWMIN // STEP - 6
    row_longest = ROWMIN + STEP * (grow_rows - 1)
    rim_width = (2 * row_longest + 15) // 16 * 16
    return (rim_width, (rim_width + points - 1) // points)


def spans(bounds):
    return list(zip(bounds[:-1], bounds[1:]))


def passed_along(value, steps):
    count = lax.axis_size("band")
    initial, last = (max(0, -steps), min(count, count - steps))
    pairs = [(source, source + steps) for source in range(initial, last)]
    return lax.ppermute(value, "band", pairs)[None]


def swapped(value, first):
    count = lax.axis_size("band")
    groups = [sorted([at, (at + 1) % count]) for at in range(first, count, 2)]
    return lax.all_gather(value, "band", axis_index_groups=groups)


def dot_nt(left, right):
    return lax.dot_general(
        left, right, (((1,), (1,)), ((), ())), preferred_element_type=jnp.float32
    )


def dot_nn(left, right):
    return jnp.dot(left, right, preferred_element_type=jnp.float32)


def head_masks():
    lanes = lax.broadcasted_iota(jnp.int32, (1, PAIR), 1)
    first = (lanes < HEAD_DIM).astype(jnp.float32)
    return (first.astype(jnp.bfloat16), (1.0 - first).astype(jnp.bfloat16))


def pack_kernel(plan, inputs, info_ref, *refs):
    sources, targets, sems = refs[:inputs], refs[inputs:-1], refs[-1]
    copies = []
    for at, (source, start_at, columns, target, slot) in enumerate(plan):
        rows = targets[target].shape[1]
        start = pl.multiple_of(info_ref[start_at], 16)
        copies.append(
            pltpu.make_async_copy(
                sources[source].at[pl.ds(start, rows), columns], targets[target].at[slot], sems.at[at]
            )
        )
    for copy in copies:
        copy.start()
    for copy in copies:
        copy.wait()


def pack(sources, starts, buffers, name):
    plan, shapes = [], []
    for target, (rows, parts) in enumerate(buffers):
        for slot, (source, start_at, columns) in enumerate(parts):
            plan.append((source, start_at, columns, target, slot))
        width = parts[0][2].stop - parts[0][2].start
        shapes.append(jax.ShapeDtypeStruct((len(parts), rows, width), jnp.bfloat16))
    return pl.pallas_call(
        functools.partial(pack_kernel, plan, len(sources)),
        in_specs=[pl.BlockSpec(memory_space=pltpu.SMEM)]
        + [pl.BlockSpec(memory_space=pl.ANY)] * len(sources),
        out_specs=[pl.BlockSpec(memory_space=pl.ANY)] * len(shapes),
        out_shape=shapes,
        scratch_shapes=[pltpu.SemaphoreType.DMA((len(plan),))],
        cost_estimate=pl.CostEstimate(
            flops=0, bytes_accessed=sum(4 * math.prod(s.shape) for s in shapes), transcendentals=0
        ),
        name=name,
    )(starts, *sources)


def own_kernel(lengths, points, carried, info_ref, *refs):
    count = len(lengths)
    win_ref, q_ref, g_ref, k_ref, v_ref = refs[:5]
    halo_refs = refs[5 : 5 + count]
    att_ref, dq_ref, dk_ref, dv_ref, stat_ref, bias_ref = refs[5 + count + carried :]
    sizes = [points, *lengths]
    rows = [sum(sizes[:at]) for at in range(count + 1)]

    @pl.when(pl.program_id(0) == 0)
    def _():
        lower = win_ref[0:1, :]
        upper = win_ref[1:2, :]
        for at in range(count + 1):
            first = 0 if at == 0 else info_ref[2 * at - 2]
            keys = first + lax.broadcasted_iota(jnp.int32, (sizes[at], points), 0)
            inside = (keys >= lower) & (keys < upper)
            bias_ref[rows[at] : rows[at] + sizes[at], :] = jnp.where(inside, 0.0, OUTSIDE)

    q = q_ref[...]
    g = g_ref[...]
    k_all = jnp.concatenate([k_ref[...]] + [ref[0, 0] for ref in halo_refs], axis=0)
    v_all = jnp.concatenate([v_ref[...]] + [ref[0, 1] for ref in halo_refs], axis=0)
    k_turned = k_all.T
    v_turned = v_all.T
    g_turned = g.T
    att, dq, stats = [], [], []
    dk = dv = None
    for head, mask in enumerate(head_masks()):
        part = slice(head * HEAD_DIM, (head + 1) * HEAD_DIM)
        q_head = q * mask
        g_head = g * mask
        scores = dot_nt(k_all, q_head) + bias_ref[...]
        top = jnp.max(scores, axis=0, keepdims=True)
        probs = jnp.exp2((scores - top) * EXP2_SCALE)
        total = jnp.sum(probs, axis=0, keepdims=True)
        probs = probs * (1.0 / total)
        stats.append(top + jnp.log(total) * (1.0 / SCALE))
        probs_low = probs.astype(jnp.bfloat16)
        att_head = dot_nn(v_turned[part], probs_low).astype(jnp.bfloat16)
        delta = jnp.sum(
            g_turned[part].astype(jnp.float32) * att_head.astype(jnp.float32), axis=0, keepdims=True
        )
        stats.append(delta)
        dscores = (probs * (dot_nt(v_all, g_head) - delta)).astype(jnp.bfloat16)
        dq_head = (dot_nn(k_turned[part], dscores) * SCALE).astype(jnp.bfloat16)
        att.append(att_head)
        dq.append(dq_head)
        dk_head = dot_nn(dscores[:points], q_head)
        dv_head = dot_nn(probs_low[:points], g_head)
        dk = dk_head if dk is None else dk + dk_head
        dv = dv_head if dv is None else dv + dv_head
    att_ref[...] = jnp.concatenate(att, axis=0).T
    dq_ref[...] = jnp.concatenate(dq, axis=0).T
    dk_ref[...] = dk
    dv_ref[...] = dv
    stat_ref[0] = jnp.concatenate(stats, axis=0)


def halo_kernel(lengths, points, carried, info_ref, *refs):
    count = len(lengths)
    win_ref, k_ref, v_ref, dk_part_ref, dv_part_ref = refs[:5]
    qg_refs = refs[5 : 5 + count]
    stat_refs = refs[5 + count : 5 + 2 * count]
    refs = refs[5 + 2 * count + carried :]
    dk_ref, dv_ref, dk_sum, dv_sum = refs[:4]
    bias_refs = refs[4:]
    firsts = [info_ref[2 * at] for at in range(count)]
    parts = [
        pl.ds(pl.multiple_of(jnp.where(first < 0, 0, points - length), 16), length)
        for first, length in zip(firsts, lengths)
    ]

    @pl.when(pl.program_id(0) == 0)
    def _():
        for at in range(count):
            queries = firsts[at] + lax.broadcasted_iota(jnp.int32, (lengths[at], lengths[at]), 1)
            window = win_ref[parts[at], :]
            inside = (queries >= window[:, 0:1]) & (queries < window[:, 1:2])
            bias_refs[at][...] = jnp.where(inside, 0.0, OUTSIDE)

    dk_sum[...] = dk_part_ref[...]
    dv_sum[...] = dv_part_ref[...]
    for at in range(count):
        k = k_ref[parts[at], :]
        v = v_ref[parts[at], :]
        q = qg_refs[at][0, 0]
        g = qg_refs[at][0, 1]
        stats = stat_refs[at][0, 0]
        stats = jnp.where(firsts[at] < 0, stats[:, points - lengths[at] :], stats[:, : lengths[at]])
        dk = dv = None
        for head, mask in enumerate(head_masks()):
            q_head = q * mask
            g_head = g * mask
            lse = stats[2 * head : 2 * head + 1]
            delta = stats[2 * head + 1 : 2 * head + 2]
            scores = dot_nt(k, q_head) + bias_refs[at][...]
            probs = jnp.exp2((scores - lse) * EXP2_SCALE)
            dscores = (probs * (dot_nt(v, g_head) - delta)).astype(jnp.bfloat16)
            dk_head = dot_nn(dscores, q_head)
            dv_head = dot_nn(probs.astype(jnp.bfloat16), g_head)
            dk = dk_head if dk is None else dk + dk_head
            dv = dv_head if dv is None else dv + dv_head
        dk_sum[parts[at], :] += dk
        dv_sum[parts[at], :] += dv
    dk_ref[...] = (dk_sum[...] * SCALE).astype(jnp.bfloat16)
    dv_ref[...] = dv_sum[...].astype(jnp.bfloat16)


def chunk_call(kernel, info, args, in_specs, carried, out_specs, out_shape, **options):
    in_specs = in_specs + [pl.BlockSpec(memory_space=pl.ANY)] * len(carried)
    grid, scratch = options.pop("grid"), options.pop("scratch_shapes")
    return pl.pallas_call(
        functools.partial(kernel, len(carried)),
        grid_spec=pltpu.PrefetchScalarGridSpec(
            num_scalar_prefetch=1,
            grid=grid,
            in_specs=in_specs,
            out_specs=out_specs,
            scratch_shapes=scratch,
        ),
        out_shape=out_shape,
        input_output_aliases={1 + len(args) + at: at for at in range(len(carried))},
        compiler_params=pltpu.CompilerParams(
            vmem_limit_bytes=VMEM_BYTES, dimension_semantics=("arbitrary",)
        ),
        **options,
    )(info, *args, *carried)


def chunk_of(chunks, pair):
    return next(at for at, (low, high) in enumerate(spans(chunks)) if low <= pair < high)


def per_device(queries, keys, values, grad_out, windows):
    points, width = queries.shape
    rim_width, reach = reach_sizes(points, lax.axis_size("band"))
    band = lax.axis_index("band")
    parity = band % 2
    near = min(points, rim_width)
    relative = windows - band * points
    columns = [slice(low * PAIR, high * PAIR) for low, high in spans(KV_CHUNKS)]
    g_columns = [slice(low * PAIR, high * PAIR) for low, high in spans(QG_CHUNKS)]
    every = slice(0, width)

    starts = jnp.stack([(1 - parity) * (points - near), parity * (points - near)])
    next_kv = pack(
        [keys, values], starts, [(near, [(0, 1, c), (1, 1, c)]) for c in columns], "pack_next_kv"
    )
    other = pack(
        [keys, values, queries, grad_out],
        starts,
        [(near, [(at, 0, every) for at in range(4)])]
        + [(near, [(2, 1, c), (3, 1, c)]) for c in g_columns],
        "pack_other",
    )
    next_kv = [swapped(piece, 1) for piece in next_kv]
    partner = swapped(other[0], 0)
    next_qg = [swapped(piece, 1) for piece in other[1:]]
    partner_first = jnp.where(parity == 0, points, -near)
    next_first = jnp.where(parity == 0, -near, points)
    sizes = [near, near]
    info = [partner_first, 1 - parity, next_first, parity]
    far = [d for d in range(-reach, reach + 1) if abs(d) > 1]
    far_kvqg = []
    for d in far:
        size = min(points, rim_width - (abs(d) - 1) * points)
        part = slice(points - size, points) if d < 0 else slice(0, size)
        both = jnp.stack([field[part] for field in (keys, values, queries, grad_out)])
        far_kvqg.append(passed_along(both, -d))
        sizes.append(size)
        info += [(d + 1) * points - size if d < 0 else d * points, 0]
    info = jnp.stack([jnp.asarray(x, jnp.int32) for x in info])
    wide = points + sum(sizes)

    def offset_block(low):
        return pl.BlockSpec((points, PAIR), lambda i, info: (0, i + low))

    def piece_block(at, rows, half, low):
        return pl.BlockSpec(
            (1, 2, rows, PAIR), lambda i, info: (info[2 * at + 1], half, 0, i + low)
        )

    whole_shape = jax.ShapeDtypeStruct((points, width), jnp.bfloat16)
    own_outs, dk_parts, dv_parts, stats = [], [], [], []
    for chunk, (low, high) in enumerate(spans(KV_CHUNKS)):
        block, local = offset_block(low), offset_block(0)
        count = high - low
        own_outs = chunk_call(
            lambda carried, *refs: own_kernel(sizes, points, carried, *refs),
            info,
            [relative.T, queries, grad_out, keys, values, partner, next_kv[chunk], *far_kvqg],
            [pl.BlockSpec((2, points), lambda i, info: (0, 0))]
            + [block] * 4
            + [piece_block(0, near, 0, low), piece_block(1, near, 0, 0)]
            + [piece_block(2 + at, sizes[2 + at], 0, low) for at in range(len(far))],
            own_outs[:2],
            [block, block, local, local, pl.BlockSpec((1, 4, points), lambda i, info: (i, 0, 0))],
            [whole_shape] * 2
            + [jax.ShapeDtypeStruct((points, count * PAIR), jnp.float32)] * 2
            + [jax.ShapeDtypeStruct((count, 4, points), jnp.float32)],
            grid=(count,),
            scratch_shapes=[pltpu.VMEM((wide, points), jnp.float32)],
            cost_estimate=pl.CostEstimate(
                flops=count * 16 * points * wide * PAIR,
                bytes_accessed=count * PAIR * (12 * points + 4 * wide + 8 * points),
                transcendentals=2 * count * points * wide,
            ),
            name=f"own_queries_{chunk}",
        )
        dk_parts.append(own_outs[2])
        dv_parts.append(own_outs[3])
        stats.append(own_outs[4])
    stats = jnp.concatenate(stats, axis=0)
    stats = [swapped(stats, 0), swapped(stats, 1)] + [passed_along(stats, -d) for d in far]

    grads = []
    for chunk, (low, high) in enumerate(spans(QG_CHUNKS)):
        block = offset_block(low)
        count = high - low
        of_own = chunk_of(KV_CHUNKS, low)
        part_block = offset_block(low - KV_CHUNKS[of_own])

        def stat_block(at, low=low):
            return pl.BlockSpec(
                (1, 1, 4, points), lambda i, info: (info[2 * at + 1], i + low, 0, 0)
            )

        grads = chunk_call(
            lambda carried, *refs: halo_kernel(sizes, points, carried, *refs),
            info,
            [relative, keys, values, dk_parts[of_own], dv_parts[of_own]]
            + [partner, next_qg[chunk], *far_kvqg, *stats],
            [pl.BlockSpec((points, 2), lambda i, info: (0, 0)), block, block]
            + [part_block] * 2
            + [piece_block(0, near, 1, low), piece_block(1, near, 0, 0)]
            + [piece_block(2 + at, sizes[2 + at], 1, low) for at in range(len(far))]
            + [stat_block(at) for at in range(len(sizes))],
            grads,
            [block] * 2,
            [whole_shape] * 2,
            grid=(count,),
            scratch_shapes=[pltpu.VMEM((points, PAIR), jnp.float32)] * 2
            + [pltpu.VMEM((n, n), jnp.float32) for n in sizes],
            cost_estimate=pl.CostEstimate(
                flops=count * 2 * sum(8 * n * n * PAIR for n in sizes),
                bytes_accessed=count * PAIR * 20 * points,
                transcendentals=count * 2 * sum(n * n for n in sizes),
            ),
            name=f"halo_queries_{chunk}",
        )
    return (own_outs[0], own_outs[1], grads[0], grads[1])


def solution(mesh):
    spread = P(("members", "band"), None)
    return jax.shard_map(
        per_device,
        mesh=mesh,
        in_specs=(spread, spread, spread, spread, P("band", None)),
        out_specs=(spread, spread, spread, spread),
        check_vma=False,
    )
```

```python
import functools
import math

import jax
import jax.numpy as jnp
from jax import lax
from jax.experimental import pallas as pl
from jax.experimental.pallas import tpu as pltpu
from jax.sharding import PartitionSpec as P

HEADS = 16
HEAD_DIM = 64
ROWMIN = 20
STEP = 4
PAIR = 2 * HEAD_DIM
PAIRS = HEADS // 2
SCALE = HEAD_DIM**-0.5
EXP2_SCALE = SCALE * math.log2(math.e)
OUTSIDE = -1e30
CHUNKS = (0, 4, 8)
VMEM_BYTES = 40 * 2**20


def reach_sizes(points, count):
    area_rows = points * count // STEP
    root_bound = min(((area_rows + 2 * 4**power) // (3 * 2**power) for power in range(3, 9)))
    grow_rows = root_bound - ROWMIN // STEP - 6
    row_longest = ROWMIN + STEP * (grow_rows - 1)
    rim_width = (2 * row_longest + 15) // 16 * 16
    return (rim_width, (rim_width + points - 1) // points)


def spans(bounds):
    return list(zip(bounds[:-1], bounds[1:]))


def passed_along(value, steps):
    count = lax.axis_size("band")
    initial, last = (max(0, -steps), min(count, count - steps))
    return lax.ppermute(value, "band", [(source, source + steps) for source in range(initial, last)])


def swapped(value, first):
    count = lax.axis_size("band")
    pairs = [(at, at + 1) for at in range(first, count - 1, 2)]
    return lax.ppermute(value, "band", pairs + [(high, low) for low, high in pairs])


def dot_nt(left, right):
    return lax.dot_general(
        left, right, (((1,), (1,)), ((), ())), preferred_element_type=jnp.float32
    )


def dot_nn(left, right):
    return jnp.dot(left, right, preferred_element_type=jnp.float32)


def head_masks():
    lanes = lax.broadcasted_iota(jnp.int32, (1, PAIR), 1)
    first = (lanes < HEAD_DIM).astype(jnp.float32)
    return (first.astype(jnp.bfloat16), (1.0 - first).astype(jnp.bfloat16))


def pack_kernel(plan, inputs, start_ref, *refs):
    for source, start_at, target, slot in plan:
        out_ref = refs[inputs + target]
        start = pl.multiple_of(start_ref[start_at], 16)
        out_ref[slot] = refs[source][pl.ds(start, out_ref.shape[1]), :]


def pack(sources, starts, buffers, low, high, name):
    points = sources[0].shape[0]
    width = (high - low) * PAIR
    plan = [
        (source, start_at, target, source)
        for target, (rows, start_at) in enumerate(buffers)
        for source in range(len(sources))
    ]
    return pl.pallas_call(
        functools.partial(pack_kernel, plan, len(sources)),
        grid=(1,),
        in_specs=[pl.BlockSpec(memory_space=pltpu.SMEM)]
        + [pl.BlockSpec((points, width), lambda i: (0, low * PAIR // width))] * len(sources),
        out_specs=[pl.BlockSpec((len(sources), rows, width), lambda i: (0, 0, 0)) for rows, _ in buffers],
        out_shape=[
            jax.ShapeDtypeStruct((len(sources), rows, width), jnp.bfloat16) for rows, _ in buffers
        ],
        cost_estimate=pl.CostEstimate(
            flops=0, bytes_accessed=4 * len(sources) * points * width, transcendentals=0
        ),
        name=name,
    )(starts, *sources)


def attention_kernel(rim, lengths, points, carried, parity_ref, *refs):
    far = len(lengths) // 2 - 1
    near = lengths[far]
    half = points // 2
    reached = half + 2 * rim
    win_ref, q_ref, g_ref, k_ref, v_ref, partner_ref, next_ref = refs[:7]
    far_refs = refs[7 : 7 + 2 * far]
    outs = refs[7 + 2 * far + carried :]
    att_ref, dq_ref, to_partner_ref, dk_ref, dv_ref, to_next_ref = outs[:6]
    to_far_refs = outs[6 : 6 + 2 * far]
    bias_ref = outs[-1]
    even = parity_ref[0] == 0

    @pl.when(pl.program_id(0) == 0)
    def _():
        for part in range(2):
            own = slice(part * half, (part + 1) * half)
            lower = jnp.concatenate([win_ref[0:1, own]] * 2, axis=1)
            upper = jnp.concatenate([win_ref[1:2, own]] * 2, axis=1)
            keys = part * half - rim + lax.broadcasted_iota(jnp.int32, (reached, points), 0)
            bias_ref[part] = jnp.where((keys >= lower) & (keys < upper), 0.0, OUTSIDE)

    def all_keys(slot, own):
        near_low = jnp.where(even, next_ref[slot], partner_ref[slot])
        near_high = jnp.where(even, partner_ref[slot], next_ref[slot])
        lows = [ref[slot] for ref in far_refs[:far]] + [near_low]
        highs = [near_high] + [ref[slot] for ref in far_refs[far:]]
        return jnp.concatenate(lows + [own] + highs, axis=0)

    k_all = all_keys(0, k_ref[...])
    v_all = all_keys(1, v_ref[...])
    k_turned = k_all.T
    v_turned = v_all.T
    g_turned = g_ref[...].T
    masks = head_masks()

    def both(turned):
        return [turned[:HEAD_DIM, :half], turned[HEAD_DIM:, half:]]

    dks, dvs = [], []
    for part in range(2):
        own = slice(part * half, (part + 1) * half)
        span = slice(part * half, part * half + reached)
        q_both = jnp.concatenate([q_ref[own, :] * mask for mask in masks], axis=0)
        g_both = jnp.concatenate([g_ref[own, :] * mask for mask in masks], axis=0)
        scores = dot_nt(k_all[span], q_both) + bias_ref[part]
        top = jnp.max(scores, axis=0, keepdims=True)
        probs = jnp.exp2((scores - top) * EXP2_SCALE)
        probs = probs * (1.0 / jnp.sum(probs, axis=0, keepdims=True))
        probs_low = probs.astype(jnp.bfloat16)
        att = [x.astype(jnp.bfloat16) for x in both(dot_nn(v_turned[:, span], probs_low))]
        delta = [
            jnp.sum(
                g_turned[head * HEAD_DIM : (head + 1) * HEAD_DIM, own].astype(jnp.float32)
                * att[head].astype(jnp.float32),
                axis=0,
                keepdims=True,
            )
            for head in range(2)
        ]
        dprobs = dot_nt(v_all[span], g_both)
        dscores = (probs * (dprobs - jnp.concatenate(delta, axis=1))).astype(jnp.bfloat16)
        dq = [(x * SCALE).astype(jnp.bfloat16) for x in both(dot_nn(k_turned[:, span], dscores))]
        att_ref[own, :] = jnp.concatenate(att, axis=0).T
        dq_ref[own, :] = jnp.concatenate(dq, axis=0).T
        dks.append(dot_nn(dscores, q_both) * SCALE)
        dvs.append(dot_nn(probs_low, g_both))

    def rows_of(sums, start, stop):
        low, high = sums
        cuts = sorted({start, stop} | {x for x in (half, reached) if start < x < stop})
        pieces = []
        for first, last in spans(cuts):
            if last <= half:
                pieces.append(low[first:last])
            elif first >= reached:
                pieces.append(high[first - half : last - half])
            else:
                pieces.append(low[first:last] + high[first - half : last - half])
        return jnp.concatenate(pieces, axis=0)

    for slot, (sums, own_ref) in enumerate([(dks, dk_ref), (dvs, dv_ref)]):
        own_ref[...] = rows_of(sums, rim, rim + points)
        near_low = rows_of(sums, rim - near, rim).astype(jnp.bfloat16)
        near_high = rows_of(sums, rim + points, rim + points + near).astype(jnp.bfloat16)
        to_partner_ref[slot] = jnp.where(even, near_high, near_low)
        to_next_ref[slot] = jnp.where(even, near_low, near_high)
        start = 0
        for at in range(far):
            ref = to_far_refs[at]
            ref[slot] = rows_of(sums, start, start + lengths[at]).astype(jnp.bfloat16)
            start += lengths[at]
        start = rim + points + near
        for at in range(far, 2 * far):
            ref = to_far_refs[at]
            ref[slot] = rows_of(sums, start, start + lengths[at + 2]).astype(jnp.bfloat16)
            start += lengths[at + 2]


def sum_kernel(far_lengths, points, carried, start_ref, *refs):
    far = len(far_lengths) // 2
    dk_ref, dv_ref, partner_ref, next_ref = refs[:4]
    far_refs = refs[4 : 4 + 2 * far]
    outs = refs[4 + 2 * far + carried :]
    total = outs[-1]
    near = partner_ref.shape[1]
    for slot, (own_ref, out_ref) in enumerate([(dk_ref, outs[0]), (dv_ref, outs[1])]):
        total[...] = own_ref[...]
        for at, ref in enumerate((partner_ref, next_ref)):
            rows = pl.ds(pl.multiple_of(start_ref[at], 16), near)
            total[rows, :] += ref[slot].astype(jnp.float32)
        for at, (ref, length) in enumerate(zip(far_refs, far_lengths)):
            rows = slice(points - length, points) if at < far else slice(0, length)
            total[rows, :] += ref[slot].astype(jnp.float32)
        out_ref[...] = total[...].astype(jnp.bfloat16)


def chunk_call(kernel, scalars, args, in_specs, carried, out_specs, out_shape, **options):
    return pl.pallas_call(
        functools.partial(kernel, len(carried)),
        in_specs=[pl.BlockSpec(memory_space=pltpu.SMEM)]
        + in_specs
        + [pl.BlockSpec(memory_space=pl.ANY)] * len(carried),
        out_specs=out_specs,
        out_shape=out_shape,
        input_output_aliases={1 + len(args) + at: at for at in range(len(carried))},
        compiler_params=pltpu.CompilerParams(
            vmem_limit_bytes=VMEM_BYTES, dimension_semantics=("arbitrary",)
        ),
        **options,
    )(scalars, *args, *carried)


def per_device(queries, keys, values, grad_out, windows):
    points, width = queries.shape
    rim_width, reach = reach_sizes(points, lax.axis_size("band"))
    band = lax.axis_index("band")
    parity = band % 2
    near = min(points, rim_width)
    far = [d for d in range(-reach, reach + 1) if abs(d) > 1]
    far_sizes = [min(points, rim_width - (abs(d) - 1) * points) for d in far]
    lows = len(far) // 2
    lengths = far_sizes[:lows] + [near, near] + far_sizes[lows:]
    wide = points + 2 * rim_width
    relative = (windows - band * points).T
    parities = parity.astype(jnp.int32).reshape(1)
    starts = jnp.stack([(1 - parity) * (points - near), parity * (points - near)]).astype(jnp.int32)

    to_next, from_next = [], []
    ready = (keys, values)
    for chunk, (low, high) in enumerate(spans(CHUNKS)):
        to_next.append(pack(ready, starts, [(near, 1)], low, high, f"pack_next_{chunk}")[0])
        from_next.append(swapped(to_next[chunk], 1))
        if chunk == 0:
            to_partner = pack(
                lax.optimization_barrier((keys, values, to_next[0]))[:2],
                starts,
                [(near, 0)],
                0,
                PAIRS,
                "pack_partner",
            )[0]
            from_partner = swapped(to_partner, 0)
            ready = lax.optimization_barrier((keys, values, from_partner))[:2]
    from_far = []
    for d, size in zip(far, far_sizes):
        part = slice(points - size, points) if d < 0 else slice(0, size)
        from_far.append(passed_along(jnp.stack([keys[part], values[part]]), -d))

    def columns(rows, low):
        return pl.BlockSpec((rows, PAIR), lambda i: (0, i + low))

    def piece(rows, low):
        return pl.BlockSpec((2, rows, PAIR), lambda i: (0, 0, i + low))

    whole = jax.ShapeDtypeStruct((points, width), jnp.bfloat16)
    reached = points // 2 + 2 * rim_width
    outs, own_terms, back_next, back_far = [], [], [], []
    for chunk, (low, high) in enumerate(spans(CHUNKS)):
        count = high - low
        chunk_width = count * PAIR
        outs = chunk_call(
            lambda carried, *refs: attention_kernel(rim_width, lengths, points, carried, *refs),
            parities,
            [relative, queries, grad_out, keys, values, from_partner, from_next[chunk], *from_far],
            [pl.BlockSpec((2, points), lambda i: (0, 0))]
            + [columns(points, low)] * 4
            + [piece(near, low), piece(near, 0)]
            + [piece(size, low) for size in far_sizes],
            outs[:3],
            [columns(points, low)] * 2
            + [piece(near, low)]
            + [columns(points, 0)] * 2
            + [piece(near, 0)]
            + [piece(size, 0) for size in far_sizes],
            [whole] * 2
            + [jax.ShapeDtypeStruct((2, near, width), jnp.bfloat16)]
            + [jax.ShapeDtypeStruct((points, chunk_width), jnp.float32)] * 2
            + [
                jax.ShapeDtypeStruct((2, size, chunk_width), jnp.bfloat16)
                for size in [near] + far_sizes
            ],
            grid=(count,),
            scratch_shapes=[pltpu.VMEM((2, reached, points), jnp.float32)],
            cost_estimate=pl.CostEstimate(
                flops=count * 24 * reached * points * PAIR,
                bytes_accessed=count * PAIR * (20 * points + 8 * wide),
                transcendentals=2 * count * points * reached,
            ),
            name=f"attention_{chunk}",
        )
        own_terms.append(outs[3:5])
        back_next.append(swapped(outs[5], 1))
        back_far.append([passed_along(term, d) for term, d in zip(outs[6:], far)])
    back_partner = swapped(outs[2], 0)

    grads = []
    for chunk, (low, high) in enumerate(spans(CHUNKS)):
        chunk_width = (high - low) * PAIR
        step = 2 * PAIR

        def sums(rows, low):
            return pl.BlockSpec((rows, step), lambda i: (0, i + low * PAIR // step))

        def terms(rows, low):
            return pl.BlockSpec((2, rows, step), lambda i: (0, 0, i + low * PAIR // step))

        grads = chunk_call(
            lambda carried, *refs: sum_kernel(far_sizes, points, carried, *refs),
            starts,
            [*own_terms[chunk], back_partner, back_next[chunk], *back_far[chunk]],
            [sums(points, 0)] * 2
            + [terms(near, low), terms(near, 0)]
            + [terms(size, 0) for size in far_sizes],
            grads,
            [sums(points, low)] * 2,
            [whole] * 2,
            grid=(chunk_width // step,),
            scratch_shapes=[pltpu.VMEM((points, step), jnp.float32)],
            cost_estimate=pl.CostEstimate(
                flops=6 * points * chunk_width,
                bytes_accessed=20 * points * chunk_width,
                transcendentals=0,
            ),
            name=f"gradient_sums_{chunk}",
        )
    return (outs[0], outs[1], grads[0], grads[1])


def solution(mesh):
    spread = P(("members", "band"), None)
    return jax.shard_map(
        per_device,
        mesh=mesh,
        in_specs=(spread, spread, spread, spread, P("band", None)),
        out_specs=(spread, spread, spread, spread),
        check_vma=False,
    )
```

```python
import functools
import math

import jax
import jax.numpy as jnp
from jax import lax
from jax.experimental import pallas as pl
from jax.experimental.pallas import tpu as pltpu
from jax.sharding import PartitionSpec as P

HEADS = 16
HEAD_DIM = 64
ROWMIN = 20
STEP = 4
PAIR = 2 * HEAD_DIM
PAIRS = HEADS // 2
SCALE = HEAD_DIM**-0.5
LOG2_E = math.log2(math.e)
BLOCK = 32
OUTSIDE = -1e30
CHUNKS = (0, 4, 8)
VMEM_BYTES = 40 * 2**20


def reach_sizes(points, count):
    area_rows = points * count // STEP
    root_bound = min(((area_rows + 2 * 4**power) // (3 * 2**power) for power in range(3, 9)))
    grow_rows = root_bound - ROWMIN // STEP - 6
    row_longest = ROWMIN + STEP * (grow_rows - 1)
    rim_width = (2 * row_longest + 15) // 16 * 16
    return (rim_width, (rim_width + points - 1) // points)


def spans(bounds):
    return list(zip(bounds[:-1], bounds[1:]))


def passed_along(value, steps):
    count = lax.axis_size("band")
    initial, last = (max(0, -steps), min(count, count - steps))
    return lax.ppermute(value, "band", [(source, source + steps) for source in range(initial, last)])


def swapped(value, first):
    count = lax.axis_size("band")
    pairs = [(at, at + 1) for at in range(first, count - 1, 2)]
    return lax.ppermute(value, "band", pairs + [(high, low) for low, high in pairs])


def dot_nt(left, right):
    return lax.dot_general(
        left, right, (((1,), (1,)), ((), ())), preferred_element_type=jnp.float32
    )


def dot_nn(left, right):
    return jnp.dot(left, right, preferred_element_type=jnp.float32)


def head_masks():
    lanes = lax.broadcasted_iota(jnp.int32, (1, PAIR), 1)
    first = (lanes < HEAD_DIM).astype(jnp.float32)
    return (first.astype(jnp.bfloat16), (1.0 - first).astype(jnp.bfloat16))


def is_even():
    return lax.axis_index("band") % 2 == 0


def pack_kernel(points, columns, *refs):
    sources, out_ref, sems = refs[:-2], refs[-2], refs[-1]
    rows = out_ref.shape[1]
    start = pl.multiple_of(jnp.where(is_even(), 0, points - rows), 16)
    copies = [
        pltpu.make_async_copy(
            source.at[pl.ds(start, rows), columns], out_ref.at[at], sems.at[at]
        )
        for at, source in enumerate(sources)
    ]
    for copy in copies:
        copy.start()
    for copy in copies:
        copy.wait()


def pack(sources, rows, low, high, name):
    points = sources[0].shape[0]
    width = (high - low) * PAIR
    return pl.pallas_call(
        functools.partial(pack_kernel, points, slice(low * PAIR, high * PAIR)),
        in_specs=[pl.BlockSpec(memory_space=pl.ANY)] * len(sources),
        out_specs=pl.BlockSpec(memory_space=pltpu.VMEM),
        out_shape=jax.ShapeDtypeStruct((len(sources), rows, width), jnp.bfloat16),
        scratch_shapes=[pltpu.SemaphoreType.DMA((len(sources),))],
        cost_estimate=pl.CostEstimate(
            flops=0, bytes_accessed=4 * len(sources) * rows * width, transcendentals=0
        ),
        name=name,
    )(*sources)


def attention_kernel(rim, lengths, points, carried, *refs):
    far = len(lengths) // 2 - 1
    near = lengths[far]
    half = points // 2
    reached = half + 2 * rim
    win_ref, q_ref, g_ref, k_ref, v_ref, partner_k_ref, partner_v_ref, next_ref = refs[:8]
    far_refs = refs[8 : 8 + 2 * far]
    outs = refs[8 + 2 * far + carried :]
    att_ref, dq_ref, to_partner_ref, dk_ref, dv_ref, to_next_ref = outs[:6]
    to_far_refs = outs[6 : 6 + 2 * far]
    bias_ref, keys_ref, turned_ref, exps_ref, probs_ref, dscores_ref = outs[-6:]
    even = is_even()

    @pl.when(pl.program_id(0) == 0)
    def _():
        for part in range(2):
            own = slice(part * half, (part + 1) * half)
            lower = jnp.concatenate([win_ref[0:1, own]] * 2, axis=1)
            upper = jnp.concatenate([win_ref[1:2, own]] * 2, axis=1)
            keys = part * half - rim + lax.broadcasted_iota(jnp.int32, (reached, points), 0)
            bias_ref[part] = jnp.where((keys >= lower) & (keys < upper), 0.0, OUTSIDE)

    for slot, (own_ref, partner_ref) in enumerate([(k_ref, partner_k_ref), (v_ref, partner_v_ref)]):
        start = 0
        for at in range(far):
            keys_ref[slot, start : start + lengths[at], :] = far_refs[at][slot]
            start += lengths[at]
        keys_ref[slot, start : start + near, :] = jnp.where(
            even, next_ref[slot], partner_ref[points - near :, :]
        )
        keys_ref[slot, rim : rim + points, :] = own_ref[...]
        start = rim + points
        keys_ref[slot, start : start + near, :] = jnp.where(
            even, partner_ref[:near, :], next_ref[slot]
        )
        start += near
        for at in range(far, 2 * far):
            keys_ref[slot, start : start + lengths[at + 2], :] = far_refs[at][slot]
            start += lengths[at + 2]
        turned_ref[slot] = keys_ref[slot].T
    g_turned = g_ref[...].T
    masks = head_masks()
    spans_of = [slice(part * half, part * half + reached) for part in range(2)]
    owns = [slice(part * half, (part + 1) * half) for part in range(2)]
    q_both = [
        jnp.concatenate([q_ref[own, :] * (mask * SCALE) for mask in masks], axis=0) for own in owns
    ]
    g_both = [jnp.concatenate([g_ref[own, :] * mask for mask in masks], axis=0) for own in owns]
    blocks = [slice(row, row + BLOCK) for row in range(0, reached, BLOCK)]

    def fold(op, total, block):
        for row in range(0, BLOCK, 8):
            total = op(total, block[row : row + 8])
        return total

    def both(turned):
        return [turned[:HEAD_DIM, :half], turned[HEAD_DIM:, half:]]

    def forward_scores(part):
        scores = dot_nt(keys_ref[0, spans_of[part], :], q_both[part])
        top = jnp.full((8, points), OUTSIDE, jnp.float32)
        for block in blocks:
            biased = scores[block] + bias_ref[part, block, :]
            exps_ref[part, block, :] = biased
            top = fold(jnp.maximum, top, biased)
        return jnp.max(top, axis=0, keepdims=True)

    def forward_probs(part, top):
        total = jnp.zeros((8, points), jnp.float32)
        for block in blocks:
            exps = jnp.exp2((exps_ref[part, block, :] - top) * LOG2_E)
            exps_ref[part, block, :] = exps
            total = fold(jnp.add, total, exps)
        inverse = 1.0 / jnp.sum(total, axis=0, keepdims=True)
        for block in blocks:
            probs_ref[part, block, :] = (exps_ref[part, block, :] * inverse).astype(jnp.bfloat16)
        return inverse

    def forward_outputs(part):
        own = owns[part]
        att = [
            x.astype(jnp.bfloat16) for x in both(dot_nn(turned_ref[1, :, spans_of[part]], probs_ref[part]))
        ]
        att_ref[own, :] = jnp.concatenate(att, axis=0).T
        return jnp.concatenate(
            [
                jnp.sum(
                    g_turned[head * HEAD_DIM : (head + 1) * HEAD_DIM, own].astype(jnp.float32)
                    * att[head].astype(jnp.float32),
                    axis=0,
                    keepdims=True,
                )
                for head in range(2)
            ],
            axis=1,
        )

    def backward_scores(part, inverse, delta):
        dprobs = dot_nt(keys_ref[1, spans_of[part], :], g_both[part])
        for block in blocks:
            probs = exps_ref[part, block, :] * inverse
            dscores_ref[part, block, :] = (probs * (dprobs[block] - delta)).astype(jnp.bfloat16)

    def backward_outputs(part):
        own = owns[part]
        dq = both(dot_nn(turned_ref[0, :, spans_of[part]], dscores_ref[part]))
        dq_ref[own, :] = jnp.concatenate([(x * SCALE).astype(jnp.bfloat16) for x in dq], axis=0).T
        return (
            dot_nn(dscores_ref[part], q_both[part]),
            dot_nn(probs_ref[part], g_both[part]),
        )

    top_0 = forward_scores(0)
    top_1 = forward_scores(1)
    inverse_0 = forward_probs(0, top_0)
    delta_0 = forward_outputs(0)
    inverse_1 = forward_probs(1, top_1)
    backward_scores(0, inverse_0, delta_0)
    delta_1 = forward_outputs(1)
    sums_0 = backward_outputs(0)
    backward_scores(1, inverse_1, delta_1)
    sums_1 = backward_outputs(1)

    def rows_of(low, high, start, stop):
        cuts = sorted({start, stop} | {x for x in (half, reached) if start < x < stop})
        pieces = []
        for first, last in spans(cuts):
            if last <= half:
                pieces.append(low[first:last])
            elif first >= reached:
                pieces.append(high[first - half : last - half])
            else:
                pieces.append(low[first:last] + high[first - half : last - half])
        return jnp.concatenate(pieces, axis=0)

    for slot, own_ref in enumerate([dk_ref, dv_ref]):
        low, high = sums_0[slot], sums_1[slot]
        own_ref[...] = rows_of(low, high, rim, rim + points)
        near_low = rows_of(low, high, rim - near, rim).astype(jnp.bfloat16)
        near_high = rows_of(low, high, rim + points, rim + points + near).astype(jnp.bfloat16)
        to_partner_ref[slot] = jnp.where(even, near_high, near_low)
        to_next_ref[slot] = jnp.where(even, near_low, near_high)
        start = 0
        for at in range(far):
            ref = to_far_refs[at]
            ref[slot] = rows_of(low, high, start, start + lengths[at]).astype(jnp.bfloat16)
            start += lengths[at]
        start = rim + points + near
        for at in range(far, 2 * far):
            ref = to_far_refs[at]
            ref[slot] = rows_of(low, high, start, start + lengths[at + 2]).astype(jnp.bfloat16)
            start += lengths[at + 2]


def sum_kernel(far_lengths, points, carried, *refs):
    far = len(far_lengths) // 2
    dk_ref, dv_ref, partner_ref, next_ref = refs[:4]
    far_refs = refs[4 : 4 + 2 * far]
    outs = refs[4 + 2 * far + carried :]
    total = outs[-1]
    near = partner_ref.shape[1]
    high = pl.multiple_of(jnp.where(is_even(), points - near, 0), 16)
    starts = (high, points - near - high)
    for slot, (own_ref, out_ref) in enumerate([(dk_ref, outs[0]), (dv_ref, outs[1])]):
        total[...] = own_ref[...]
        for at, ref in enumerate((partner_ref, next_ref)):
            rows = pl.ds(pl.multiple_of(starts[at], 16), near)
            total[rows, :] += ref[slot].astype(jnp.float32)
        for at, (ref, length) in enumerate(zip(far_refs, far_lengths)):
            rows = slice(points - length, points) if at < far else slice(0, length)
            total[rows, :] += ref[slot].astype(jnp.float32)
        out_ref[...] = total[...].astype(jnp.bfloat16)


def chunk_call(kernel, args, in_specs, carried, out_specs, out_shape, **options):
    return pl.pallas_call(
        functools.partial(kernel, len(carried)),
        in_specs=in_specs + [pl.BlockSpec(memory_space=pl.ANY)] * len(carried),
        out_specs=out_specs,
        out_shape=out_shape,
        input_output_aliases={len(args) + at: at for at in range(len(carried))},
        compiler_params=pltpu.CompilerParams(
            vmem_limit_bytes=VMEM_BYTES, dimension_semantics=("arbitrary",)
        ),
        **options,
    )(*args, *carried)


def per_device(queries, keys, values, grad_out, windows):
    points, width = queries.shape
    rim_width, reach = reach_sizes(points, lax.axis_size("band"))
    band = lax.axis_index("band")
    near = min(points, rim_width)
    far = [d for d in range(-reach, reach + 1) if abs(d) > 1]
    far_sizes = [min(points, rim_width - (abs(d) - 1) * points) for d in far]
    lows = len(far) // 2
    lengths = far_sizes[:lows] + [near, near] + far_sizes[lows:]
    wide = points + 2 * rim_width
    relative = (windows - band * points).T

    to_next, from_next = [], []
    ready = (keys, values)
    for chunk, (low, high) in enumerate(spans(CHUNKS)):
        to_next.append(pack(ready, near, low, high, f"pack_next_{chunk}"))
        ready = lax.optimization_barrier((keys, values, to_next[chunk]))[:2]
    from_next.append(swapped(to_next[0], 1))
    from_partner = [swapped(field, 0) for field in ready]
    for piece in to_next[1:]:
        from_next.append(swapped(lax.optimization_barrier((piece, *from_partner))[0], 1))
    from_far = []
    for d, size in zip(far, far_sizes):
        part = slice(points - size, points) if d < 0 else slice(0, size)
        from_far.append(passed_along(jnp.stack([keys[part], values[part]]), -d))

    def columns(rows, low):
        return pl.BlockSpec((rows, PAIR), lambda i: (0, i + low))

    def piece(rows, low):
        return pl.BlockSpec((2, rows, PAIR), lambda i: (0, 0, i + low))

    whole = jax.ShapeDtypeStruct((points, width), jnp.bfloat16)
    reached = points // 2 + 2 * rim_width
    outs, own_terms, back_next, back_far = [], [], [], []
    for chunk, (low, high) in enumerate(spans(CHUNKS)):
        count = high - low
        chunk_width = count * PAIR
        outs = chunk_call(
            lambda carried, *refs: attention_kernel(rim_width, lengths, points, carried, *refs),
            [relative, queries, grad_out, keys, values, *from_partner, from_next[chunk], *from_far],
            [pl.BlockSpec((2, points), lambda i: (0, 0))]
            + [columns(points, low)] * 6
            + [piece(near, 0)]
            + [piece(size, low) for size in far_sizes],
            outs[:3],
            [columns(points, low)] * 2
            + [piece(near, low)]
            + [columns(points, 0)] * 2
            + [piece(near, 0)]
            + [piece(size, 0) for size in far_sizes],
            [whole] * 2
            + [jax.ShapeDtypeStruct((2, near, width), jnp.bfloat16)]
            + [jax.ShapeDtypeStruct((points, chunk_width), jnp.float32)] * 2
            + [
                jax.ShapeDtypeStruct((2, size, chunk_width), jnp.bfloat16)
                for size in [near] + far_sizes
            ],
            grid=(count,),
            scratch_shapes=[
                pltpu.VMEM((2, reached, points), jnp.float32),
                pltpu.VMEM((2, wide, PAIR), jnp.bfloat16),
                pltpu.VMEM((2, PAIR, wide), jnp.bfloat16),
                pltpu.VMEM((2, reached, points), jnp.float32),
                pltpu.VMEM((2, reached, points), jnp.bfloat16),
                pltpu.VMEM((2, reached, points), jnp.bfloat16),
            ],
            cost_estimate=pl.CostEstimate(
                flops=count * 24 * reached * points * PAIR,
                bytes_accessed=count * PAIR * (20 * points + 8 * wide),
                transcendentals=2 * count * points * reached,
            ),
            name=f"attention_{chunk}",
        )
        own_terms.append(outs[3:5])
        to_back = outs[5]
        if back_next:
            to_back = lax.optimization_barrier((to_back, back_next[-1]))[0]
        back_next.append(swapped(to_back, 1))
        back_far.append([passed_along(term, d) for term, d in zip(outs[6:], far)])
    back_partner = swapped(outs[2], 0)

    grads = []
    for chunk, (low, high) in enumerate(spans(CHUNKS)):
        chunk_width = (high - low) * PAIR
        step = 2 * PAIR

        def sums(rows, low):
            return pl.BlockSpec((rows, step), lambda i: (0, i + low * PAIR // step))

        def terms(rows, low):
            return pl.BlockSpec((2, rows, step), lambda i: (0, 0, i + low * PAIR // step))

        grads = chunk_call(
            lambda carried, *refs: sum_kernel(far_sizes, points, carried, *refs),
            [*own_terms[chunk], back_partner, back_next[chunk], *back_far[chunk]],
            [sums(points, 0)] * 2
            + [terms(near, low), terms(near, 0)]
            + [terms(size, 0) for size in far_sizes],
            grads,
            [sums(points, low)] * 2,
            [whole] * 2,
            grid=(chunk_width // step,),
            scratch_shapes=[pltpu.VMEM((points, step), jnp.float32)],
            cost_estimate=pl.CostEstimate(
                flops=6 * points * chunk_width,
                bytes_accessed=20 * points * chunk_width,
                transcendentals=0,
            ),
            name=f"gradient_sums_{chunk}",
        )
    return (outs[0], outs[1], grads[0], grads[1])


def solution(mesh):
    spread = P(("members", "band"), None)
    return jax.shard_map(
        per_device,
        mesh=mesh,
        in_specs=(spread, spread, spread, spread, P("band", None)),
        out_specs=(spread, spread, spread, spread),
        check_vma=False,
    )
```

```python
import functools
import math

import jax
import jax.numpy as jnp
from jax import lax
from jax.experimental import pallas as pl
from jax.experimental.pallas import tpu as pltpu
from jax.sharding import PartitionSpec as P

HEADS = 16
HEAD_DIM = 64
ROWMIN = 20
STEP = 4
PAIR = 2 * HEAD_DIM
PAIRS = HEADS // 2
SCALE = HEAD_DIM**-0.5
LOG2_E = math.log2(math.e)
BLOCK = 32
OUTSIDE = -1e30
CHUNKS = (0, 4, 8)
NEXT_CHUNKS = (0, 4, 8)
VMEM_BYTES = 40 * 2**20


def reach_sizes(points, count):
    area_rows = points * count // STEP
    root_bound = min(((area_rows + 2 * 4**power) // (3 * 2**power) for power in range(3, 9)))
    grow_rows = root_bound - ROWMIN // STEP - 6
    row_longest = ROWMIN + STEP * (grow_rows - 1)
    rim_width = (2 * row_longest + 15) // 16 * 16
    return (rim_width, (rim_width + points - 1) // points)


def spans(bounds):
    return list(zip(bounds[:-1], bounds[1:]))


def passed_along(value, steps):
    count = lax.axis_size("band")
    initial, last = (max(0, -steps), min(count, count - steps))
    return lax.ppermute(value, "band", [(source, source + steps) for source in range(initial, last)])


def swapped(value, first):
    count = lax.axis_size("band")
    pairs = [(at, at + 1) for at in range(first, count - 1, 2)]
    return lax.ppermute(value, "band", pairs + [(high, low) for low, high in pairs])


def dot_nt(left, right):
    return lax.dot_general(
        left, right, (((1,), (1,)), ((), ())), preferred_element_type=jnp.float32
    )


def dot_nn(left, right):
    return jnp.dot(left, right, preferred_element_type=jnp.float32)


def head_masks():
    lanes = lax.broadcasted_iota(jnp.int32, (1, PAIR), 1)
    first = (lanes < HEAD_DIM).astype(jnp.float32)
    return (first.astype(jnp.bfloat16), (1.0 - first).astype(jnp.bfloat16))


def is_even():
    return lax.axis_index("band") % 2 == 0


def pack_kernel(points, columns, *refs):
    sources, out_ref, sems = refs[:-2], refs[-2], refs[-1]
    rows = out_ref.shape[1]
    start = pl.multiple_of(jnp.where(is_even(), 0, points - rows), 16)
    copies = [
        pltpu.make_async_copy(
            source.at[pl.ds(start, rows), columns], out_ref.at[at], sems.at[at]
        )
        for at, source in enumerate(sources)
    ]
    for copy in copies:
        copy.start()
    for copy in copies:
        copy.wait()


def pack(sources, rows, low, high, name):
    points = sources[0].shape[0]
    width = (high - low) * PAIR
    return pl.pallas_call(
        functools.partial(pack_kernel, points, slice(low * PAIR, high * PAIR)),
        in_specs=[pl.BlockSpec(memory_space=pl.ANY)] * len(sources),
        out_specs=pl.BlockSpec(memory_space=pltpu.VMEM),
        out_shape=jax.ShapeDtypeStruct((len(sources), rows, width), jnp.bfloat16),
        scratch_shapes=[pltpu.SemaphoreType.DMA((len(sources),))],
        cost_estimate=pl.CostEstimate(
            flops=0, bytes_accessed=4 * len(sources) * rows * width, transcendentals=0
        ),
        name=name,
    )(*sources)


def attention_kernel(rim, lengths, points, low_pair, next_pairs, carried, *refs):
    far = len(lengths) // 2 - 1
    near = lengths[far]
    half = points // 2
    reached = half + 2 * rim
    wide = points + 2 * rim
    pairs = sum(next_pairs)
    win_ref, q_ref, g_ref, k_ref, v_ref, partner_k_ref, partner_v_ref = refs[:7]
    next_refs = refs[7 : 7 + len(next_pairs)]
    refs = refs[7 + len(next_pairs) :]
    far_refs = refs[: 2 * far]
    outs = refs[2 * far + carried :]
    att_out, dq_out, to_partner_ref, to_next_ref, dk_ref, dv_ref = outs[:6]
    to_far_refs = outs[6 : 6 + 2 * far]
    (bias_ref, keys_ref, turned_ref, exps_ref, probs_ref, dscores_ref, sums_ref, att_ref, dq_ref, sems) = outs[-10:]
    even = is_even()
    owns = [slice(part * half, (part + 1) * half) for part in range(2)]
    spans_of = [slice(part * half, part * half + reached) for part in range(2)]
    blocks = [slice(row, row + BLOCK) for row in range(0, reached, BLOCK)]
    masks = head_masks()

    for part, own in enumerate(owns):
        lower = jnp.concatenate([win_ref[0:1, own]] * 2, axis=1)
        upper = jnp.concatenate([win_ref[1:2, own]] * 2, axis=1)
        for block in blocks:
            keys = lax.broadcasted_iota(jnp.int32, (BLOCK, points), 0) + (part * half - rim + block.start)
            inside = (keys >= lower) & (keys < upper)
            bias_ref[part, block, :] = jnp.where(inside, 0.0, OUTSIDE)

    where_next = [
        (chunk, at) for chunk, count in enumerate(next_pairs) for at in range(count)
    ]

    def columns_of(pair):
        return slice((low_pair + pair) * PAIR, (low_pair + pair + 1) * PAIR)

    def local_columns(pair):
        return slice(pair * PAIR, (pair + 1) * PAIR)

    def gather_keys(pair):
        columns = columns_of(pair)
        chunk, at = where_next[pair]
        next_columns = local_columns(at)
        into = keys_ref.at[pair % 2]
        for slot, (own_ref, partner_ref) in enumerate([(k_ref, partner_k_ref), (v_ref, partner_v_ref)]):
            start = 0
            for at in range(far):
                into[slot, start : start + lengths[at], :] = far_refs[at][slot, :, columns]
                start += lengths[at]
            into[slot, start : start + near, :] = jnp.where(
                even, next_refs[chunk][slot, :, next_columns], partner_ref[points - near :, columns]
            )
            into[slot, rim : rim + points, :] = own_ref[:, columns]
            start = rim + points
            into[slot, start : start + near, :] = jnp.where(
                even, partner_ref[:near, columns], next_refs[chunk][slot, :, next_columns]
            )
            start += near
            for at in range(far, 2 * far):
                into[slot, start : start + lengths[at + 2], :] = far_refs[at][slot, :, columns]
                start += lengths[at + 2]
            turned_ref[pair % 2, slot] = into[slot].T

    def fold(op, total, block):
        for row in range(0, BLOCK, 8):
            total = op(total, block[row : row + 8])
        return total

    def both(turned):
        return [turned[:HEAD_DIM, :half], turned[HEAD_DIM:, half:]]

    def q_both(pair, part):
        q = q_ref[owns[part], columns_of(pair)]
        return jnp.concatenate([q * (mask * SCALE) for mask in masks], axis=0)

    def g_both(pair, part):
        g = g_ref[owns[part], columns_of(pair)]
        return jnp.concatenate([g * mask for mask in masks], axis=0)

    def forward_scores(pair, part):
        exps = exps_ref.at[pair % 2, part]
        scores = dot_nt(keys_ref[pair % 2, 0, spans_of[part], :], q_both(pair, part))
        top = jnp.full((8, points), OUTSIDE, jnp.float32)
        for block in blocks:
            biased = scores[block] + bias_ref[part, block, :]
            exps[block, :] = biased
            top = fold(jnp.maximum, top, biased)
        return jnp.max(top, axis=0, keepdims=True)

    def forward_probs(pair, part, top):
        exps = exps_ref.at[pair % 2, part]
        total = jnp.zeros((8, points), jnp.float32)
        for block in blocks:
            values = jnp.exp2((exps[block, :] - top) * LOG2_E)
            exps[block, :] = values
            total = fold(jnp.add, total, values)
        inverse = 1.0 / jnp.sum(total, axis=0, keepdims=True)
        for block in blocks:
            probs_ref[pair % 2, part, block, :] = (exps[block, :] * inverse).astype(jnp.bfloat16)
        return inverse

    def forward_outputs(pair, part):
        own = owns[part]
        att = [
            x.astype(jnp.bfloat16)
            for x in both(
                dot_nn(turned_ref[pair % 2, 1, :, spans_of[part]], probs_ref[pair % 2, part])
            )
        ]
        att_ref[pair, own, :] = jnp.concatenate(att, axis=0).T
        g_turned = g_ref[own, columns_of(pair)].T
        return jnp.concatenate(
            [
                jnp.sum(
                    g_turned[head * HEAD_DIM : (head + 1) * HEAD_DIM].astype(jnp.float32)
                    * att[head].astype(jnp.float32),
                    axis=0,
                    keepdims=True,
                )
                for head in range(2)
            ],
            axis=1,
        )

    def backward_scores(pair, part, inverse, delta):
        dprobs = dot_nt(keys_ref[pair % 2, 1, spans_of[part], :], g_both(pair, part))
        for block in blocks:
            probs = exps_ref[pair % 2, part, block, :] * inverse
            dscores_ref[pair % 2, part, block, :] = (probs * (dprobs[block] - delta)).astype(jnp.bfloat16)

    def backward_outputs(pair, part):
        dscores = dscores_ref[pair % 2, part]
        dq = both(dot_nn(turned_ref[pair % 2, 0, :, spans_of[part]], dscores))
        dq_ref[pair, owns[part], :] = jnp.concatenate(
            [(x * SCALE).astype(jnp.bfloat16) for x in dq], axis=0
        ).T
        terms = (dot_nn(dscores, q_both(pair, part)), dot_nn(probs_ref[pair % 2, part], g_both(pair, part)))
        for slot, term in enumerate(terms):
            into = sums_ref.at[pair % 2, slot]
            if part == 0:
                into[:reached, :] = term
            else:
                into[half:reached, :] += term[: reached - half]
                into[reached:, :] = term[reached - half :]

    copies = []

    def send_out(pair):
        columns = local_columns(pair)
        for slot, own_ref in enumerate([dk_ref, dv_ref]):
            sums = sums_ref.at[pair % 2, slot]
            own_ref[:, columns] = sums[rim : rim + points, :]
            near_low = sums[rim - near : rim, :].astype(jnp.bfloat16)
            near_high = sums[rim + points : rim + points + near, :].astype(jnp.bfloat16)
            to_partner_ref[slot, :, columns] = jnp.where(even, near_high, near_low)
            to_next_ref[slot, :, columns] = jnp.where(even, near_low, near_high)
            start = 0
            for at in range(far):
                size = lengths[at]
                to_far_refs[at][slot, :, columns] = sums[start : start + size, :].astype(jnp.bfloat16)
                start += size
            start = rim + points + near
            for at in range(far, 2 * far):
                size = lengths[at + 2]
                to_far_refs[at][slot, :, columns] = sums[start : start + size, :].astype(jnp.bfloat16)
                start += size
        for at, (ref, out) in enumerate([(att_ref, att_out), (dq_ref, dq_out)]):
            copy = pltpu.make_async_copy(ref.at[pair], out.at[:, columns_of(pair)], sems.at[at, pair])
            copy.start()
            copies.append(copy)

    units = [(pair, part) for pair in range(pairs) for part in range(2)]
    gather_keys(0)
    tops = {units[0]: forward_scores(*units[0])}
    for at, unit in enumerate(units):
        if at + 1 < len(units):
            following = units[at + 1]
            if following[1] == 0:
                gather_keys(following[0])
            tops[following] = forward_scores(*following)
        if at > 0:
            backward_outputs(*units[at - 1])
            if units[at - 1][1] == 1:
                send_out(units[at - 1][0])
        inverse = forward_probs(*unit, tops.pop(unit))
        delta = forward_outputs(*unit)
        backward_scores(*unit, inverse, delta)
    backward_outputs(*units[-1])
    send_out(units[-1][0])
    for copy in copies:
        copy.wait()


def sum_kernel(far_lengths, points, low, high, carried, *refs):
    far = len(far_lengths) // 2
    own_refs, partner_ref, next_ref = refs[:2], refs[2], refs[3]
    far_refs = refs[4 : 4 + 2 * far]
    outs = refs[4 + 2 * far + carried :]
    total, low_ref, sems = outs[-3:]
    near = partner_ref.shape[1]
    first = pl.multiple_of(jnp.where(is_even(), points - near, 0), 16)
    starts = (first, points - near - first)
    copies = []
    for slot in range(2):
        total[...] = own_refs[slot][...]
        for at, ref in enumerate((partner_ref, next_ref)):
            rows = pl.ds(pl.multiple_of(starts[at], 16), near)
            total[rows, :] += ref[slot].astype(jnp.float32)
        for at, (ref, length) in enumerate(zip(far_refs, far_lengths)):
            rows = slice(points - length, points) if at < far else slice(0, length)
            total[rows, :] += ref[slot].astype(jnp.float32)
        low_ref[slot] = total[...].astype(jnp.bfloat16)
        copy = pltpu.make_async_copy(
            low_ref.at[slot], outs[slot].at[:, low * PAIR : high * PAIR], sems.at[slot]
        )
        copy.start()
        copies.append(copy)
    for copy in copies:
        copy.wait()


def chunk_call(kernel, args, carried, count, out_shape, **options):
    vmem = pl.BlockSpec(memory_space=pltpu.VMEM)
    anywhere = pl.BlockSpec(memory_space=pl.ANY)
    return pl.pallas_call(
        functools.partial(kernel, len(carried)),
        in_specs=[vmem] * len(args) + [anywhere] * len(carried),
        out_specs=[anywhere] * count + [vmem] * (len(out_shape) - count),
        out_shape=out_shape,
        input_output_aliases={len(args) + at: at for at in range(len(carried))},
        compiler_params=pltpu.CompilerParams(vmem_limit_bytes=VMEM_BYTES),
        **options,
    )(*args, *carried)


def per_device(queries, keys, values, grad_out, windows):
    points, width = queries.shape
    rim_width, reach = reach_sizes(points, lax.axis_size("band"))
    band = lax.axis_index("band")
    near = min(points, rim_width)
    far = [d for d in range(-reach, reach + 1) if abs(d) > 1]
    far_sizes = [min(points, rim_width - (abs(d) - 1) * points) for d in far]
    lows = len(far) // 2
    lengths = far_sizes[:lows] + [near, near] + far_sizes[lows:]
    wide = points + 2 * rim_width
    reached = points // 2 + 2 * rim_width
    relative = (windows - band * points).T

    to_next, from_next, from_partner = [], [], []
    ready = (keys, values)
    for chunk, (low, high) in enumerate(spans(NEXT_CHUNKS)):
        to_next.append(pack(ready, near, low, high, f"pack_next_{chunk}"))
        from_next.append(swapped(to_next[chunk], 1))
        if chunk == 0:
            ready = lax.optimization_barrier((keys, values, to_next[0]))[:2]
            from_partner = [swapped(field, 0) for field in ready]
            ready = lax.optimization_barrier((keys, values, *from_partner))[:2]
        else:
            ready = lax.optimization_barrier((*ready, to_next[chunk], from_next[chunk - 1]))[:2]
    from_far = []
    for d, size in zip(far, far_sizes):
        part = slice(points - size, points) if d < 0 else slice(0, size)
        from_far.append(passed_along(jnp.stack([keys[part], values[part]]), -d))

    whole = jax.ShapeDtypeStruct((points, width), jnp.bfloat16)
    outs, own_terms, back_partner, back_next, back_far = [], [], [], [], []
    for chunk, (low, high) in enumerate(spans(CHUNKS)):
        count = high - low
        chunk_width = count * PAIR
        parts = [
            (at, last - first)
            for at, (first, last) in enumerate(spans(NEXT_CHUNKS))
            if low <= first and last <= high
        ]
        next_pairs = [size for _, size in parts]
        assert sum(next_pairs) == count
        outs = chunk_call(
            functools.partial(attention_kernel, rim_width, lengths, points, low, next_pairs),
            [relative, queries, grad_out, keys, values, *from_partner]
            + [from_next[at] for at, _ in parts]
            + from_far,
            outs[:2],
            2,
            [whole] * 2
            + [jax.ShapeDtypeStruct((2, near, chunk_width), jnp.bfloat16)] * 2
            + [jax.ShapeDtypeStruct((points, chunk_width), jnp.float32)] * 2
            + [jax.ShapeDtypeStruct((2, size, chunk_width), jnp.bfloat16) for size in far_sizes],
            scratch_shapes=[
                pltpu.VMEM((2, reached, points), jnp.float32),
                pltpu.VMEM((2, 2, wide, PAIR), jnp.bfloat16),
                pltpu.VMEM((2, 2, PAIR, wide), jnp.bfloat16),
                pltpu.VMEM((2, 2, reached, points), jnp.float32),
                pltpu.VMEM((2, 2, reached, points), jnp.bfloat16),
                pltpu.VMEM((2, 2, reached, points), jnp.bfloat16),
                pltpu.VMEM((2, 2, wide, PAIR), jnp.float32),
                pltpu.VMEM((count, points, PAIR), jnp.bfloat16),
                pltpu.VMEM((count, points, PAIR), jnp.bfloat16),
                pltpu.SemaphoreType.DMA((2, count)),
            ],
            cost_estimate=pl.CostEstimate(
                flops=count * 24 * reached * points * PAIR,
                bytes_accessed=count * PAIR * (20 * points + 8 * wide),
                transcendentals=2 * count * points * reached,
            ),
            name=f"attention_{chunk}",
        )
        own_terms.append(outs[4:6])
        back_partner.append(swapped(outs[2], 0))
        back_next.append(swapped(outs[3], 1))
        back_far.append([passed_along(term, d) for term, d in zip(outs[6:], far)])

    grads = []
    for chunk, (low, high) in enumerate(spans(CHUNKS)):
        chunk_width = (high - low) * PAIR
        grads = chunk_call(
            functools.partial(sum_kernel, far_sizes, points, low, high),
            [*own_terms[chunk], back_partner[chunk], back_next[chunk], *back_far[chunk]],
            grads,
            2,
            [whole] * 2,
            scratch_shapes=[
                pltpu.VMEM((points, chunk_width), jnp.float32),
                pltpu.VMEM((2, points, chunk_width), jnp.bfloat16),
                pltpu.SemaphoreType.DMA((2,)),
            ],
            cost_estimate=pl.CostEstimate(
                flops=6 * points * chunk_width,
                bytes_accessed=20 * points * chunk_width,
                transcendentals=0,
            ),
            name=f"gradient_sums_{chunk}",
        )
    return (outs[0], outs[1], grads[0], grads[1])


def solution(mesh):
    spread = P(("members", "band"), None)
    return jax.shard_map(
        per_device,
        mesh=mesh,
        in_specs=(spread, spread, spread, spread, P("band", None)),
        out_specs=(spread, spread, spread, spread),
        check_vma=False,
    )
```

```python
import functools
import math

import jax
import jax.numpy as jnp
from jax import lax
from jax.experimental import pallas as pl
from jax.experimental.pallas import tpu as pltpu
from jax.sharding import PartitionSpec as P

HEADS = 16
HEAD_DIM = 64
ROWMIN = 20
STEP = 4
PAIR = 2 * HEAD_DIM
PAIRS = HEADS // 2
SCALE = HEAD_DIM**-0.5
LOG2_E = math.log2(math.e)
BLOCK = 32
OUTSIDE = -1e30
CHUNKS = (0, 4, 8)
NEXT_CHUNKS = (0, 2, 4, 8)


def reach_sizes(points, count):
    area_rows = points * count // STEP
    root_bound = min(((area_rows + 2 * 4**power) // (3 * 2**power) for power in range(3, 9)))
    grow_rows = root_bound - ROWMIN // STEP - 6
    row_longest = ROWMIN + STEP * (grow_rows - 1)
    rim_width = (2 * row_longest + 15) // 16 * 16
    return (rim_width, (rim_width + points - 1) // points)


def spans(bounds):
    return list(zip(bounds[:-1], bounds[1:]))


def passed_along(value, steps):
    count = lax.axis_size("band")
    initial, last = (max(0, -steps), min(count, count - steps))
    return lax.ppermute(value, "band", [(source, source + steps) for source in range(initial, last)])


def swapped(value, first):
    count = lax.axis_size("band")
    pairs = [(at, at + 1) for at in range(first, count - 1, 2)]
    return lax.ppermute(value, "band", pairs + [(high, low) for low, high in pairs])


def dot_nt(left, right):
    return lax.dot_general(
        left, right, (((1,), (1,)), ((), ())), preferred_element_type=jnp.float32
    )


def dot_nn(left, right):
    return jnp.dot(left, right, preferred_element_type=jnp.float32)


def head_masks():
    lanes = lax.broadcasted_iota(jnp.int32, (1, PAIR), 1)
    first = (lanes < HEAD_DIM).astype(jnp.float32)
    return (first.astype(jnp.bfloat16), (1.0 - first).astype(jnp.bfloat16))


def is_even():
    return lax.axis_index("band") % 2 == 0


def pack_kernel(points, columns, *refs):
    sources, out_ref, sems = refs[:-2], refs[-2], refs[-1]
    rows = out_ref.shape[1]
    start = pl.multiple_of(jnp.where(is_even(), 0, points - rows), 16)
    copies = [
        pltpu.make_async_copy(
            source.at[pl.ds(start, rows), columns], out_ref.at[at], sems.at[at]
        )
        for at, source in enumerate(sources)
    ]
    for copy in copies:
        copy.start()
    for copy in copies:
        copy.wait()


def pack(sources, rows, low, high, name):
    points = sources[0].shape[0]
    width = (high - low) * PAIR
    return pl.pallas_call(
        functools.partial(pack_kernel, points, slice(low * PAIR, high * PAIR)),
        in_specs=[pl.BlockSpec(memory_space=pl.ANY)] * len(sources),
        out_specs=pl.BlockSpec(memory_space=pltpu.VMEM),
        out_shape=jax.ShapeDtypeStruct((len(sources), rows, width), jnp.bfloat16),
        scratch_shapes=[pltpu.SemaphoreType.DMA((len(sources),))],
        cost_estimate=pl.CostEstimate(
            flops=0, bytes_accessed=4 * len(sources) * rows * width, transcendentals=0
        ),
        name=name,
    )(*sources)


def attention_kernel(rim, lengths, points, low_pair, next_pairs, carried, *refs):
    far = len(lengths) // 2 - 1
    near = lengths[far]
    half = points // 2
    reached = half + 2 * rim
    wide = points + 2 * rim
    pairs = sum(next_pairs)
    win_ref, q_ref, g_ref, k_ref, v_ref, partner_k_ref, partner_v_ref = refs[:7]
    next_refs = refs[7 : 7 + len(next_pairs)]
    refs = refs[7 + len(next_pairs) :]
    far_refs = refs[: 2 * far]
    outs = refs[2 * far + carried :]
    att_out, dq_out, to_partner_ref, to_next_ref, dk_ref, dv_ref = outs[:6]
    to_far_refs = outs[6 : 6 + 2 * far]
    (bias_ref, keys_ref, turned_ref, exps_ref, probs_ref, dscores_ref, sums_ref, att_ref, dq_ref, sems) = outs[-10:]
    even = is_even()
    owns = [slice(part * half, (part + 1) * half) for part in range(2)]
    spans_of = [slice(part * half, part * half + reached) for part in range(2)]
    blocks = [slice(row, row + BLOCK) for row in range(0, reached, BLOCK)]
    masks = head_masks()

    for part, own in enumerate(owns):
        lower = jnp.concatenate([win_ref[0:1, own]] * 2, axis=1)
        upper = jnp.concatenate([win_ref[1:2, own]] * 2, axis=1)
        for block in blocks:
            keys = lax.broadcasted_iota(jnp.int32, (BLOCK, points), 0) + (part * half - rim + block.start)
            inside = (keys >= lower) & (keys < upper)
            bias_ref[part, block, :] = jnp.where(inside, 0.0, OUTSIDE)

    where_next = [
        (chunk, at) for chunk, count in enumerate(next_pairs) for at in range(count)
    ]

    def columns_of(pair):
        return slice((low_pair + pair) * PAIR, (low_pair + pair + 1) * PAIR)

    def local_columns(pair):
        return slice(pair * PAIR, (pair + 1) * PAIR)

    def gather_keys(pair):
        columns = columns_of(pair)
        chunk, at = where_next[pair]
        next_columns = local_columns(at)
        into = keys_ref.at[pair % 2]
        for slot, (own_ref, partner_ref) in enumerate([(k_ref, partner_k_ref), (v_ref, partner_v_ref)]):
            start = 0
            for at in range(far):
                into[slot, start : start + lengths[at], :] = far_refs[at][slot, :, columns]
                start += lengths[at]
            into[slot, start : start + near, :] = jnp.where(
                even, next_refs[chunk][slot, :, next_columns], partner_ref[points - near :, columns]
            )
            into[slot, rim : rim + points, :] = own_ref[:, columns]
            start = rim + points
            into[slot, start : start + near, :] = jnp.where(
                even, partner_ref[:near, columns], next_refs[chunk][slot, :, next_columns]
            )
            start += near
            for at in range(far, 2 * far):
                into[slot, start : start + lengths[at + 2], :] = far_refs[at][slot, :, columns]
                start += lengths[at + 2]
            turned_ref[pair % 2, slot] = into[slot].T

    def fold(op, total, block):
        for row in range(0, BLOCK, 8):
            total = op(total, block[row : row + 8])
        return total

    def both(turned):
        return [turned[:HEAD_DIM, :half], turned[HEAD_DIM:, half:]]

    def q_both(pair, part):
        q = q_ref[owns[part], columns_of(pair)]
        return jnp.concatenate([q * (mask * SCALE) for mask in masks], axis=0)

    def g_both(pair, part):
        g = g_ref[owns[part], columns_of(pair)]
        return jnp.concatenate([g * mask for mask in masks], axis=0)

    def forward_scores(pair, part):
        exps = exps_ref.at[pair % 2, part]
        scores = dot_nt(keys_ref[pair % 2, 0, spans_of[part], :], q_both(pair, part))
        top = jnp.full((8, points), OUTSIDE, jnp.float32)
        for block in blocks:
            biased = scores[block] + bias_ref[part, block, :]
            exps[block, :] = biased
            top = fold(jnp.maximum, top, biased)
        return jnp.max(top, axis=0, keepdims=True)

    def forward_probs(pair, part, top):
        exps = exps_ref.at[pair % 2, part]
        total = jnp.zeros((8, points), jnp.float32)
        for block in blocks:
            values = jnp.exp2((exps[block, :] - top) * LOG2_E)
            exps[block, :] = values
            total = fold(jnp.add, total, values)
        inverse = 1.0 / jnp.sum(total, axis=0, keepdims=True)
        for block in blocks:
            probs_ref[pair % 2, part, block, :] = (exps[block, :] * inverse).astype(jnp.bfloat16)
        return inverse

    def forward_outputs(pair, part):
        own = owns[part]
        att = [
            x.astype(jnp.bfloat16)
            for x in both(
                dot_nn(turned_ref[pair % 2, 1, :, spans_of[part]], probs_ref[pair % 2, part])
            )
        ]
        att_ref[pair, own, :] = jnp.concatenate(att, axis=0).T
        g_turned = g_ref[own, columns_of(pair)].T
        return jnp.concatenate(
            [
                jnp.sum(
                    g_turned[head * HEAD_DIM : (head + 1) * HEAD_DIM].astype(jnp.float32)
                    * att[head].astype(jnp.float32),
                    axis=0,
                    keepdims=True,
                )
                for head in range(2)
            ],
            axis=1,
        )

    def backward_scores(pair, part, inverse, delta):
        dprobs = dot_nt(keys_ref[pair % 2, 1, spans_of[part], :], g_both(pair, part))
        for block in blocks:
            probs = exps_ref[pair % 2, part, block, :] * inverse
            dscores_ref[pair % 2, part, block, :] = (probs * (dprobs[block] - delta)).astype(jnp.bfloat16)

    def backward_outputs(pair, part):
        dscores = dscores_ref[pair % 2, part]
        dq = both(dot_nn(turned_ref[pair % 2, 0, :, spans_of[part]], dscores))
        dq_ref[pair, owns[part], :] = jnp.concatenate(
            [(x * SCALE).astype(jnp.bfloat16) for x in dq], axis=0
        ).T
        terms = (dot_nn(dscores, q_both(pair, part)), dot_nn(probs_ref[pair % 2, part], g_both(pair, part)))
        for slot, term in enumerate(terms):
            into = sums_ref.at[pair % 2, slot]
            if part == 0:
                into[:reached, :] = term
            else:
                into[half:reached, :] += term[: reached - half]
                into[reached:, :] = term[reached - half :]

    copies = []

    def send_out(pair):
        columns = local_columns(pair)
        for slot, own_ref in enumerate([dk_ref, dv_ref]):
            sums = sums_ref.at[pair % 2, slot]
            own_ref[:, columns] = sums[rim : rim + points, :]
            near_low = sums[rim - near : rim, :].astype(jnp.bfloat16)
            near_high = sums[rim + points : rim + points + near, :].astype(jnp.bfloat16)
            to_partner_ref[slot, :, columns] = jnp.where(even, near_high, near_low)
            to_next_ref[slot, :, columns] = jnp.where(even, near_low, near_high)
            start = 0
            for at in range(far):
                size = lengths[at]
                to_far_refs[at][slot, :, columns] = sums[start : start + size, :].astype(jnp.bfloat16)
                start += size
            start = rim + points + near
            for at in range(far, 2 * far):
                size = lengths[at + 2]
                to_far_refs[at][slot, :, columns] = sums[start : start + size, :].astype(jnp.bfloat16)
                start += size
        for at, (ref, out) in enumerate([(att_ref, att_out), (dq_ref, dq_out)]):
            copy = pltpu.make_async_copy(ref.at[pair], out.at[:, columns_of(pair)], sems.at[at, pair])
            copy.start()
            copies.append(copy)

    units = [(pair, part) for pair in range(pairs) for part in range(2)]
    gather_keys(0)
    tops = {units[0]: forward_scores(*units[0])}
    for at, unit in enumerate(units):
        if at + 1 < len(units):
            following = units[at + 1]
            if following[1] == 0:
                gather_keys(following[0])
            tops[following] = forward_scores(*following)
        if at > 0:
            backward_outputs(*units[at - 1])
            if units[at - 1][1] == 1:
                send_out(units[at - 1][0])
        inverse = forward_probs(*unit, tops.pop(unit))
        delta = forward_outputs(*unit)
        backward_scores(*unit, inverse, delta)
    backward_outputs(*units[-1])
    send_out(units[-1][0])
    for copy in copies:
        copy.wait()


def sum_kernel(far_lengths, points, low, high, carried, *refs):
    far = len(far_lengths) // 2
    own_refs, partner_ref, next_ref = refs[:2], refs[2], refs[3]
    far_refs = refs[4 : 4 + 2 * far]
    outs = refs[4 + 2 * far + carried :]
    total, low_ref, sems = outs[-3:]
    near = partner_ref.shape[1]
    first = pl.multiple_of(jnp.where(is_even(), points - near, 0), 16)
    starts = (first, points - near - first)
    copies = []
    for slot in range(2):
        total[...] = own_refs[slot][...]
        for at, ref in enumerate((partner_ref, next_ref)):
            rows = pl.ds(pl.multiple_of(starts[at], 16), near)
            total[rows, :] += ref[slot].astype(jnp.float32)
        for at, (ref, length) in enumerate(zip(far_refs, far_lengths)):
            rows = slice(points - length, points) if at < far else slice(0, length)
            total[rows, :] += ref[slot].astype(jnp.float32)
        low_ref[slot] = total[...].astype(jnp.bfloat16)
        copy = pltpu.make_async_copy(
            low_ref.at[slot], outs[slot].at[:, low * PAIR : high * PAIR], sems.at[slot]
        )
        copy.start()
        copies.append(copy)
    for copy in copies:
        copy.wait()


def chunk_call(kernel, args, carried, count, out_shape, vmem_bytes, **options):
    vmem = pl.BlockSpec(memory_space=pltpu.VMEM)
    anywhere = pl.BlockSpec(memory_space=pl.ANY)
    return pl.pallas_call(
        functools.partial(kernel, len(carried)),
        in_specs=[vmem] * len(args) + [anywhere] * len(carried),
        out_specs=[anywhere] * count + [vmem] * (len(out_shape) - count),
        out_shape=out_shape,
        input_output_aliases={len(args) + at: at for at in range(len(carried))},
        compiler_params=pltpu.CompilerParams(vmem_limit_bytes=vmem_bytes),
        **options,
    )(*args, *carried)


def per_device(queries, keys, values, grad_out, windows):
    points, width = queries.shape
    rim_width, reach = reach_sizes(points, lax.axis_size("band"))
    band = lax.axis_index("band")
    near = min(points, rim_width)
    far = [d for d in range(-reach, reach + 1) if abs(d) > 1]
    far_sizes = [min(points, rim_width - (abs(d) - 1) * points) for d in far]
    lows = len(far) // 2
    lengths = far_sizes[:lows] + [near, near] + far_sizes[lows:]
    wide = points + 2 * rim_width
    reached = points // 2 + 2 * rim_width
    relative = (windows - band * points).T

    to_next, from_next, from_partner = [], [], []
    ready = (keys, values)
    for chunk, (low, high) in enumerate(spans(NEXT_CHUNKS)):
        to_next.append(pack(ready, near, low, high, f"pack_next_{chunk}"))
        from_next.append(swapped(to_next[chunk], 1))
        if chunk == 0:
            ready = lax.optimization_barrier((keys, values, to_next[0]))[:2]
            from_partner = [swapped(field, 0) for field in ready]
            ready = lax.optimization_barrier((keys, values, *from_partner))[:2]
        else:
            ready = lax.optimization_barrier((*ready, to_next[chunk], from_next[chunk - 1]))[:2]
    from_far = []
    for d, size in zip(far, far_sizes):
        part = slice(points - size, points) if d < 0 else slice(0, size)
        from_far.append(passed_along(jnp.stack([keys[part], values[part]]), -d))

    whole = jax.ShapeDtypeStruct((points, width), jnp.bfloat16)
    outs, own_terms, back_partner, back_next, back_far = [], [], [], [], []
    for chunk, (low, high) in enumerate(spans(CHUNKS)):
        count = high - low
        chunk_width = count * PAIR
        parts = [
            (at, last - first)
            for at, (first, last) in enumerate(spans(NEXT_CHUNKS))
            if low <= first and last <= high
        ]
        next_pairs = [size for _, size in parts]
        assert sum(next_pairs) == count
        outs = chunk_call(
            functools.partial(attention_kernel, rim_width, lengths, points, low, next_pairs),
            [relative, queries, grad_out, keys, values, *from_partner]
            + [from_next[at] for at, _ in parts]
            + from_far,
            outs[:2],
            2,
            [whole] * 2
            + [jax.ShapeDtypeStruct((2, near, chunk_width), jnp.bfloat16)] * 2
            + [jax.ShapeDtypeStruct((points, chunk_width), jnp.float32)] * 2
            + [jax.ShapeDtypeStruct((2, size, chunk_width), jnp.bfloat16) for size in far_sizes],
            48 * wide * points + 12 * 2**20,
            scratch_shapes=[
                pltpu.VMEM((2, reached, points), jnp.float32),
                pltpu.VMEM((2, 2, wide, PAIR), jnp.bfloat16),
                pltpu.VMEM((2, 2, PAIR, wide), jnp.bfloat16),
                pltpu.VMEM((2, 2, reached, points), jnp.float32),
                pltpu.VMEM((2, 2, reached, points), jnp.bfloat16),
                pltpu.VMEM((2, 2, reached, points), jnp.bfloat16),
                pltpu.VMEM((2, 2, wide, PAIR), jnp.float32),
                pltpu.VMEM((count, points, PAIR), jnp.bfloat16),
                pltpu.VMEM((count, points, PAIR), jnp.bfloat16),
                pltpu.SemaphoreType.DMA((2, count)),
            ],
            cost_estimate=pl.CostEstimate(
                flops=count * 120 * reached * points * PAIR,
                bytes_accessed=count * PAIR * (20 * points + 8 * wide),
                transcendentals=2 * count * points * reached,
            ),
            name=f"attention_{chunk}",
        )
        own_terms.append(outs[4:6])
        back_partner.append(swapped(outs[2], 0))
        back_next.append(swapped(outs[3], 1))
        back_far.append([passed_along(term, d) for term, d in zip(outs[6:], far)])

    grads = []
    for chunk, (low, high) in enumerate(spans(CHUNKS)):
        chunk_width = (high - low) * PAIR
        grads = chunk_call(
            functools.partial(sum_kernel, far_sizes, points, low, high),
            [*own_terms[chunk], back_partner[chunk], back_next[chunk], *back_far[chunk]],
            grads,
            2,
            [whole] * 2,
            12 * 2**20,
            scratch_shapes=[
                pltpu.VMEM((points, chunk_width), jnp.float32),
                pltpu.VMEM((2, points, chunk_width), jnp.bfloat16),
                pltpu.SemaphoreType.DMA((2,)),
            ],
            cost_estimate=pl.CostEstimate(
                flops=6 * points * chunk_width,
                bytes_accessed=20 * points * chunk_width,
                transcendentals=0,
            ),
            name=f"gradient_sums_{chunk}",
        )
    return (outs[0], outs[1], grads[0], grads[1])


def solution(mesh):
    spread = P(("members", "band"), None)
    return jax.shard_map(
        per_device,
        mesh=mesh,
        in_specs=(spread, spread, spread, spread, P("band", None)),
        out_specs=(spread, spread, spread, spread),
        check_vma=False,
    )
```

```python
import functools
import math

import jax
import jax.numpy as jnp
from jax import lax
from jax.experimental import pallas as pl
from jax.experimental.pallas import tpu as pltpu
from jax.sharding import PartitionSpec as P

HEADS = 16
HEAD_DIM = 64
ROWMIN = 20
STEP = 4
PAIR = 2 * HEAD_DIM
PAIRS = HEADS // 2
SCALE = HEAD_DIM**-0.5
LOG2_E = math.log2(math.e)
BLOCK = 32
OUTSIDE = -1e30
CHUNKS = (0, 4, 8)
NEXT_CHUNKS = (0, 2, 4, 8)


def reach_sizes(points, count):
    area_rows = points * count // STEP
    root_bound = min(((area_rows + 2 * 4**power) // (3 * 2**power) for power in range(3, 9)))
    grow_rows = root_bound - ROWMIN // STEP - 6
    row_longest = ROWMIN + STEP * (grow_rows - 1)
    rim_width = 2 * row_longest
    return (rim_width, (rim_width + points - 1) // points)


def spans(bounds):
    return list(zip(bounds[:-1], bounds[1:]))


def passed_along(value, steps):
    count = lax.axis_size("band")
    initial, last = (max(0, -steps), min(count, count - steps))
    return lax.ppermute(value, "band", [(source, source + steps) for source in range(initial, last)])


def swapped(value, first):
    count = lax.axis_size("band")
    pairs = [(at, at + 1) for at in range(first, count - 1, 2)]
    return lax.ppermute(value, "band", pairs + [(high, low) for low, high in pairs])


def dot_nt(left, right):
    return lax.dot_general(
        left, right, (((1,), (1,)), ((), ())), preferred_element_type=jnp.float32
    )


def dot_nn(left, right):
    return jnp.dot(left, right, preferred_element_type=jnp.float32)


def head_masks():
    lanes = lax.broadcasted_iota(jnp.int32, (1, PAIR), 1)
    first = (lanes < HEAD_DIM).astype(jnp.float32)
    return (first.astype(jnp.bfloat16), (1.0 - first).astype(jnp.bfloat16))


def is_even():
    return lax.axis_index("band") % 2 == 0


def pack(sources, rows, low, high):
    points = sources[0].shape[0]
    columns = slice(low * PAIR, high * PAIR)
    parts = [
        jnp.where(is_even(), field[:rows, columns], field[points - rows :, columns])
        for field in sources
    ]
    return jnp.stack(parts)


def padded(rows):
    return (rows + 15) // 16 * 16


def attention_kernel(rim_width, lengths, points, low_pair, next_pairs, carried, *refs):
    far = len(lengths) // 2 - 1
    near = lengths[far]
    half = points // 2
    rim = padded(rim_width)
    reached = half + 2 * rim
    wide = points + 2 * rim
    pairs = sum(next_pairs)
    win_ref, q_ref, g_ref, k_ref, v_ref, partner_k_ref, partner_v_ref = refs[:7]
    next_refs = refs[7 : 7 + len(next_pairs)]
    refs = refs[7 + len(next_pairs) :]
    far_refs = refs[: 2 * far]
    outs = refs[2 * far + carried :]
    att_out, dq_out, to_partner_ref, to_next_ref, dk_ref, dv_ref = outs[:6]
    to_far_refs = outs[6 : 6 + 2 * far]
    (bias_ref, keys_ref, turned_ref, exps_ref, probs_ref, dscores_ref, sums_ref, att_ref, dq_ref, sems) = outs[-10:]
    even = is_even()
    owns = [slice(part * half, (part + 1) * half) for part in range(2)]
    spans_of = [slice(part * half, part * half + reached) for part in range(2)]
    blocks = [slice(row, row + BLOCK) for row in range(0, reached, BLOCK)]
    masks = head_masks()

    for part, own in enumerate(owns):
        lower = jnp.concatenate([win_ref[0:1, own]] * 2, axis=1)
        upper = jnp.concatenate([win_ref[1:2, own]] * 2, axis=1)
        for block in blocks:
            keys = lax.broadcasted_iota(jnp.int32, (BLOCK, points), 0) + (part * half - rim + block.start)
            if rim > rim_width:
                below = jnp.where(keys < rim_width - rim, keys + (rim - rim_width), -wide)
                keys = jnp.where(keys < 0, below, jnp.where(keys < points + rim_width, keys, 2 * wide))
            inside = (keys >= lower) & (keys < upper)
            bias_ref[part, block, :] = jnp.where(inside, 0.0, OUTSIDE)

    if rim > rim_width:
        for gap in (slice(rim - 16, rim), slice(wide - 16, wide)):
            keys_ref[:, :, gap, :] = jnp.zeros((2, 2, 16, PAIR), jnp.bfloat16)

    where_next = [
        (chunk, at) for chunk, count in enumerate(next_pairs) for at in range(count)
    ]

    def columns_of(pair):
        return slice((low_pair + pair) * PAIR, (low_pair + pair + 1) * PAIR)

    def local_columns(pair):
        return slice(pair * PAIR, (pair + 1) * PAIR)

    def gather_keys(pair):
        columns = columns_of(pair)
        chunk, at = where_next[pair]
        next_columns = local_columns(at)
        into = keys_ref.at[pair % 2]
        for slot, (own_ref, partner_ref) in enumerate([(k_ref, partner_k_ref), (v_ref, partner_v_ref)]):
            start = 0
            for at in range(far):
                into[slot, start : start + lengths[at], :] = far_refs[at][slot, :, columns]
                start += lengths[at]
            into[slot, start : start + near, :] = jnp.where(
                even, next_refs[chunk][slot, :, next_columns], partner_ref[points - near :, columns]
            )
            into[slot, rim : rim + points, :] = own_ref[:, columns]
            start = rim + points
            into[slot, start : start + near, :] = jnp.where(
                even, partner_ref[:near, columns], next_refs[chunk][slot, :, next_columns]
            )
            start += near
            for at in range(far, 2 * far):
                into[slot, start : start + lengths[at + 2], :] = far_refs[at][slot, :, columns]
                start += lengths[at + 2]
            turned_ref[pair % 2, slot] = into[slot].T

    def fold(op, total, block):
        for row in range(0, BLOCK, 8):
            total = op(total, block[row : row + 8])
        return total

    def both(turned):
        return [turned[:HEAD_DIM, :half], turned[HEAD_DIM:, half:]]

    def q_both(pair, part):
        q = q_ref[owns[part], columns_of(pair)]
        return jnp.concatenate([q * (mask * SCALE) for mask in masks], axis=0)

    def g_both(pair, part):
        g = g_ref[owns[part], columns_of(pair)]
        return jnp.concatenate([g * mask for mask in masks], axis=0)

    def forward_scores(pair, part):
        exps = exps_ref.at[pair % 2, part]
        scores = dot_nt(keys_ref[pair % 2, 0, spans_of[part], :], q_both(pair, part))
        top = jnp.full((8, points), OUTSIDE, jnp.float32)
        for block in blocks:
            biased = scores[block] + bias_ref[part, block, :]
            exps[block, :] = biased
            top = fold(jnp.maximum, top, biased)
        return jnp.max(top, axis=0, keepdims=True)

    def forward_probs(pair, part, top):
        exps = exps_ref.at[pair % 2, part]
        total = jnp.zeros((8, points), jnp.float32)
        for block in blocks:
            values = jnp.exp2((exps[block, :] - top) * LOG2_E)
            exps[block, :] = values
            total = fold(jnp.add, total, values)
        inverse = 1.0 / jnp.sum(total, axis=0, keepdims=True)
        for block in blocks:
            probs_ref[pair % 2, part, block, :] = (exps[block, :] * inverse).astype(jnp.bfloat16)
        return inverse

    def forward_outputs(pair, part):
        own = owns[part]
        att = [
            x.astype(jnp.bfloat16)
            for x in both(
                dot_nn(turned_ref[pair % 2, 1, :, spans_of[part]], probs_ref[pair % 2, part])
            )
        ]
        att_ref[pair, own, :] = jnp.concatenate(att, axis=0).T
        g_turned = g_ref[own, columns_of(pair)].T
        return jnp.concatenate(
            [
                jnp.sum(
                    g_turned[head * HEAD_DIM : (head + 1) * HEAD_DIM].astype(jnp.float32)
                    * att[head].astype(jnp.float32),
                    axis=0,
                    keepdims=True,
                )
                for head in range(2)
            ],
            axis=1,
        )

    def backward_scores(pair, part, inverse, delta):
        dprobs = dot_nt(keys_ref[pair % 2, 1, spans_of[part], :], g_both(pair, part))
        for block in blocks:
            probs = exps_ref[pair % 2, part, block, :] * inverse
            dscores_ref[pair % 2, part, block, :] = (probs * (dprobs[block] - delta)).astype(jnp.bfloat16)

    def backward_outputs(pair, part):
        dscores = dscores_ref[pair % 2, part]
        dq = both(dot_nn(turned_ref[pair % 2, 0, :, spans_of[part]], dscores))
        dq_ref[pair, owns[part], :] = jnp.concatenate(
            [(x * SCALE).astype(jnp.bfloat16) for x in dq], axis=0
        ).T
        terms = (dot_nn(dscores, q_both(pair, part)), dot_nn(probs_ref[pair % 2, part], g_both(pair, part)))
        for slot, term in enumerate(terms):
            into = sums_ref.at[pair % 2, slot]
            if part == 0:
                into[:reached, :] = term
            else:
                into[half:reached, :] += term[: reached - half]
                into[reached:, :] = term[reached - half :]

    copies = []

    def send_out(pair):
        columns = local_columns(pair)
        for slot, own_ref in enumerate([dk_ref, dv_ref]):
            sums = sums_ref.at[pair % 2, slot]
            own_ref[:, columns] = sums[rim : rim + points, :]
            near_low = sums[rim_width - near : rim_width, :].astype(jnp.bfloat16)
            near_high = sums[rim + points : rim + points + near, :].astype(jnp.bfloat16)
            to_partner_ref[slot, :, columns] = jnp.where(even, near_high, near_low)
            to_next_ref[slot, :, columns] = jnp.where(even, near_low, near_high)
            start = 0
            for at in range(far):
                size = lengths[at]
                to_far_refs[at][slot, :, columns] = sums[start : start + size, :].astype(jnp.bfloat16)
                start += size
            start = rim + points + near
            for at in range(far, 2 * far):
                size = lengths[at + 2]
                to_far_refs[at][slot, :, columns] = sums[start : start + size, :].astype(jnp.bfloat16)
                start += size
        for at, (ref, out) in enumerate([(att_ref, att_out), (dq_ref, dq_out)]):
            copy = pltpu.make_async_copy(ref.at[pair], out.at[:, columns_of(pair)], sems.at[at, pair])
            copy.start()
            copies.append(copy)

    units = [(pair, part) for pair in range(pairs) for part in range(2)]
    gather_keys(0)
    tops = {units[0]: forward_scores(*units[0])}
    for at, unit in enumerate(units):
        if at + 1 < len(units):
            following = units[at + 1]
            if following[1] == 0:
                gather_keys(following[0])
            tops[following] = forward_scores(*following)
        if at > 0:
            backward_outputs(*units[at - 1])
            if units[at - 1][1] == 1:
                send_out(units[at - 1][0])
        inverse = forward_probs(*unit, tops.pop(unit))
        delta = forward_outputs(*unit)
        backward_scores(*unit, inverse, delta)
    backward_outputs(*units[-1])
    send_out(units[-1][0])
    for copy in copies:
        copy.wait()


def sum_kernel(far_lengths, points, low, high, carried, *refs):
    far = len(far_lengths) // 2
    own_refs, partner_ref, next_ref = refs[:2], refs[2], refs[3]
    far_refs = refs[4 : 4 + 2 * far]
    outs = refs[4 + 2 * far + carried :]
    total, low_ref, sems = outs[-3:]
    near = partner_ref.shape[1]
    first = pl.multiple_of(jnp.where(is_even(), points - near, 0), 8)
    starts = (first, points - near - first)
    copies = []
    for slot in range(2):
        total[...] = own_refs[slot][...]
        for at, ref in enumerate((partner_ref, next_ref)):
            rows = pl.ds(pl.multiple_of(starts[at], 8), near)
            total[rows, :] += ref[slot].astype(jnp.float32)
        for at, (ref, length) in enumerate(zip(far_refs, far_lengths)):
            rows = slice(points - length, points) if at < far else slice(0, length)
            total[rows, :] += ref[slot].astype(jnp.float32)
        low_ref[slot] = total[...].astype(jnp.bfloat16)
        copy = pltpu.make_async_copy(
            low_ref.at[slot], outs[slot].at[:, low * PAIR : high * PAIR], sems.at[slot]
        )
        copy.start()
        copies.append(copy)
    for copy in copies:
        copy.wait()


def chunk_call(kernel, args, carried, count, out_shape, vmem_bytes, **options):
    vmem = pl.BlockSpec(memory_space=pltpu.VMEM)
    anywhere = pl.BlockSpec(memory_space=pl.ANY)
    return pl.pallas_call(
        functools.partial(kernel, len(carried)),
        in_specs=[vmem] * len(args) + [anywhere] * len(carried),
        out_specs=[anywhere] * count + [vmem] * (len(out_shape) - count),
        out_shape=out_shape,
        input_output_aliases={len(args) + at: at for at in range(len(carried))},
        compiler_params=pltpu.CompilerParams(vmem_limit_bytes=vmem_bytes),
        **options,
    )(*args, *carried)


def per_device(queries, keys, values, grad_out, windows):
    points, width = queries.shape
    rim_width, reach = reach_sizes(points, lax.axis_size("band"))
    band = lax.axis_index("band")
    near = min(points, rim_width)
    far = [d for d in range(-reach, reach + 1) if abs(d) > 1]
    far_sizes = [min(points, rim_width - (abs(d) - 1) * points) for d in far]
    lows = len(far) // 2
    lengths = far_sizes[:lows] + [near, near] + far_sizes[lows:]
    wide = points + 2 * padded(rim_width)
    reached = points // 2 + 2 * padded(rim_width)
    relative = (windows - band * points).T

    to_next, from_next, from_partner = [], [], []
    ready = (keys, values)
    for chunk, (low, high) in enumerate(spans(NEXT_CHUNKS)):
        piece = pack(ready, near, low, high)
        to_next.append(piece)
        ready = lax.optimization_barrier((*ready, piece))[:2]
        if chunk > 1:
            piece = lax.optimization_barrier((piece, from_next[chunk - 2]))[0]
        from_next.append(swapped(piece, 1))
        if chunk == 0:
            from_partner = [swapped(field, 0) for field in ready]
        elif chunk == 1:
            ready = lax.optimization_barrier((*ready, *from_partner))[:2]
    from_far = []
    for d, size in zip(far, far_sizes):
        part = slice(points - size, points) if d < 0 else slice(0, size)
        from_far.append(passed_along(jnp.stack([keys[part], values[part]]), -d))

    whole = jax.ShapeDtypeStruct((points, width), jnp.bfloat16)
    outs, own_terms, back_partner, back_next, back_far = [], [], [], [], []
    for chunk, (low, high) in enumerate(spans(CHUNKS)):
        count = high - low
        chunk_width = count * PAIR
        parts = [
            (at, last - first)
            for at, (first, last) in enumerate(spans(NEXT_CHUNKS))
            if low <= first and last <= high
        ]
        next_pairs = [size for _, size in parts]
        assert sum(next_pairs) == count
        outs = chunk_call(
            functools.partial(attention_kernel, rim_width, lengths, points, low, next_pairs),
            [relative, queries, grad_out, keys, values, *from_partner]
            + [from_next[at] for at, _ in parts]
            + from_far,
            outs[:2],
            2,
            [whole] * 2
            + [jax.ShapeDtypeStruct((2, near, chunk_width), jnp.bfloat16)] * 2
            + [jax.ShapeDtypeStruct((points, chunk_width), jnp.float32)] * 2
            + [jax.ShapeDtypeStruct((2, size, chunk_width), jnp.bfloat16) for size in far_sizes],
            48 * wide * points + 12 * 2**20,
            scratch_shapes=[
                pltpu.VMEM((2, reached, points), jnp.float32),
                pltpu.VMEM((2, 2, wide, PAIR), jnp.bfloat16),
                pltpu.VMEM((2, 2, PAIR, wide), jnp.bfloat16),
                pltpu.VMEM((2, 2, reached, points), jnp.float32),
                pltpu.VMEM((2, 2, reached, points), jnp.bfloat16),
                pltpu.VMEM((2, 2, reached, points), jnp.bfloat16),
                pltpu.VMEM((2, 2, wide, PAIR), jnp.float32),
                pltpu.VMEM((count, points, PAIR), jnp.bfloat16),
                pltpu.VMEM((count, points, PAIR), jnp.bfloat16),
                pltpu.SemaphoreType.DMA((2, count)),
            ],
            cost_estimate=pl.CostEstimate(
                flops=count * 120 * reached * points * PAIR,
                bytes_accessed=count * PAIR * (20 * points + 8 * wide),
                transcendentals=2 * count * points * reached,
            ),
            name=f"attention_{chunk}",
        )
        own_terms.append(outs[4:6])
        back_partner.append(swapped(outs[2], 0))
        back_next.append(swapped(outs[3], 1))
        back_far.append([passed_along(term, d) for term, d in zip(outs[6:], far)])

    grads = []
    for chunk, (low, high) in enumerate(spans(CHUNKS)):
        chunk_width = (high - low) * PAIR
        grads = chunk_call(
            functools.partial(sum_kernel, far_sizes, points, low, high),
            [*own_terms[chunk], back_partner[chunk], back_next[chunk], *back_far[chunk]],
            grads,
            2,
            [whole] * 2,
            12 * 2**20,
            scratch_shapes=[
                pltpu.VMEM((points, chunk_width), jnp.float32),
                pltpu.VMEM((2, points, chunk_width), jnp.bfloat16),
                pltpu.SemaphoreType.DMA((2,)),
            ],
            cost_estimate=pl.CostEstimate(
                flops=6 * points * chunk_width,
                bytes_accessed=20 * points * chunk_width,
                transcendentals=0,
            ),
            name=f"gradient_sums_{chunk}",
        )
    return (outs[0], outs[1], grads[0], grads[1])


def solution(mesh):
    spread = P(("members", "band"), None)
    return jax.shard_map(
        per_device,
        mesh=mesh,
        in_specs=(spread, spread, spread, spread, P("band", None)),
        out_specs=(spread, spread, spread, spread),
        check_vma=False,
    )
```

```python
import functools
import math

import jax
import jax.numpy as jnp
from jax import lax
from jax.experimental import pallas as pl
from jax.experimental.pallas import tpu as pltpu
from jax.sharding import PartitionSpec as P

HEADS = 16
HEAD_DIM = 64
ROWMIN = 20
STEP = 4
PAIR = 2 * HEAD_DIM
PAIRS = HEADS // 2
SCALE = HEAD_DIM**-0.5
LOG2_E = math.log2(math.e)
BLOCK = 32
OUTSIDE = -1e30
CHUNKS = (0, 4, 8)
NEXT_CHUNKS = (0, 2, 4, 8)


def reach_sizes(points, count):
    area_rows = points * count // STEP
    root_bound = min(((area_rows + 2 * 4**power) // (3 * 2**power) for power in range(3, 9)))
    grow_rows = root_bound - ROWMIN // STEP - 6
    row_longest = ROWMIN + STEP * (grow_rows - 1)
    rim_width = 2 * row_longest
    return (rim_width, (rim_width + points - 1) // points)


def spans(bounds):
    return list(zip(bounds[:-1], bounds[1:]))


def passed_along(value, steps):
    count = lax.axis_size("band")
    initial, last = (max(0, -steps), min(count, count - steps))
    return lax.ppermute(value, "band", [(source, source + steps) for source in range(initial, last)])


def swapped(value, first):
    count = lax.axis_size("band")
    pairs = [(at, at + 1) for at in range(first, count - 1, 2)]
    return lax.ppermute(value, "band", pairs + [(high, low) for low, high in pairs])


def dot_nt(left, right):
    return lax.dot_general(
        left, right, (((1,), (1,)), ((), ())), preferred_element_type=jnp.float32
    )


def dot_nn(left, right):
    return jnp.dot(left, right, preferred_element_type=jnp.float32)


def head_masks():
    lanes = lax.broadcasted_iota(jnp.int32, (1, PAIR), 1)
    first = (lanes < HEAD_DIM).astype(jnp.float32)
    return (first.astype(jnp.bfloat16), (1.0 - first).astype(jnp.bfloat16))


def is_even():
    return lax.axis_index("band") % 2 == 0


def pack(sources, rows, low, high):
    points = sources[0].shape[0]
    columns = slice(low * PAIR, high * PAIR)
    first = jnp.stack([field[:rows, columns] for field in sources])
    last = jnp.stack([field[points - rows :, columns] for field in sources])
    return jnp.where(is_even(), first, last)


def padded(rows):
    return (rows + 15) // 16 * 16


def attention_kernel(rim_width, lengths, points, low_pair, next_pairs, carried, *refs):
    far = len(lengths) // 2 - 1
    near = lengths[far]
    half = points // 2
    rim = padded(rim_width)
    reached = half + 2 * rim
    wide = points + 2 * rim
    pairs = sum(next_pairs)
    win_ref, q_ref, g_ref, k_ref, v_ref, partner_k_ref, partner_v_ref = refs[:7]
    next_refs = refs[7 : 7 + len(next_pairs)]
    refs = refs[7 + len(next_pairs) :]
    far_refs = refs[: 2 * far]
    outs = refs[2 * far + carried :]
    att_out, dq_out, to_partner_ref, to_next_ref, dk_ref, dv_ref = outs[:6]
    to_far_refs = outs[6 : 6 + 2 * far]
    (bias_ref, keys_ref, turned_ref, exps_ref, probs_ref, dscores_ref, att_ref, dq_ref, sems) = outs[-9:]
    even = is_even()
    owns = [slice(part * half, (part + 1) * half) for part in range(2)]
    spans_of = [slice(part * half, part * half + reached) for part in range(2)]
    blocks = [slice(row, row + BLOCK) for row in range(0, reached, BLOCK)]
    masks = head_masks()

    for part, own in enumerate(owns):
        lower = jnp.concatenate([win_ref[0:1, own]] * 2, axis=1)
        upper = jnp.concatenate([win_ref[1:2, own]] * 2, axis=1)
        for block in blocks:
            keys = lax.broadcasted_iota(jnp.int32, (BLOCK, points), 0) + (part * half - rim + block.start)
            if rim > rim_width:
                below = jnp.where(keys < rim_width - rim, keys + (rim - rim_width), -wide)
                keys = jnp.where(keys < 0, below, jnp.where(keys < points + rim_width, keys, 2 * wide))
            inside = (keys >= lower) & (keys < upper)
            bias_ref[part, block, :] = jnp.where(inside, 0.0, OUTSIDE)

    if rim > rim_width:
        for gap in (slice(rim - 16, rim), slice(wide - 16, wide)):
            keys_ref[:, :, gap, :] = jnp.zeros((2, 2, 16, PAIR), jnp.bfloat16)

    where_next = [
        (chunk, at) for chunk, count in enumerate(next_pairs) for at in range(count)
    ]

    def columns_of(pair):
        return slice((low_pair + pair) * PAIR, (low_pair + pair + 1) * PAIR)

    def local_columns(pair):
        return slice(pair * PAIR, (pair + 1) * PAIR)

    def gather_keys(pair):
        columns = columns_of(pair)
        chunk, at = where_next[pair]
        next_columns = local_columns(at)
        into = keys_ref.at[pair % 2]
        for slot, (own_ref, partner_ref) in enumerate([(k_ref, partner_k_ref), (v_ref, partner_v_ref)]):
            start = 0
            for at in range(far):
                into[slot, start : start + lengths[at], :] = far_refs[at][slot, :, columns]
                start += lengths[at]
            into[slot, start : start + near, :] = jnp.where(
                even, next_refs[chunk][slot, :, next_columns], partner_ref[points - near :, columns]
            )
            into[slot, rim : rim + points, :] = own_ref[:, columns]
            start = rim + points
            into[slot, start : start + near, :] = jnp.where(
                even, partner_ref[:near, columns], next_refs[chunk][slot, :, next_columns]
            )
            start += near
            for at in range(far, 2 * far):
                into[slot, start : start + lengths[at + 2], :] = far_refs[at][slot, :, columns]
                start += lengths[at + 2]
            turned_ref[pair % 2, slot] = into[slot].T

    def fold(op, total, block):
        for row in range(0, BLOCK, 8):
            total = op(total, block[row : row + 8])
        return total

    def both(turned):
        return [turned[:HEAD_DIM, :half], turned[HEAD_DIM:, half:]]

    def q_both(pair, part):
        q = q_ref[owns[part], columns_of(pair)]
        return jnp.concatenate([q * (mask * SCALE) for mask in masks], axis=0)

    def g_both(pair, part):
        g = g_ref[owns[part], columns_of(pair)]
        return jnp.concatenate([g * mask for mask in masks], axis=0)

    def forward_scores(pair, part):
        exps = exps_ref.at[pair % 2, part]
        scores = dot_nt(keys_ref[pair % 2, 0, spans_of[part], :], q_both(pair, part))
        top = jnp.full((8, points), OUTSIDE, jnp.float32)
        for block in blocks:
            biased = scores[block] + bias_ref[part, block, :]
            exps[block, :] = biased
            top = fold(jnp.maximum, top, biased)
        return jnp.max(top, axis=0, keepdims=True)

    def forward_probs(pair, part, top):
        exps = exps_ref.at[pair % 2, part]
        total = jnp.zeros((8, points), jnp.float32)
        for block in blocks:
            values = jnp.exp2((exps[block, :] - top) * LOG2_E)
            exps[block, :] = values
            total = fold(jnp.add, total, values)
        inverse = 1.0 / jnp.sum(total, axis=0, keepdims=True)
        for block in blocks:
            probs_ref[pair % 2, part, block, :] = (exps[block, :] * inverse).astype(jnp.bfloat16)
        return inverse

    def forward_outputs(pair, part):
        own = owns[part]
        att = [
            x.astype(jnp.bfloat16)
            for x in both(
                dot_nn(turned_ref[pair % 2, 1, :, spans_of[part]], probs_ref[pair % 2, part])
            )
        ]
        att_ref[pair, own, :] = jnp.concatenate(att, axis=0).T
        g_turned = g_ref[own, columns_of(pair)].T
        return jnp.concatenate(
            [
                jnp.sum(
                    g_turned[head * HEAD_DIM : (head + 1) * HEAD_DIM].astype(jnp.float32)
                    * att[head].astype(jnp.float32),
                    axis=0,
                    keepdims=True,
                )
                for head in range(2)
            ],
            axis=1,
        )

    def backward_scores(pair, part, inverse, delta):
        dprobs = dot_nt(keys_ref[pair % 2, 1, spans_of[part], :], g_both(pair, part))
        for block in blocks:
            probs = exps_ref[pair % 2, part, block, :] * inverse
            dscores_ref[pair % 2, part, block, :] = (probs * (dprobs[block] - delta)).astype(jnp.bfloat16)

    copies = []

    def backward_outputs(pair):
        for part in range(2):
            dq = both(dot_nn(turned_ref[pair % 2, 0, :, spans_of[part]], dscores_ref[pair % 2, part]))
            dq_ref[pair, owns[part], :] = jnp.concatenate(
                [(x * SCALE).astype(jnp.bfloat16) for x in dq], axis=0
            ).T
        for slot, (scores_ref, own_both, own_ref) in enumerate(
            [(dscores_ref, q_both, dk_ref), (probs_ref, g_both, dv_ref)]
        ):
            low_scores, high_scores = (scores_ref.at[pair % 2, part] for part in range(2))
            low, high = (own_both(pair, part) for part in range(2))
            shared = jnp.concatenate([low_scores[half:, :], high_scores[: reached - half, :]], axis=1)
            sums = [
                dot_nn(low_scores[:half, :], low),
                dot_nn(shared, jnp.concatenate([low, high], axis=0)),
                dot_nn(high_scores[reached - half :, :], high),
            ]
            send_out(pair, slot, own_ref, sums)

    def send_out(pair, slot, own_ref, sums):
        columns = local_columns(pair)
        bounds = spans((0, half, reached, wide))

        def rows(start, stop):
            pieces = [
                term[max(start, first) - first : min(stop, last) - first]
                for term, (first, last) in zip(sums, bounds)
                if start < last and stop > first
            ]
            return jnp.concatenate(pieces, axis=0)

        own_ref[:, columns] = rows(rim, rim + points)
        near_low = rows(rim_width - near, rim_width).astype(jnp.bfloat16)
        near_high = rows(rim + points, rim + points + near).astype(jnp.bfloat16)
        to_partner_ref[slot, :, columns] = jnp.where(even, near_high, near_low)
        to_next_ref[slot, :, columns] = jnp.where(even, near_low, near_high)
        start = 0
        for at in range(far):
            to_far_refs[at][slot, :, columns] = rows(start, start + lengths[at]).astype(jnp.bfloat16)
            start += lengths[at]
        start = rim + points + near
        for at in range(far, 2 * far):
            size = lengths[at + 2]
            to_far_refs[at][slot, :, columns] = rows(start, start + size).astype(jnp.bfloat16)
            start += size

    def finish(pair):
        backward_outputs(pair)
        for at, (ref, out) in enumerate([(att_ref, att_out), (dq_ref, dq_out)]):
            copy = pltpu.make_async_copy(ref.at[pair], out.at[:, columns_of(pair)], sems.at[at, pair])
            copy.start()
            copies.append(copy)

    units = [(pair, part) for pair in range(pairs) for part in range(2)]
    gather_keys(0)
    tops = {units[0]: forward_scores(*units[0])}
    for at, unit in enumerate(units):
        if at + 1 < len(units):
            following = units[at + 1]
            if following[1] == 0:
                gather_keys(following[0])
            tops[following] = forward_scores(*following)
        if unit[1] == 0 and unit[0] > 0:
            finish(unit[0] - 1)
        inverse = forward_probs(*unit, tops.pop(unit))
        delta = forward_outputs(*unit)
        backward_scores(*unit, inverse, delta)
    finish(units[-1][0])
    for copy in copies:
        copy.wait()


def sum_kernel(far_lengths, points, low, high, carried, *refs):
    far = len(far_lengths) // 2
    own_refs, partner_ref, next_ref = refs[:2], refs[2], refs[3]
    far_refs = refs[4 : 4 + 2 * far]
    outs = refs[4 + 2 * far + carried :]
    total, low_ref, sems = outs[-3:]
    near = partner_ref.shape[1]
    first = pl.multiple_of(jnp.where(is_even(), points - near, 0), 8)
    starts = (first, points - near - first)
    copies = []
    for slot in range(2):
        total[...] = own_refs[slot][...]
        for at, ref in enumerate((partner_ref, next_ref)):
            rows = pl.ds(pl.multiple_of(starts[at], 8), near)
            total[rows, :] += ref[slot].astype(jnp.float32)
        for at, (ref, length) in enumerate(zip(far_refs, far_lengths)):
            rows = slice(points - length, points) if at < far else slice(0, length)
            total[rows, :] += ref[slot].astype(jnp.float32)
        low_ref[slot] = total[...].astype(jnp.bfloat16)
        copy = pltpu.make_async_copy(
            low_ref.at[slot], outs[slot].at[:, low * PAIR : high * PAIR], sems.at[slot]
        )
        copy.start()
        copies.append(copy)
    for copy in copies:
        copy.wait()


def chunk_call(kernel, args, carried, count, out_shape, vmem_bytes, **options):
    vmem = pl.BlockSpec(memory_space=pltpu.VMEM)
    anywhere = pl.BlockSpec(memory_space=pl.ANY)
    return pl.pallas_call(
        functools.partial(kernel, len(carried)),
        in_specs=[vmem] * len(args) + [anywhere] * len(carried),
        out_specs=[anywhere] * count + [vmem] * (len(out_shape) - count),
        out_shape=out_shape,
        input_output_aliases={len(args) + at: at for at in range(len(carried))},
        compiler_params=pltpu.CompilerParams(vmem_limit_bytes=vmem_bytes),
        **options,
    )(*args, *carried)


def per_device(queries, keys, values, grad_out, windows):
    points, width = queries.shape
    rim_width, reach = reach_sizes(points, lax.axis_size("band"))
    band = lax.axis_index("band")
    near = min(points, rim_width)
    far = [d for d in range(-reach, reach + 1) if abs(d) > 1]
    far_sizes = [min(points, rim_width - (abs(d) - 1) * points) for d in far]
    lows = len(far) // 2
    lengths = far_sizes[:lows] + [near, near] + far_sizes[lows:]
    wide = points + 2 * padded(rim_width)
    reached = points // 2 + 2 * padded(rim_width)
    relative = (windows - band * points).T

    to_next, from_next, from_partner = [], [], []
    ready = (keys, values)
    for chunk, (low, high) in enumerate(spans(NEXT_CHUNKS)):
        piece = pack(ready, near, low, high)
        to_next.append(piece)
        ready = lax.optimization_barrier((*ready, piece))[:2]
        if chunk > 1:
            piece = lax.optimization_barrier((piece, from_next[chunk - 2]))[0]
        from_next.append(swapped(piece, 1))
        if chunk == 0:
            from_partner = [swapped(field, 0) for field in ready]
        elif chunk == 1:
            ready = lax.optimization_barrier((*ready, *from_partner))[:2]
    from_far = []
    for d, size in zip(far, far_sizes):
        part = slice(points - size, points) if d < 0 else slice(0, size)
        from_far.append(passed_along(jnp.stack([keys[part], values[part]]), -d))

    whole = jax.ShapeDtypeStruct((points, width), jnp.bfloat16)
    outs, own_terms, back_partner, back_next, back_far = [], [], [], [], []
    for chunk, (low, high) in enumerate(spans(CHUNKS)):
        count = high - low
        chunk_width = count * PAIR
        parts = [
            (at, last - first)
            for at, (first, last) in enumerate(spans(NEXT_CHUNKS))
            if low <= first and last <= high
        ]
        next_pairs = [size for _, size in parts]
        assert sum(next_pairs) == count
        outs = chunk_call(
            functools.partial(attention_kernel, rim_width, lengths, points, low, next_pairs),
            [relative, queries, grad_out, keys, values, *from_partner]
            + [from_next[at] for at, _ in parts]
            + from_far,
            outs[:2],
            2,
            [whole] * 2
            + [jax.ShapeDtypeStruct((2, near, chunk_width), jnp.bfloat16)] * 2
            + [jax.ShapeDtypeStruct((points, chunk_width), jnp.float32)] * 2
            + [jax.ShapeDtypeStruct((2, size, chunk_width), jnp.bfloat16) for size in far_sizes],
            48 * wide * points + 12 * 2**20,
            scratch_shapes=[
                pltpu.VMEM((2, reached, points), jnp.float32),
                pltpu.VMEM((2, 2, wide, PAIR), jnp.bfloat16),
                pltpu.VMEM((2, 2, PAIR, wide), jnp.bfloat16),
                pltpu.VMEM((2, 2, reached, points), jnp.float32),
                pltpu.VMEM((2, 2, reached, points), jnp.bfloat16),
                pltpu.VMEM((2, 2, reached, points), jnp.bfloat16),
                pltpu.VMEM((count, points, PAIR), jnp.bfloat16),
                pltpu.VMEM((count, points, PAIR), jnp.bfloat16),
                pltpu.SemaphoreType.DMA((2, count)),
            ],
            cost_estimate=pl.CostEstimate(
                flops=count * 120 * reached * points * PAIR,
                bytes_accessed=count * PAIR * (20 * points + 8 * wide),
                transcendentals=2 * count * points * reached,
            ),
            name=f"attention_{chunk}",
        )
        own_terms.append(outs[4:6])
        back_partner.append(swapped(outs[2], 0))
        back_next.append(swapped(outs[3], 1))
        back_far.append([passed_along(term, d) for term, d in zip(outs[6:], far)])

    grads = []
    for chunk, (low, high) in enumerate(spans(CHUNKS)):
        chunk_width = (high - low) * PAIR
        grads = chunk_call(
            functools.partial(sum_kernel, far_sizes, points, low, high),
            [*own_terms[chunk], back_partner[chunk], back_next[chunk], *back_far[chunk]],
            grads,
            2,
            [whole] * 2,
            12 * 2**20,
            scratch_shapes=[
                pltpu.VMEM((points, chunk_width), jnp.float32),
                pltpu.VMEM((2, points, chunk_width), jnp.bfloat16),
                pltpu.SemaphoreType.DMA((2,)),
            ],
            cost_estimate=pl.CostEstimate(
                flops=6 * points * chunk_width,
                bytes_accessed=20 * points * chunk_width,
                transcendentals=0,
            ),
            name=f"gradient_sums_{chunk}",
        )
    return (outs[0], outs[1], grads[0], grads[1])


def solution(mesh):
    spread = P(("members", "band"), None)
    return jax.shard_map(
        per_device,
        mesh=mesh,
        in_specs=(spread, spread, spread, spread, P("band", None)),
        out_specs=(spread, spread, spread, spread),
        check_vma=False,
    )
```

```python
import functools
import math

import jax
import jax.numpy as jnp
from jax import lax
from jax.experimental import pallas as pl
from jax.experimental.pallas import tpu as pltpu
from jax.sharding import PartitionSpec as P

HEADS = 16
HEAD_DIM = 64
ROWMIN = 20
STEP = 4
PAIR = 2 * HEAD_DIM
PAIRS = HEADS // 2
SCALE = HEAD_DIM**-0.5
LOG2_E = math.log2(math.e)
BLOCK = 32
OUTSIDE = -1e30
CHUNKS = (0, 4, 8)
NEXT_CHUNKS = (0, 2, 4, 8)


def reach_sizes(points, count):
    area_rows = points * count // STEP
    root_bound = min(((area_rows + 2 * 4**power) // (3 * 2**power) for power in range(3, 9)))
    grow_rows = root_bound - ROWMIN // STEP - 6
    row_longest = ROWMIN + STEP * (grow_rows - 1)
    rim_width = 2 * row_longest
    return (rim_width, (rim_width + points - 1) // points)


def spans(bounds):
    return list(zip(bounds[:-1], bounds[1:]))


def passed_along(value, steps):
    count = lax.axis_size("band")
    initial, last = (max(0, -steps), min(count, count - steps))
    return lax.ppermute(value, "band", [(source, source + steps) for source in range(initial, last)])


def swapped(value, first):
    count = lax.axis_size("band")
    pairs = [(at, at + 1) for at in range(first, count - 1, 2)]
    return lax.ppermute(value, "band", pairs + [(high, low) for low, high in pairs])


def dot_nt(left, right):
    return lax.dot_general(
        left, right, (((1,), (1,)), ((), ())), preferred_element_type=jnp.float32
    )


def dot_nn(left, right):
    return jnp.dot(left, right, preferred_element_type=jnp.float32)


def head_masks():
    lanes = lax.broadcasted_iota(jnp.int32, (1, PAIR), 1)
    first = (lanes < HEAD_DIM).astype(jnp.float32)
    return (first.astype(jnp.bfloat16), (1.0 - first).astype(jnp.bfloat16))


def is_even():
    return lax.axis_index("band") % 2 == 0


def pack(sources, rows, low, high):
    points = sources[0].shape[0]
    columns = slice(low * PAIR, high * PAIR)
    first = jnp.stack([field[:rows, columns] for field in sources])
    last = jnp.stack([field[points - rows :, columns] for field in sources])
    return jnp.where(is_even(), first, last)


def padded(rows):
    return (rows + 15) // 16 * 16


def attention_kernel(rim_width, lengths, points, low_pair, next_pairs, carried, *refs):
    far = len(lengths) // 2 - 1
    near = lengths[far]
    half = points // 2
    rim = padded(rim_width)
    reached = half + 2 * rim
    wide = points + 2 * rim
    pairs = sum(next_pairs)
    win_ref, q_ref, g_ref, k_ref, v_ref, partner_k_ref, partner_v_ref = refs[:7]
    next_refs = refs[7 : 7 + len(next_pairs)]
    refs = refs[7 + len(next_pairs) :]
    far_refs = refs[: 2 * far]
    outs = refs[2 * far + carried :]
    att_out, dq_out, to_partner_ref, to_next_ref, dk_ref, dv_ref = outs[:6]
    to_far_refs = outs[6 : 6 + 2 * far]
    (bias_ref, keys_ref, turned_ref, exps_ref, probs_ref, dscores_ref, att_ref, dq_ref, sems) = outs[-9:]
    even = is_even()
    owns = [slice(part * half, (part + 1) * half) for part in range(2)]
    spans_of = [slice(part * half, part * half + reached) for part in range(2)]
    blocks = [slice(row, row + BLOCK) for row in range(0, reached, BLOCK)]
    masks = head_masks()

    for part, own in enumerate(owns):
        lower = jnp.concatenate([win_ref[0:1, own]] * 2, axis=1)
        upper = jnp.concatenate([win_ref[1:2, own]] * 2, axis=1)
        for block in blocks:
            keys = lax.broadcasted_iota(jnp.int32, (BLOCK, points), 0) + (part * half - rim + block.start)
            if rim > rim_width:
                below = jnp.where(keys < rim_width - rim, keys + (rim - rim_width), -wide)
                keys = jnp.where(keys < 0, below, jnp.where(keys < points + rim_width, keys, 2 * wide))
            inside = (keys >= lower) & (keys < upper)
            bias_ref[part, block, :] = jnp.where(inside, 0.0, OUTSIDE)

    if rim > rim_width:
        for gap in (slice(rim - 16, rim), slice(wide - 16, wide)):
            keys_ref[:, :, gap, :] = jnp.zeros((2, 2, 16, PAIR), jnp.bfloat16)

    where_next = [
        (chunk, at) for chunk, count in enumerate(next_pairs) for at in range(count)
    ]

    def columns_of(pair):
        return slice((low_pair + pair) * PAIR, (low_pair + pair + 1) * PAIR)

    def local_columns(pair):
        return slice(pair * PAIR, (pair + 1) * PAIR)

    def gather_keys(pair):
        columns = columns_of(pair)
        chunk, at = where_next[pair]
        next_columns = local_columns(at)
        into = keys_ref.at[pair % 2]
        for slot, (own_ref, partner_ref) in enumerate([(k_ref, partner_k_ref), (v_ref, partner_v_ref)]):
            start = 0
            for at in range(far):
                into[slot, start : start + lengths[at], :] = far_refs[at][slot, :, columns]
                start += lengths[at]
            into[slot, start : start + near, :] = jnp.where(
                even, next_refs[chunk][slot, :, next_columns], partner_ref[points - near :, columns]
            )
            into[slot, rim : rim + points, :] = own_ref[:, columns]
            start = rim + points
            into[slot, start : start + near, :] = jnp.where(
                even, partner_ref[:near, columns], next_refs[chunk][slot, :, next_columns]
            )
            start += near
            for at in range(far, 2 * far):
                into[slot, start : start + lengths[at + 2], :] = far_refs[at][slot, :, columns]
                start += lengths[at + 2]
            turned_ref[pair % 2, slot] = into[slot].T

    def fold(op, total, block):
        for row in range(0, BLOCK, 8):
            total = op(total, block[row : row + 8])
        return total

    def both(turned):
        return [turned[:HEAD_DIM, :half], turned[HEAD_DIM:, half:]]

    def q_both(pair, part):
        q = q_ref[owns[part], columns_of(pair)]
        return jnp.concatenate([q * (mask * SCALE) for mask in masks], axis=0)

    def g_both(pair, part):
        g = g_ref[owns[part], columns_of(pair)]
        return jnp.concatenate([g * mask for mask in masks], axis=0)

    def forward_scores(pair, part):
        exps = exps_ref.at[pair % 2, part]
        scores = dot_nt(keys_ref[pair % 2, 0, spans_of[part], :], q_both(pair, part))
        top = jnp.full((8, points), OUTSIDE, jnp.float32)
        for block in blocks:
            biased = scores[block] + bias_ref[part, block, :]
            exps[block, :] = biased
            top = fold(jnp.maximum, top, biased)
        return jnp.max(top, axis=0, keepdims=True)

    def forward_probs(pair, part, top):
        exps = exps_ref.at[pair % 2, part]
        total = jnp.zeros((8, points), jnp.float32)
        for block in blocks:
            values = jnp.exp2((exps[block, :] - top) * LOG2_E)
            exps[block, :] = values
            total = fold(jnp.add, total, values)
        inverse = 1.0 / jnp.sum(total, axis=0, keepdims=True)
        for block in blocks:
            probs_ref[pair % 2, part, block, :] = (exps[block, :] * inverse).astype(jnp.bfloat16)
        return inverse

    def forward_outputs(pair, part):
        own = owns[part]
        att = [
            x.astype(jnp.bfloat16)
            for x in both(
                dot_nn(turned_ref[pair % 2, 1, :, spans_of[part]], probs_ref[pair % 2, part])
            )
        ]
        att_ref[pair, own, :] = jnp.concatenate(att, axis=0).T
        g_turned = g_ref[own, columns_of(pair)].T
        return jnp.concatenate(
            [
                jnp.sum(
                    g_turned[head * HEAD_DIM : (head + 1) * HEAD_DIM].astype(jnp.float32)
                    * att[head].astype(jnp.float32),
                    axis=0,
                    keepdims=True,
                )
                for head in range(2)
            ],
            axis=1,
        )

    def backward_scores(pair, part, inverse, delta):
        dprobs = dot_nt(keys_ref[pair % 2, 1, spans_of[part], :], g_both(pair, part))
        for block in blocks:
            probs = exps_ref[pair % 2, part, block, :] * inverse
            dscores_ref[pair % 2, part, block, :] = (probs * (dprobs[block] - delta)).astype(jnp.bfloat16)

    copies = []

    def backward_outputs(pair):
        for part in range(2):
            dq = both(dot_nn(turned_ref[pair % 2, 0, :, spans_of[part]], dscores_ref[pair % 2, part]))
            dq_ref[pair, owns[part], :] = jnp.concatenate(
                [(x * SCALE).astype(jnp.bfloat16) for x in dq], axis=0
            ).T
        for slot, (scores_ref, own_both, own_ref) in enumerate(
            [(dscores_ref, q_both, dk_ref), (probs_ref, g_both, dv_ref)]
        ):
            low_scores, high_scores = (scores_ref.at[pair % 2, part] for part in range(2))
            low, high = (own_both(pair, part) for part in range(2))
            shared = jnp.concatenate([low_scores[half:, :], high_scores[: reached - half, :]], axis=1)
            sums = [
                dot_nn(low_scores[:half, :], low),
                dot_nn(shared, jnp.concatenate([low, high], axis=0)),
                dot_nn(high_scores[reached - half :, :], high),
            ]
            send_out(pair, slot, own_ref, sums)

    def send_out(pair, slot, own_ref, sums):
        columns = local_columns(pair)
        bounds = spans((0, half, reached, wide))

        def rows(start, stop):
            pieces = [
                term[max(start, first) - first : min(stop, last) - first]
                for term, (first, last) in zip(sums, bounds)
                if start < last and stop > first
            ]
            return jnp.concatenate(pieces, axis=0)

        own_ref[:, columns] = rows(rim, rim + points)
        near_low = rows(rim_width - near, rim_width).astype(jnp.bfloat16)
        near_high = rows(rim + points, rim + points + near).astype(jnp.bfloat16)
        to_partner_ref[slot, :, columns] = jnp.where(even, near_high, near_low)
        to_next_ref[slot, :, columns] = jnp.where(even, near_low, near_high)
        start = 0
        for at in range(far):
            to_far_refs[at][slot, :, columns] = rows(start, start + lengths[at]).astype(jnp.bfloat16)
            start += lengths[at]
        start = rim + points + near
        for at in range(far, 2 * far):
            size = lengths[at + 2]
            to_far_refs[at][slot, :, columns] = rows(start, start + size).astype(jnp.bfloat16)
            start += size

    def finish(pair):
        backward_outputs(pair)
        for at, (ref, out) in enumerate([(att_ref, att_out), (dq_ref, dq_out)]):
            copy = pltpu.make_async_copy(ref.at[pair], out.at[:, columns_of(pair)], sems.at[at, pair])
            copy.start()
            copies.append(copy)

    units = [(pair, part) for pair in range(pairs) for part in range(2)]
    gather_keys(0)
    top = forward_scores(*units[0])
    for at, unit in enumerate(units):
        if unit[1] == 0 and unit[0] > 0:
            finish(unit[0] - 1)
        inverse = forward_probs(*unit, top)
        delta = forward_outputs(*unit)
        if at + 1 < len(units):
            if units[at + 1][1] == 0:
                gather_keys(units[at + 1][0])
            top = forward_scores(*units[at + 1])
        backward_scores(*unit, inverse, delta)
    finish(units[-1][0])
    for copy in copies:
        copy.wait()


def sum_kernel(far_lengths, points, low, high, carried, *refs):
    far = len(far_lengths) // 2
    own_refs, partner_ref, next_ref = refs[:2], refs[2], refs[3]
    far_refs = refs[4 : 4 + 2 * far]
    outs = refs[4 + 2 * far + carried :]
    total, low_ref, sems = outs[-3:]
    near = partner_ref.shape[1]
    first = pl.multiple_of(jnp.where(is_even(), points - near, 0), 8)
    starts = (first, points - near - first)
    copies = []
    for slot in range(2):
        total[...] = own_refs[slot][...]
        for at, ref in enumerate((partner_ref, next_ref)):
            rows = pl.ds(pl.multiple_of(starts[at], 8), near)
            total[rows, :] += ref[slot].astype(jnp.float32)
        for at, (ref, length) in enumerate(zip(far_refs, far_lengths)):
            rows = slice(points - length, points) if at < far else slice(0, length)
            total[rows, :] += ref[slot].astype(jnp.float32)
        low_ref[slot] = total[...].astype(jnp.bfloat16)
        copy = pltpu.make_async_copy(
            low_ref.at[slot], outs[slot].at[:, low * PAIR : high * PAIR], sems.at[slot]
        )
        copy.start()
        copies.append(copy)
    for copy in copies:
        copy.wait()


def chunk_call(kernel, args, carried, count, out_shape, vmem_bytes, **options):
    vmem = pl.BlockSpec(memory_space=pltpu.VMEM)
    anywhere = pl.BlockSpec(memory_space=pl.ANY)
    return pl.pallas_call(
        functools.partial(kernel, len(carried)),
        in_specs=[vmem] * len(args) + [anywhere] * len(carried),
        out_specs=[anywhere] * count + [vmem] * (len(out_shape) - count),
        out_shape=out_shape,
        input_output_aliases={len(args) + at: at for at in range(len(carried))},
        compiler_params=pltpu.CompilerParams(vmem_limit_bytes=vmem_bytes),
        **options,
    )(*args, *carried)


def per_device(queries, keys, values, grad_out, windows):
    points, width = queries.shape
    rim_width, reach = reach_sizes(points, lax.axis_size("band"))
    band = lax.axis_index("band")
    near = min(points, rim_width)
    far = [d for d in range(-reach, reach + 1) if abs(d) > 1]
    far_sizes = [min(points, rim_width - (abs(d) - 1) * points) for d in far]
    lows = len(far) // 2
    lengths = far_sizes[:lows] + [near, near] + far_sizes[lows:]
    wide = points + 2 * padded(rim_width)
    reached = points // 2 + 2 * padded(rim_width)
    relative = (windows - band * points).T

    to_next, from_next, from_partner = [], [], []
    ready = (keys, values)
    for chunk, (low, high) in enumerate(spans(NEXT_CHUNKS)):
        piece = pack(ready, near, low, high)
        to_next.append(piece)
        ready = lax.optimization_barrier((*ready, piece))[:2]
        if chunk > 1:
            piece = lax.optimization_barrier((piece, from_next[chunk - 2]))[0]
        from_next.append(swapped(piece, 1))
        if chunk == 0:
            from_partner = [swapped(field, 0) for field in ready]
        elif chunk == 1:
            ready = lax.optimization_barrier((*ready, *from_partner))[:2]
    from_far = []
    for d, size in zip(far, far_sizes):
        part = slice(points - size, points) if d < 0 else slice(0, size)
        from_far.append(passed_along(jnp.stack([keys[part], values[part]]), -d))

    whole = jax.ShapeDtypeStruct((points, width), jnp.bfloat16)
    outs, own_terms, back_partner, back_next, back_far = [], [], [], [], []
    for chunk, (low, high) in enumerate(spans(CHUNKS)):
        count = high - low
        chunk_width = count * PAIR
        parts = [
            (at, last - first)
            for at, (first, last) in enumerate(spans(NEXT_CHUNKS))
            if low <= first and last <= high
        ]
        next_pairs = [size for _, size in parts]
        assert sum(next_pairs) == count
        outs = chunk_call(
            functools.partial(attention_kernel, rim_width, lengths, points, low, next_pairs),
            [relative, queries, grad_out, keys, values, *from_partner]
            + [from_next[at] for at, _ in parts]
            + from_far,
            outs[:2],
            2,
            [whole] * 2
            + [jax.ShapeDtypeStruct((2, near, chunk_width), jnp.bfloat16)] * 2
            + [jax.ShapeDtypeStruct((points, chunk_width), jnp.float32)] * 2
            + [jax.ShapeDtypeStruct((2, size, chunk_width), jnp.bfloat16) for size in far_sizes],
            48 * wide * points + 12 * 2**20,
            scratch_shapes=[
                pltpu.VMEM((2, reached, points), jnp.float32),
                pltpu.VMEM((2, 2, wide, PAIR), jnp.bfloat16),
                pltpu.VMEM((2, 2, PAIR, wide), jnp.bfloat16),
                pltpu.VMEM((2, 2, reached, points), jnp.float32),
                pltpu.VMEM((2, 2, reached, points), jnp.bfloat16),
                pltpu.VMEM((2, 2, reached, points), jnp.bfloat16),
                pltpu.VMEM((count, points, PAIR), jnp.bfloat16),
                pltpu.VMEM((count, points, PAIR), jnp.bfloat16),
                pltpu.SemaphoreType.DMA((2, count)),
            ],
            cost_estimate=pl.CostEstimate(
                flops=count * 120 * reached * points * PAIR,
                bytes_accessed=count * PAIR * (20 * points + 8 * wide),
                transcendentals=2 * count * points * reached,
            ),
            name=f"attention_{chunk}",
        )
        own_terms.append(outs[4:6])
        back_partner.append(swapped(outs[2], 0))
        back_next.append(swapped(outs[3], 1))
        back_far.append([passed_along(term, d) for term, d in zip(outs[6:], far)])

    grads = []
    for chunk, (low, high) in enumerate(spans(CHUNKS)):
        chunk_width = (high - low) * PAIR
        grads = chunk_call(
            functools.partial(sum_kernel, far_sizes, points, low, high),
            [*own_terms[chunk], back_partner[chunk], back_next[chunk], *back_far[chunk]],
            grads,
            2,
            [whole] * 2,
            12 * 2**20,
            scratch_shapes=[
                pltpu.VMEM((points, chunk_width), jnp.float32),
                pltpu.VMEM((2, points, chunk_width), jnp.bfloat16),
                pltpu.SemaphoreType.DMA((2,)),
            ],
            cost_estimate=pl.CostEstimate(
                flops=6 * points * chunk_width,
                bytes_accessed=20 * points * chunk_width,
                transcendentals=0,
            ),
            name=f"gradient_sums_{chunk}",
        )
    return (outs[0], outs[1], grads[0], grads[1])


def solution(mesh):
    spread = P(("members", "band"), None)
    return jax.shard_map(
        per_device,
        mesh=mesh,
        in_specs=(spread, spread, spread, spread, P("band", None)),
        out_specs=(spread, spread, spread, spread),
        check_vma=False,
    )
```

```python
import functools
import math

import jax
import jax.numpy as jnp
from jax import lax
from jax.experimental import pallas as pl
from jax.experimental.pallas import tpu as pltpu
from jax.sharding import PartitionSpec as P

HEADS = 16
HEAD_DIM = 64
ROWMIN = 20
STEP = 4
PAIR = 2 * HEAD_DIM
PAIRS = HEADS // 2
SCALE = HEAD_DIM**-0.5
LOG2_E = math.log2(math.e)
BLOCK = 32
COST = 120
OUTSIDE = -1e30
CHUNKS = (0, 4, 8)
NEXT_CHUNKS = (0, 2, 4, 8)
CALLS = (0, 2, 4, 8)


def reach_sizes(points, count):
    area_rows = points * count // STEP
    root_bound = min(((area_rows + 2 * 4**power) // (3 * 2**power) for power in range(3, 9)))
    grow_rows = root_bound - ROWMIN // STEP - 6
    row_longest = ROWMIN + STEP * (grow_rows - 1)
    rim_width = 2 * row_longest
    return (rim_width, (rim_width + points - 1) // points)


def spans(bounds):
    return list(zip(bounds[:-1], bounds[1:]))


def passed_along(value, steps):
    count = lax.axis_size("band")
    initial, last = (max(0, -steps), min(count, count - steps))
    return lax.ppermute(value, "band", [(source, source + steps) for source in range(initial, last)])


def swapped(value, first):
    count = lax.axis_size("band")
    pairs = [(at, at + 1) for at in range(first, count - 1, 2)]
    return lax.ppermute(value, "band", pairs + [(high, low) for low, high in pairs])


def dot_nt(left, right):
    return lax.dot_general(
        left, right, (((1,), (1,)), ((), ())), preferred_element_type=jnp.float32
    )


def dot_nn(left, right):
    return jnp.dot(left, right, preferred_element_type=jnp.float32)


def head_masks():
    lanes = lax.broadcasted_iota(jnp.int32, (1, PAIR), 1)
    first = (lanes < HEAD_DIM).astype(jnp.float32)
    return (first.astype(jnp.bfloat16), (1.0 - first).astype(jnp.bfloat16))


def is_even():
    return lax.axis_index("band") % 2 == 0


def pack(sources, rows, low, high):
    points = sources[0].shape[0]
    columns = slice(low * PAIR, high * PAIR)
    first = jnp.stack([field[:rows, columns] for field in sources])
    last = jnp.stack([field[points - rows :, columns] for field in sources])
    return jnp.where(is_even(), first, last)


def padded(rows):
    return (rows + 15) // 16 * 16


def attention_kernel(rim_width, lengths, points, low_pair, next_pairs, earlier, carried, *refs):
    far = len(lengths) // 2 - 1
    near = lengths[far]
    half = points // 2
    rim = padded(rim_width)
    reached = half + 2 * rim
    wide = points + 2 * rim
    pairs = sum(next_pairs)
    win_ref, q_ref, g_ref, k_ref, v_ref, partner_k_ref, partner_v_ref = refs[:7]
    next_refs = refs[7 : 7 + len(next_pairs)]
    refs = refs[7 + len(next_pairs) :]
    far_refs = refs[: 2 * far]
    before_refs = refs[2 * far : 2 * far + (1 if earlier else 0)]
    outs = refs[2 * far + len(before_refs) + carried :]
    att_out, dq_out, to_partner_ref, to_next_ref, dk_ref, dv_ref = outs[:6]
    to_far_refs = outs[6 : 6 + 2 * far]
    (bias_ref, keys_ref, turned_ref, exps_ref, probs_ref, dscores_ref, att_ref, dq_ref, sems) = outs[-9:]
    even = is_even()
    owns = [slice(part * half, (part + 1) * half) for part in range(2)]
    spans_of = [slice(part * half, part * half + reached) for part in range(2)]
    blocks = [slice(row, row + BLOCK) for row in range(0, reached, BLOCK)]
    masks = head_masks()

    for part, own in enumerate(owns):
        lower = jnp.concatenate([win_ref[0:1, own]] * 2, axis=1)
        upper = jnp.concatenate([win_ref[1:2, own]] * 2, axis=1)
        for block in blocks:
            keys = lax.broadcasted_iota(jnp.int32, (BLOCK, points), 0) + (part * half - rim + block.start)
            if rim > rim_width:
                below = jnp.where(keys < rim_width - rim, keys + (rim - rim_width), -wide)
                keys = jnp.where(keys < 0, below, jnp.where(keys < points + rim_width, keys, 2 * wide))
            inside = (keys >= lower) & (keys < upper)
            bias_ref[part, block, :] = jnp.where(inside, 0.0, OUTSIDE)

    if rim > rim_width:
        for gap in (slice(rim - 16, rim), slice(wide - 16, wide)):
            keys_ref[:, :, gap, :] = jnp.zeros((2, 2, 16, PAIR), jnp.bfloat16)

    if earlier:
        to_next_ref[:, :, : earlier * PAIR] = before_refs[0][...]

    where_next = [
        (chunk, at) for chunk, count in enumerate(next_pairs) for at in range(count)
    ]

    def columns_of(pair):
        return slice((low_pair + pair) * PAIR, (low_pair + pair + 1) * PAIR)

    def local_columns(pair):
        return slice(pair * PAIR, (pair + 1) * PAIR)

    def gather_keys(pair):
        columns = columns_of(pair)
        chunk, at = where_next[pair]
        next_columns = local_columns(at)
        into = keys_ref.at[pair % 2]
        for slot, (own_ref, partner_ref) in enumerate([(k_ref, partner_k_ref), (v_ref, partner_v_ref)]):
            start = 0
            for at in range(far):
                into[slot, start : start + lengths[at], :] = far_refs[at][slot, :, columns]
                start += lengths[at]
            into[slot, start : start + near, :] = jnp.where(
                even, next_refs[chunk][slot, :, next_columns], partner_ref[points - near :, columns]
            )
            into[slot, rim : rim + points, :] = own_ref[:, columns]
            start = rim + points
            into[slot, start : start + near, :] = jnp.where(
                even, partner_ref[:near, columns], next_refs[chunk][slot, :, next_columns]
            )
            start += near
            for at in range(far, 2 * far):
                into[slot, start : start + lengths[at + 2], :] = far_refs[at][slot, :, columns]
                start += lengths[at + 2]
            turned_ref[pair % 2, slot] = into[slot].T

    def fold(op, total, block):
        for row in range(0, BLOCK, 8):
            total = op(total, block[row : row + 8])
        return total

    def both(turned):
        return [turned[:HEAD_DIM, :half], turned[HEAD_DIM:, half:]]

    def q_both(pair, part):
        q = q_ref[owns[part], columns_of(pair)]
        return jnp.concatenate([q * (mask * SCALE) for mask in masks], axis=0)

    def g_both(pair, part):
        g = g_ref[owns[part], columns_of(pair)]
        return jnp.concatenate([g * mask for mask in masks], axis=0)

    def forward_scores(pair, part):
        exps = exps_ref.at[pair % 2, part]
        scores = dot_nt(keys_ref[pair % 2, 0, spans_of[part], :], q_both(pair, part))
        top = jnp.full((8, points), OUTSIDE, jnp.float32)
        for block in blocks:
            biased = scores[block] + bias_ref[part, block, :]
            exps[block, :] = biased
            top = fold(jnp.maximum, top, biased)
        return jnp.max(top, axis=0, keepdims=True)

    def forward_probs(pair, part, top):
        exps = exps_ref.at[pair % 2, part]
        total = jnp.zeros((8, points), jnp.float32)
        for block in blocks:
            values = jnp.exp2((exps[block, :] - top) * LOG2_E)
            exps[block, :] = values
            total = fold(jnp.add, total, values)
        inverse = 1.0 / jnp.sum(total, axis=0, keepdims=True)
        for block in blocks:
            probs_ref[pair % 2, part, block, :] = (exps[block, :] * inverse).astype(jnp.bfloat16)
        return inverse

    def forward_outputs(pair, part):
        own = owns[part]
        att = [
            x.astype(jnp.bfloat16)
            for x in both(
                dot_nn(turned_ref[pair % 2, 1, :, spans_of[part]], probs_ref[pair % 2, part])
            )
        ]
        att_ref[pair, own, :] = jnp.concatenate(att, axis=0).T
        g_turned = g_ref[own, columns_of(pair)].T
        return jnp.concatenate(
            [
                jnp.sum(
                    g_turned[head * HEAD_DIM : (head + 1) * HEAD_DIM].astype(jnp.float32)
                    * att[head].astype(jnp.float32),
                    axis=0,
                    keepdims=True,
                )
                for head in range(2)
            ],
            axis=1,
        )

    def backward_scores(pair, part, inverse, delta):
        dprobs = dot_nt(keys_ref[pair % 2, 1, spans_of[part], :], g_both(pair, part))
        for block in blocks:
            probs = exps_ref[pair % 2, part, block, :] * inverse
            dscores_ref[pair % 2, part, block, :] = (probs * (dprobs[block] - delta)).astype(jnp.bfloat16)

    copies = []

    def backward_queries(pair, part):
        dq = both(dot_nn(turned_ref[pair % 2, 0, :, spans_of[part]], dscores_ref[pair % 2, part]))
        dq_ref[pair, owns[part], :] = jnp.concatenate(
            [(x * SCALE).astype(jnp.bfloat16) for x in dq], axis=0
        ).T
        if part == 1:
            for at, (ref, out) in enumerate([(att_ref, att_out), (dq_ref, dq_out)]):
                copy = pltpu.make_async_copy(
                    ref.at[pair], out.at[:, columns_of(pair)], sems.at[at, pair]
                )
                copy.start()
                copies.append(copy)

    def backward_keys(pair, slot):
        scores_ref, own_both, own_ref = [(dscores_ref, q_both, dk_ref), (probs_ref, g_both, dv_ref)][slot]
        low_scores, high_scores = (scores_ref.at[pair % 2, part] for part in range(2))
        low, high = (own_both(pair, part) for part in range(2))
        shared = jnp.concatenate([low_scores[half:, :], high_scores[: reached - half, :]], axis=1)
        sums = [
            dot_nn(low_scores[:half, :], low),
            dot_nn(shared, jnp.concatenate([low, high], axis=0)),
            dot_nn(high_scores[reached - half :, :], high),
        ]
        send_out(pair, slot, own_ref, sums)

    def send_out(pair, slot, own_ref, sums):
        columns = local_columns(pair)
        bounds = spans((0, half, reached, wide))

        def rows(start, stop):
            pieces = [
                term[max(start, first) - first : min(stop, last) - first]
                for term, (first, last) in zip(sums, bounds)
                if start < last and stop > first
            ]
            return jnp.concatenate(pieces, axis=0)

        own_ref[:, columns] = rows(rim, rim + points)
        near_low = rows(rim_width - near, rim_width).astype(jnp.bfloat16)
        near_high = rows(rim + points, rim + points + near).astype(jnp.bfloat16)
        to_partner_ref[slot, :, columns] = jnp.where(even, near_high, near_low)
        to_next_ref[slot, :, local_columns(earlier + pair)] = jnp.where(even, near_low, near_high)
        start = 0
        for at in range(far):
            to_far_refs[at][slot, :, columns] = rows(start, start + lengths[at]).astype(jnp.bfloat16)
            start += lengths[at]
        start = rim + points + near
        for at in range(far, 2 * far):
            size = lengths[at + 2]
            to_far_refs[at][slot, :, columns] = rows(start, start + size).astype(jnp.bfloat16)
            start += size

    units = [(pair, part) for pair in range(pairs) for part in range(2)]
    gather_keys(0)
    tops = {units[0]: forward_scores(*units[0])}
    for at, unit in enumerate(units):
        pair, part = unit
        if at + 1 < len(units):
            following = units[at + 1]
            if following[1] == 0:
                gather_keys(following[0])
            tops[following] = forward_scores(*following)
        if at > 0:
            backward_queries(*units[at - 1])
        if pair > 0:
            backward_keys(pair - 1, part)
        inverse = forward_probs(*unit, tops.pop(unit))
        delta = forward_outputs(*unit)
        backward_scores(*unit, inverse, delta)
    backward_queries(*units[-1])
    backward_keys(pairs - 1, 0)
    backward_keys(pairs - 1, 1)
    for copy in copies:
        copy.wait()


def sum_kernel(far_lengths, points, low, high, parts, carried, *refs):
    far = len(far_lengths) // 2
    part_refs, refs = [refs[3 * at : 3 * at + 3] for at in range(len(parts))], refs[3 * len(parts) :]
    far_refs, refs = [refs[2 * far * at : 2 * far * (at + 1)] for at in range(len(parts))], refs[2 * far * len(parts) :]
    next_ref, outs = refs[0], refs[1 + carried :]
    total, low_ref, sems = outs[-3:]
    near = next_ref.shape[1]
    first = pl.multiple_of(jnp.where(is_even(), points - near, 0), 8)
    partner_rows = pl.ds(first, near)
    next_rows = pl.ds(pl.multiple_of(points - near - first, 8), near)
    copies = []
    for slot in range(2):
        start = 0
        for pairs, part, fars in zip(parts, part_refs, far_refs):
            columns = slice(start * PAIR, (start + pairs) * PAIR)
            start += pairs
            total[:, columns] = part[slot][...]
            total[partner_rows, columns] += part[2][slot].astype(jnp.float32)
            for at, (ref, length) in enumerate(zip(fars, far_lengths)):
                rows = slice(points - length, points) if at < far else slice(0, length)
                total[rows, columns] += ref[slot].astype(jnp.float32)
        total[next_rows, :] += next_ref[slot].astype(jnp.float32)
        low_ref[slot] = total[...].astype(jnp.bfloat16)
        copy = pltpu.make_async_copy(
            low_ref.at[slot], outs[slot].at[:, low * PAIR : high * PAIR], sems.at[slot]
        )
        copy.start()
        copies.append(copy)
    for copy in copies:
        copy.wait()


def chunk_call(kernel, args, carried, count, out_shape, vmem_bytes, **options):
    vmem = pl.BlockSpec(memory_space=pltpu.VMEM)
    anywhere = pl.BlockSpec(memory_space=pl.ANY)
    return pl.pallas_call(
        functools.partial(kernel, len(carried)),
        in_specs=[vmem] * len(args) + [anywhere] * len(carried),
        out_specs=[anywhere] * count + [vmem] * (len(out_shape) - count),
        out_shape=out_shape,
        input_output_aliases={len(args) + at: at for at in range(len(carried))},
        compiler_params=pltpu.CompilerParams(vmem_limit_bytes=vmem_bytes),
        **options,
    )(*args, *carried)


def per_device(queries, keys, values, grad_out, windows):
    points, width = queries.shape
    rim_width, reach = reach_sizes(points, lax.axis_size("band"))
    band = lax.axis_index("band")
    near = min(points, rim_width)
    far = [d for d in range(-reach, reach + 1) if abs(d) > 1]
    far_sizes = [min(points, rim_width - (abs(d) - 1) * points) for d in far]
    lows = len(far) // 2
    lengths = far_sizes[:lows] + [near, near] + far_sizes[lows:]
    wide = points + 2 * padded(rim_width)
    reached = points // 2 + 2 * padded(rim_width)
    relative = (windows - band * points).T

    to_next, from_next, from_partner = [], [], []
    ready = (keys, values)
    for chunk, (low, high) in enumerate(spans(NEXT_CHUNKS)):
        piece = pack(ready, near, low, high)
        to_next.append(piece)
        ready = lax.optimization_barrier((*ready, piece))[:2]
        from_next.append(swapped(piece, 1))
        if chunk == 0:
            from_partner = [swapped(field, 0) for field in ready]
        elif chunk == 1:
            ready = lax.optimization_barrier((*ready, *from_partner))[:2]
    from_far = []
    for d, size in zip(far, far_sizes):
        part = slice(points - size, points) if d < 0 else slice(0, size)
        from_far.append(passed_along(jnp.stack([keys[part], values[part]]), -d))

    whole = jax.ShapeDtypeStruct((points, width), jnp.bfloat16)
    outs, own_terms, back_next = [], [[] for _ in spans(CHUNKS)], []
    back_far = [[] for _ in spans(CHUNKS)]
    for call, (low, high) in enumerate(spans(CALLS)):
        count = high - low
        call_width = count * PAIR
        chunk, (first_pair, last_pair) = next(
            (at, bounds) for at, bounds in enumerate(spans(CHUNKS)) if bounds[0] <= low < bounds[1]
        )
        earlier = low - first_pair
        parts = [
            (at, last - first)
            for at, (first, last) in enumerate(spans(NEXT_CHUNKS))
            if low <= first and last <= high
        ]
        next_pairs = [size for _, size in parts]
        assert sum(next_pairs) == count
        outs = chunk_call(
            functools.partial(
                attention_kernel, rim_width, lengths, points, low, next_pairs, earlier
            ),
            [relative, queries, grad_out, keys, values, *from_partner]
            + [from_next[at] for at, _ in parts]
            + from_far
            + ([outs[3]] if earlier else []),
            outs[:2],
            2,
            [whole] * 2
            + [
                jax.ShapeDtypeStruct((2, near, call_width), jnp.bfloat16),
                jax.ShapeDtypeStruct((2, near, call_width + earlier * PAIR), jnp.bfloat16),
            ]
            + [jax.ShapeDtypeStruct((points, call_width), jnp.float32)] * 2
            + [jax.ShapeDtypeStruct((2, size, call_width), jnp.bfloat16) for size in far_sizes],
            48 * wide * points + 12 * 2**20,
            scratch_shapes=[
                pltpu.VMEM((2, reached, points), jnp.float32),
                pltpu.VMEM((2, 2, wide, PAIR), jnp.bfloat16),
                pltpu.VMEM((2, 2, PAIR, wide), jnp.bfloat16),
                pltpu.VMEM((2, 2, reached, points), jnp.float32),
                pltpu.VMEM((2, 2, reached, points), jnp.bfloat16),
                pltpu.VMEM((2, 2, reached, points), jnp.bfloat16),
                pltpu.VMEM((count, points, PAIR), jnp.bfloat16),
                pltpu.VMEM((count, points, PAIR), jnp.bfloat16),
                pltpu.SemaphoreType.DMA((2, count)),
            ],
            cost_estimate=pl.CostEstimate(
                flops=count * COST * reached * points * PAIR,
                bytes_accessed=count * PAIR * (20 * points + 8 * wide),
                transcendentals=2 * count * points * reached,
            ),
            name=f"attention_{call}",
        )
        own_terms[chunk] += [outs[4], outs[5], swapped(outs[2], 0)]
        back_far[chunk] += [passed_along(term, d) for term, d in zip(outs[6:], far)]
        if high == last_pair:
            back_next.append(swapped(outs[3], 1))

    grads = []
    for chunk, (low, high) in enumerate(spans(CHUNKS)):
        chunk_width = (high - low) * PAIR
        parts = [last - first for first, last in spans(CALLS) if low <= first and last <= high]
        grads = chunk_call(
            functools.partial(sum_kernel, far_sizes, points, low, high, parts),
            [*own_terms[chunk], *back_far[chunk], back_next[chunk]],
            grads,
            2,
            [whole] * 2,
            12 * 2**20,
            scratch_shapes=[
                pltpu.VMEM((points, chunk_width), jnp.float32),
                pltpu.VMEM((2, points, chunk_width), jnp.bfloat16),
                pltpu.SemaphoreType.DMA((2,)),
            ],
            cost_estimate=pl.CostEstimate(
                flops=6 * points * chunk_width,
                bytes_accessed=20 * points * chunk_width,
                transcendentals=0,
            ),
            name=f"gradient_sums_{chunk}",
        )
    return (outs[0], outs[1], grads[0], grads[1])


def solution(mesh):
    spread = P(("members", "band"), None)
    return jax.shard_map(
        per_device,
        mesh=mesh,
        in_specs=(spread, spread, spread, spread, P("band", None)),
        out_specs=(spread, spread, spread, spread),
        check_vma=False,
    )
```

```python
import functools
import math

import jax
import jax.numpy as jnp
from jax import lax
from jax.experimental import pallas as pl
from jax.experimental.pallas import tpu as pltpu
from jax.sharding import PartitionSpec as P

HEADS = 16
HEAD_DIM = 64
ROWMIN = 20
STEP = 4
PAIR = 2 * HEAD_DIM
PAIRS = HEADS // 2
SCALE = HEAD_DIM**-0.5
LOG2_E = math.log2(math.e)
BLOCK = 16
OUTSIDE = -1e30
CHUNKS = (0, 4, 8)
NEXT_CHUNKS = (0, 2, 4, 8)


def reach_sizes(points, count):
    area_rows = points * count // STEP
    root_bound = min(((area_rows + 2 * 4**power) // (3 * 2**power) for power in range(3, 9)))
    grow_rows = root_bound - ROWMIN // STEP - 6
    row_longest = ROWMIN + STEP * (grow_rows - 1)
    rim_width = 2 * row_longest
    return (rim_width, (rim_width + points - 1) // points)


def spans(bounds):
    return list(zip(bounds[:-1], bounds[1:]))


def passed_along(value, steps):
    count = lax.axis_size("band")
    initial, last = (max(0, -steps), min(count, count - steps))
    return lax.ppermute(value, "band", [(source, source + steps) for source in range(initial, last)])


def swapped(value, first):
    count = lax.axis_size("band")
    pairs = [(at, at + 1) for at in range(first, count - 1, 2)]
    return lax.ppermute(value, "band", pairs + [(high, low) for low, high in pairs])


def dot_nt(left, right):
    return lax.dot_general(
        left, right, (((1,), (1,)), ((), ())), preferred_element_type=jnp.float32
    )


def dot_nn(left, right):
    return jnp.dot(left, right, preferred_element_type=jnp.float32)


def head_masks():
    lanes = lax.broadcasted_iota(jnp.int32, (1, PAIR), 1)
    first = (lanes < HEAD_DIM).astype(jnp.float32)
    return (first.astype(jnp.bfloat16), (1.0 - first).astype(jnp.bfloat16))


def is_even():
    return lax.axis_index("band") % 2 == 0


def pack(sources, rows, low, high):
    points = sources[0].shape[0]
    columns = slice(low * PAIR, high * PAIR)
    first = jnp.stack([field[:rows, columns] for field in sources])
    last = jnp.stack([field[points - rows :, columns] for field in sources])
    return jnp.where(is_even(), first, last)


def padded(rows):
    return (rows + 15) // 16 * 16


def attention_kernel(rim_width, lengths, points, low_pair, next_pairs, carried, *refs):
    far = len(lengths) // 2 - 1
    near = lengths[far]
    half = points // 2
    rim = padded(rim_width)
    reached = half + 2 * rim
    wide = points + 2 * rim
    pairs = sum(next_pairs)
    win_ref, q_ref, g_ref, k_ref, v_ref, partner_k_ref, partner_v_ref = refs[:7]
    next_refs = refs[7 : 7 + len(next_pairs)]
    refs = refs[7 + len(next_pairs) :]
    far_refs = refs[: 2 * far]
    outs = refs[2 * far + carried :]
    att_out, dq_out, to_partner_ref, to_next_ref, dk_ref, dv_ref = outs[:6]
    to_far_refs = outs[6 : 6 + 2 * far]
    (bias_ref, keys_ref, turned_ref, exps_ref, probs_ref, dscores_ref, att_ref, dq_ref, sems) = outs[-9:]
    even = is_even()
    owns = [slice(part * half, (part + 1) * half) for part in range(2)]
    spans_of = [slice(part * half, part * half + reached) for part in range(2)]
    blocks = [slice(row, row + BLOCK) for row in range(0, reached, BLOCK)]
    masks = head_masks()

    for part, own in enumerate(owns):
        lower = jnp.concatenate([win_ref[0:1, own]] * 2, axis=1)
        upper = jnp.concatenate([win_ref[1:2, own]] * 2, axis=1)
        for block in blocks:
            keys = lax.broadcasted_iota(jnp.int32, (BLOCK, points), 0) + (part * half - rim + block.start)
            if rim > rim_width:
                below = jnp.where(keys < rim_width - rim, keys + (rim - rim_width), -wide)
                keys = jnp.where(keys < 0, below, jnp.where(keys < points + rim_width, keys, 2 * wide))
            inside = (keys >= lower) & (keys < upper)
            bias_ref[part, block, :] = jnp.where(inside, 0.0, OUTSIDE)

    if rim > rim_width:
        for gap in (slice(rim - 16, rim), slice(wide - 16, wide)):
            keys_ref[:, :, gap, :] = jnp.zeros((2, 2, 16, PAIR), jnp.bfloat16)

    where_next = [
        (chunk, at) for chunk, count in enumerate(next_pairs) for at in range(count)
    ]

    def columns_of(pair):
        return slice((low_pair + pair) * PAIR, (low_pair + pair + 1) * PAIR)

    def local_columns(pair):
        return slice(pair * PAIR, (pair + 1) * PAIR)

    def gather_keys(pair):
        columns = columns_of(pair)
        chunk, at = where_next[pair]
        next_columns = local_columns(at)
        into = keys_ref.at[pair % 2]
        for slot, (own_ref, partner_ref) in enumerate([(k_ref, partner_k_ref), (v_ref, partner_v_ref)]):
            start = 0
            for at in range(far):
                into[slot, start : start + lengths[at], :] = far_refs[at][slot, :, columns]
                start += lengths[at]
            into[slot, start : start + near, :] = jnp.where(
                even, next_refs[chunk][slot, :, next_columns], partner_ref[points - near :, columns]
            )
            into[slot, rim : rim + points, :] = own_ref[:, columns]
            start = rim + points
            into[slot, start : start + near, :] = jnp.where(
                even, partner_ref[:near, columns], next_refs[chunk][slot, :, next_columns]
            )
            start += near
            for at in range(far, 2 * far):
                into[slot, start : start + lengths[at + 2], :] = far_refs[at][slot, :, columns]
                start += lengths[at + 2]
            turned_ref[pair % 2, slot] = into[slot].T

    def fold(op, total, block):
        for row in range(0, BLOCK, 8):
            total = op(total, block[row : row + 8])
        return total

    def both(turned):
        return [turned[:HEAD_DIM, :half], turned[HEAD_DIM:, half:]]

    def q_both(pair, part):
        q = q_ref[owns[part], columns_of(pair)]
        return jnp.concatenate([q * (mask * SCALE) for mask in masks], axis=0)

    def g_both(pair, part):
        g = g_ref[owns[part], columns_of(pair)]
        return jnp.concatenate([g * mask for mask in masks], axis=0)

    def forward_scores(pair, part):
        exps = exps_ref.at[pair % 2, part]
        scores = dot_nt(keys_ref[pair % 2, 0, spans_of[part], :], q_both(pair, part))
        top = jnp.full((8, points), OUTSIDE, jnp.float32)
        for block in blocks:
            biased = scores[block] + bias_ref[part, block, :]
            exps[block, :] = biased
            top = fold(jnp.maximum, top, biased)
        return jnp.max(top, axis=0, keepdims=True)

    def forward_probs(pair, part, top):
        exps = exps_ref.at[pair % 2, part]
        total = jnp.zeros((8, points), jnp.float32)
        for block in blocks:
            values = jnp.exp2((exps[block, :] - top) * LOG2_E)
            exps[block, :] = values
            total = fold(jnp.add, total, values)
        inverse = 1.0 / jnp.sum(total, axis=0, keepdims=True)
        for block in blocks:
            probs_ref[pair % 2, part, block, :] = (exps[block, :] * inverse).astype(jnp.bfloat16)
        return inverse

    def forward_outputs(pair, part):
        own = owns[part]
        att = [
            x.astype(jnp.bfloat16)
            for x in both(
                dot_nn(turned_ref[pair % 2, 1, :, spans_of[part]], probs_ref[pair % 2, part])
            )
        ]
        att_ref[pair, own, :] = jnp.concatenate(att, axis=0).T
        g_turned = g_ref[own, columns_of(pair)].T
        return jnp.concatenate(
            [
                jnp.sum(
                    g_turned[head * HEAD_DIM : (head + 1) * HEAD_DIM].astype(jnp.float32)
                    * att[head].astype(jnp.float32),
                    axis=0,
                    keepdims=True,
                )
                for head in range(2)
            ],
            axis=1,
        )

    def backward_scores(pair, part, inverse, delta):
        dprobs = dot_nt(keys_ref[pair % 2, 1, spans_of[part], :], g_both(pair, part))
        for block in blocks:
            probs = exps_ref[pair % 2, part, block, :] * inverse
            dscores_ref[pair % 2, part, block, :] = (probs * (dprobs[block] - delta)).astype(jnp.bfloat16)

    copies = []

    def backward_outputs(pair):
        for part in range(2):
            dq = both(dot_nn(turned_ref[pair % 2, 0, :, spans_of[part]], dscores_ref[pair % 2, part]))
            dq_ref[pair, owns[part], :] = jnp.concatenate(
                [(x * SCALE).astype(jnp.bfloat16) for x in dq], axis=0
            ).T
        for slot, (scores_ref, own_both, own_ref) in enumerate(
            [(dscores_ref, q_both, dk_ref), (probs_ref, g_both, dv_ref)]
        ):
            low_scores, high_scores = (scores_ref.at[pair % 2, part] for part in range(2))
            low, high = (own_both(pair, part) for part in range(2))
            shared = jnp.concatenate([low_scores[half:, :], high_scores[: reached - half, :]], axis=1)
            sums = [
                dot_nn(low_scores[:half, :], low),
                dot_nn(shared, jnp.concatenate([low, high], axis=0)),
                dot_nn(high_scores[reached - half :, :], high),
            ]
            send_out(pair, slot, own_ref, sums)

    def send_out(pair, slot, own_ref, sums):
        columns = local_columns(pair)
        bounds = spans((0, half, reached, wide))

        def rows(start, stop):
            pieces = [
                term[max(start, first) - first : min(stop, last) - first]
                for term, (first, last) in zip(sums, bounds)
                if start < last and stop > first
            ]
            return jnp.concatenate(pieces, axis=0)

        own_ref[:, columns] = rows(rim, rim + points)
        near_low = rows(rim_width - near, rim_width).astype(jnp.bfloat16)
        near_high = rows(rim + points, rim + points + near).astype(jnp.bfloat16)
        to_partner_ref[slot, :, columns] = jnp.where(even, near_high, near_low)
        to_next_ref[slot, :, columns] = jnp.where(even, near_low, near_high)
        start = 0
        for at in range(far):
            to_far_refs[at][slot, :, columns] = rows(start, start + lengths[at]).astype(jnp.bfloat16)
            start += lengths[at]
        start = rim + points + near
        for at in range(far, 2 * far):
            size = lengths[at + 2]
            to_far_refs[at][slot, :, columns] = rows(start, start + size).astype(jnp.bfloat16)
            start += size

    def finish(pair):
        backward_outputs(pair)
        for at, (ref, out) in enumerate([(att_ref, att_out), (dq_ref, dq_out)]):
            copy = pltpu.make_async_copy(ref.at[pair], out.at[:, columns_of(pair)], sems.at[at, pair])
            copy.start()
            copies.append(copy)

    units = [(pair, part) for pair in range(pairs) for part in range(2)]
    gather_keys(0)
    tops = {units[0]: forward_scores(*units[0])}
    for at, unit in enumerate(units):
        if at + 1 < len(units):
            following = units[at + 1]
            if following[1] == 0:
                gather_keys(following[0])
            tops[following] = forward_scores(*following)
        if unit[1] == 0 and unit[0] > 0:
            finish(unit[0] - 1)
        inverse = forward_probs(*unit, tops.pop(unit))
        delta = forward_outputs(*unit)
        backward_scores(*unit, inverse, delta)
    finish(units[-1][0])
    for copy in copies:
        copy.wait()


def sum_kernel(far_lengths, points, low, high, carried, *refs):
    far = len(far_lengths) // 2
    own_refs, partner_ref, next_ref = refs[:2], refs[2], refs[3]
    far_refs = refs[4 : 4 + 2 * far]
    outs = refs[4 + 2 * far + carried :]
    total, low_ref, sems = outs[-3:]
    near = partner_ref.shape[1]
    first = pl.multiple_of(jnp.where(is_even(), points - near, 0), 8)
    starts = (first, points - near - first)
    copies = []
    for slot in range(2):
        total[...] = own_refs[slot][...]
        for at, ref in enumerate((partner_ref, next_ref)):
            rows = pl.ds(pl.multiple_of(starts[at], 8), near)
            total[rows, :] += ref[slot].astype(jnp.float32)
        for at, (ref, length) in enumerate(zip(far_refs, far_lengths)):
            rows = slice(points - length, points) if at < far else slice(0, length)
            total[rows, :] += ref[slot].astype(jnp.float32)
        low_ref[slot] = total[...].astype(jnp.bfloat16)
        copy = pltpu.make_async_copy(
            low_ref.at[slot], outs[slot].at[:, low * PAIR : high * PAIR], sems.at[slot]
        )
        copy.start()
        copies.append(copy)
    for copy in copies:
        copy.wait()


def chunk_call(kernel, args, carried, count, out_shape, vmem_bytes, **options):
    vmem = pl.BlockSpec(memory_space=pltpu.VMEM)
    anywhere = pl.BlockSpec(memory_space=pl.ANY)
    return pl.pallas_call(
        functools.partial(kernel, len(carried)),
        in_specs=[vmem] * len(args) + [anywhere] * len(carried),
        out_specs=[anywhere] * count + [vmem] * (len(out_shape) - count),
        out_shape=out_shape,
        input_output_aliases={len(args) + at: at for at in range(len(carried))},
        compiler_params=pltpu.CompilerParams(vmem_limit_bytes=vmem_bytes),
        **options,
    )(*args, *carried)


def per_device(queries, keys, values, grad_out, windows):
    points, width = queries.shape
    rim_width, reach = reach_sizes(points, lax.axis_size("band"))
    band = lax.axis_index("band")
    near = min(points, rim_width)
    far = [d for d in range(-reach, reach + 1) if abs(d) > 1]
    far_sizes = [min(points, rim_width - (abs(d) - 1) * points) for d in far]
    lows = len(far) // 2
    lengths = far_sizes[:lows] + [near, near] + far_sizes[lows:]
    wide = points + 2 * padded(rim_width)
    reached = points // 2 + 2 * padded(rim_width)
    relative = (windows - band * points).T

    to_next, from_next, from_partner = [], [], []
    ready = (keys, values)
    for chunk, (low, high) in enumerate(spans(NEXT_CHUNKS)):
        piece = pack(ready, near, low, high)
        to_next.append(piece)
        ready = lax.optimization_barrier((*ready, piece))[:2]
        if chunk > 1:
            piece = lax.optimization_barrier((piece, from_next[chunk - 2]))[0]
        from_next.append(swapped(piece, 1))
        if chunk == 0:
            from_partner = [swapped(field, 0) for field in ready]
        elif chunk == 1:
            ready = lax.optimization_barrier((*ready, *from_partner))[:2]
    from_far = []
    for d, size in zip(far, far_sizes):
        part = slice(points - size, points) if d < 0 else slice(0, size)
        from_far.append(passed_along(jnp.stack([keys[part], values[part]]), -d))

    whole = jax.ShapeDtypeStruct((points, width), jnp.bfloat16)
    outs, own_terms, back_partner, back_next, back_far = [], [], [], [], []
    for chunk, (low, high) in enumerate(spans(CHUNKS)):
        count = high - low
        chunk_width = count * PAIR
        parts = [
            (at, last - first)
            for at, (first, last) in enumerate(spans(NEXT_CHUNKS))
            if low <= first and last <= high
        ]
        next_pairs = [size for _, size in parts]
        assert sum(next_pairs) == count
        outs = chunk_call(
            functools.partial(attention_kernel, rim_width, lengths, points, low, next_pairs),
            [relative, queries, grad_out, keys, values, *from_partner]
            + [from_next[at] for at, _ in parts]
            + from_far,
            outs[:2],
            2,
            [whole] * 2
            + [jax.ShapeDtypeStruct((2, near, chunk_width), jnp.bfloat16)] * 2
            + [jax.ShapeDtypeStruct((points, chunk_width), jnp.float32)] * 2
            + [jax.ShapeDtypeStruct((2, size, chunk_width), jnp.bfloat16) for size in far_sizes],
            48 * wide * points + 12 * 2**20,
            scratch_shapes=[
                pltpu.VMEM((2, reached, points), jnp.float32),
                pltpu.VMEM((2, 2, wide, PAIR), jnp.bfloat16),
                pltpu.VMEM((2, 2, PAIR, wide), jnp.bfloat16),
                pltpu.VMEM((2, 2, reached, points), jnp.float32),
                pltpu.VMEM((2, 2, reached, points), jnp.bfloat16),
                pltpu.VMEM((2, 2, reached, points), jnp.bfloat16),
                pltpu.VMEM((count, points, PAIR), jnp.bfloat16),
                pltpu.VMEM((count, points, PAIR), jnp.bfloat16),
                pltpu.SemaphoreType.DMA((2, count)),
            ],
            cost_estimate=pl.CostEstimate(
                flops=count * 120 * reached * points * PAIR,
                bytes_accessed=count * PAIR * (20 * points + 8 * wide),
                transcendentals=2 * count * points * reached,
            ),
            name=f"attention_{chunk}",
        )
        own_terms.append(outs[4:6])
        back_partner.append(swapped(outs[2], 0))
        back_next.append(swapped(outs[3], 1))
        back_far.append([passed_along(term, d) for term, d in zip(outs[6:], far)])

    grads = []
    for chunk, (low, high) in enumerate(spans(CHUNKS)):
        chunk_width = (high - low) * PAIR
        grads = chunk_call(
            functools.partial(sum_kernel, far_sizes, points, low, high),
            [*own_terms[chunk], back_partner[chunk], back_next[chunk], *back_far[chunk]],
            grads,
            2,
            [whole] * 2,
            12 * 2**20,
            scratch_shapes=[
                pltpu.VMEM((points, chunk_width), jnp.float32),
                pltpu.VMEM((2, points, chunk_width), jnp.bfloat16),
                pltpu.SemaphoreType.DMA((2,)),
            ],
            cost_estimate=pl.CostEstimate(
                flops=6 * points * chunk_width,
                bytes_accessed=20 * points * chunk_width,
                transcendentals=0,
            ),
            name=f"gradient_sums_{chunk}",
        )
    return (outs[0], outs[1], grads[0], grads[1])


def solution(mesh):
    spread = P(("members", "band"), None)
    return jax.shard_map(
        per_device,
        mesh=mesh,
        in_specs=(spread, spread, spread, spread, P("band", None)),
        out_specs=(spread, spread, spread, spread),
        check_vma=False,
    )
```

```python
import functools
import math

import jax
import jax.numpy as jnp
from jax import lax
from jax.experimental import pallas as pl
from jax.experimental.pallas import tpu as pltpu
from jax.sharding import PartitionSpec as P

HEADS = 16
HEAD_DIM = 64
ROWMIN = 20
STEP = 4
PAIR = 2 * HEAD_DIM
PAIRS = HEADS // 2
SCALE = HEAD_DIM**-0.5
LOG2_E = math.log2(math.e)
BLOCK = 32
OUTSIDE = -1e30
CHUNKS = (0, 4, 8)
NEXT_CHUNKS = (0, 2, 4, 8)


def reach_sizes(points, count):
    area_rows = points * count // STEP
    root_bound = min(((area_rows + 2 * 4**power) // (3 * 2**power) for power in range(3, 9)))
    grow_rows = root_bound - ROWMIN // STEP - 6
    row_longest = ROWMIN + STEP * (grow_rows - 1)
    rim_width = 2 * row_longest
    return (rim_width, (rim_width + points - 1) // points)


def spans(bounds):
    return list(zip(bounds[:-1], bounds[1:]))


def passed_along(value, steps):
    count = lax.axis_size("band")
    initial, last = (max(0, -steps), min(count, count - steps))
    return lax.ppermute(value, "band", [(source, source + steps) for source in range(initial, last)])


def swapped(value, first):
    count = lax.axis_size("band")
    pairs = [(at, at + 1) for at in range(first, count - 1, 2)]
    return lax.ppermute(value, "band", pairs + [(high, low) for low, high in pairs])


def dot_nt(left, right):
    return lax.dot_general(
        left, right, (((1,), (1,)), ((), ())), preferred_element_type=jnp.float32
    )


def dot_nn(left, right):
    return jnp.dot(left, right, preferred_element_type=jnp.float32)


def head_masks():
    lanes = lax.broadcasted_iota(jnp.int32, (1, PAIR), 1)
    first = (lanes < HEAD_DIM).astype(jnp.float32)
    return (first.astype(jnp.bfloat16), (1.0 - first).astype(jnp.bfloat16))


def is_even():
    return lax.axis_index("band") % 2 == 0


def pack(sources, rows, low, high):
    points = sources[0].shape[0]
    columns = slice(low * PAIR, high * PAIR)
    first = jnp.stack([field[:rows, columns] for field in sources])
    last = jnp.stack([field[points - rows :, columns] for field in sources])
    return jnp.where(is_even(), first, last)


def padded(rows):
    return (rows + 15) // 16 * 16


def head_blocks(turned, half):
    return [turned[:HEAD_DIM, :half], turned[HEAD_DIM:, half:]]


def query_gradient(turned_keys, dscores, half):
    dq = head_blocks(dot_nn(turned_keys, dscores), half)
    return jnp.concatenate([(x * SCALE).astype(jnp.bfloat16) for x in dq], axis=0).T


def attention_kernel(rim_width, lengths, points, low_pair, next_pairs, deferred, carried, *refs):
    far = len(lengths) // 2 - 1
    near = lengths[far]
    half = points // 2
    rim = padded(rim_width)
    reached = half + 2 * rim
    wide = points + 2 * rim
    pairs = sum(next_pairs)
    win_ref, q_ref, g_ref, k_ref, v_ref, partner_k_ref, partner_v_ref = refs[:7]
    next_refs = refs[7 : 7 + len(next_pairs)]
    refs = refs[7 + len(next_pairs) :]
    far_refs = refs[: 2 * far]
    outs = refs[2 * far + carried :]
    att_out, dq_out, to_partner_ref, to_next_ref, dk_ref, dv_ref = outs[:6]
    to_far_refs = outs[6 : 6 + 2 * far]
    (bias_ref, keys_ref, turned_ref, exps_ref, probs_ref, dscores_ref, att_ref, dq_ref, sems) = outs[-9:]
    kept_scores, kept_keys = outs[6 + 2 * far : 8 + 2 * far] if deferred else (None, None)
    even = is_even()
    owns = [slice(part * half, (part + 1) * half) for part in range(2)]
    spans_of = [slice(part * half, part * half + reached) for part in range(2)]
    blocks = [slice(row, row + BLOCK) for row in range(0, reached, BLOCK)]
    masks = head_masks()

    for part, own in enumerate(owns):
        lower = jnp.concatenate([win_ref[0:1, own]] * 2, axis=1)
        upper = jnp.concatenate([win_ref[1:2, own]] * 2, axis=1)
        for block in blocks:
            keys = lax.broadcasted_iota(jnp.int32, (BLOCK, points), 0) + (part * half - rim + block.start)
            if rim > rim_width:
                below = jnp.where(keys < rim_width - rim, keys + (rim - rim_width), -wide)
                keys = jnp.where(keys < 0, below, jnp.where(keys < points + rim_width, keys, 2 * wide))
            inside = (keys >= lower) & (keys < upper)
            bias_ref[part, block, :] = jnp.where(inside, 0.0, OUTSIDE)

    if rim > rim_width:
        for gap in (slice(rim - 16, rim), slice(wide - 16, wide)):
            keys_ref[:, :, gap, :] = jnp.zeros((2, 2, 16, PAIR), jnp.bfloat16)

    where_next = [
        (chunk, at) for chunk, count in enumerate(next_pairs) for at in range(count)
    ]

    def columns_of(pair):
        return slice((low_pair + pair) * PAIR, (low_pair + pair + 1) * PAIR)

    def local_columns(pair):
        return slice(pair * PAIR, (pair + 1) * PAIR)

    def gather_keys(pair):
        columns = columns_of(pair)
        chunk, at = where_next[pair]
        next_columns = local_columns(at)
        into = keys_ref.at[pair % 2]
        for slot, (own_ref, partner_ref) in enumerate([(k_ref, partner_k_ref), (v_ref, partner_v_ref)]):
            start = 0
            for at in range(far):
                into[slot, start : start + lengths[at], :] = far_refs[at][slot, :, columns]
                start += lengths[at]
            into[slot, start : start + near, :] = jnp.where(
                even, next_refs[chunk][slot, :, next_columns], partner_ref[points - near :, columns]
            )
            into[slot, rim : rim + points, :] = own_ref[:, columns]
            start = rim + points
            into[slot, start : start + near, :] = jnp.where(
                even, partner_ref[:near, columns], next_refs[chunk][slot, :, next_columns]
            )
            start += near
            for at in range(far, 2 * far):
                into[slot, start : start + lengths[at + 2], :] = far_refs[at][slot, :, columns]
                start += lengths[at + 2]
            if deferred and slot == 0:
                kept_keys[pair] = into[slot].T
            else:
                turned_ref[pair % 2, slot] = into[slot].T

    def fold(op, total, block):
        for row in range(0, BLOCK, 8):
            total = op(total, block[row : row + 8])
        return total

    def both(turned):
        return head_blocks(turned, half)

    def dscores_of(pair, part):
        return kept_scores.at[pair, part] if deferred else dscores_ref.at[pair % 2, part]

    def probs_of(pair, part):
        return probs_ref.at[pair % 2, part]

    def q_both(pair, part):
        q = q_ref[owns[part], columns_of(pair)]
        return jnp.concatenate([q * (mask * SCALE) for mask in masks], axis=0)

    def g_both(pair, part):
        g = g_ref[owns[part], columns_of(pair)]
        return jnp.concatenate([g * mask for mask in masks], axis=0)

    def forward_scores(pair, part):
        exps = exps_ref.at[pair % 2, part]
        scores = dot_nt(keys_ref[pair % 2, 0, spans_of[part], :], q_both(pair, part))
        top = jnp.full((8, points), OUTSIDE, jnp.float32)
        for block in blocks:
            biased = scores[block] + bias_ref[part, block, :]
            exps[block, :] = biased
            top = fold(jnp.maximum, top, biased)
        return jnp.max(top, axis=0, keepdims=True)

    def forward_probs(pair, part, top):
        exps = exps_ref.at[pair % 2, part]
        total = jnp.zeros((8, points), jnp.float32)
        for block in blocks:
            values = jnp.exp2((exps[block, :] - top) * LOG2_E)
            exps[block, :] = values
            total = fold(jnp.add, total, values)
        inverse = 1.0 / jnp.sum(total, axis=0, keepdims=True)
        for block in blocks:
            probs_ref[pair % 2, part, block, :] = (exps[block, :] * inverse).astype(jnp.bfloat16)
        return inverse

    def forward_outputs(pair, part):
        own = owns[part]
        att = [
            x.astype(jnp.bfloat16)
            for x in both(
                dot_nn(turned_ref[pair % 2, 1, :, spans_of[part]], probs_ref[pair % 2, part])
            )
        ]
        att_ref[pair, own, :] = jnp.concatenate(att, axis=0).T
        g_turned = g_ref[own, columns_of(pair)].T
        return jnp.concatenate(
            [
                jnp.sum(
                    g_turned[head * HEAD_DIM : (head + 1) * HEAD_DIM].astype(jnp.float32)
                    * att[head].astype(jnp.float32),
                    axis=0,
                    keepdims=True,
                )
                for head in range(2)
            ],
            axis=1,
        )

    def backward_scores(pair, part, inverse, delta):
        dprobs = dot_nt(keys_ref[pair % 2, 1, spans_of[part], :], g_both(pair, part))
        for block in blocks:
            probs = exps_ref[pair % 2, part, block, :] * inverse
            dscores_of(pair, part)[block, :] = (probs * (dprobs[block] - delta)).astype(jnp.bfloat16)

    copies = []

    def backward_outputs(pair):
        for part in range(0 if deferred else 2):
            dq_ref[pair, owns[part], :] = query_gradient(
                turned_ref[pair % 2, 0, :, spans_of[part]], dscores_of(pair, part)[...], half
            )
        for slot, (scores_of, own_both, own_ref) in enumerate(
            [(dscores_of, q_both, dk_ref), (probs_of, g_both, dv_ref)]
        ):
            low_scores, high_scores = (scores_of(pair, part) for part in range(2))
            low, high = (own_both(pair, part) for part in range(2))
            shared = jnp.concatenate([low_scores[half:, :], high_scores[: reached - half, :]], axis=1)
            sums = [
                dot_nn(low_scores[:half, :], low),
                dot_nn(shared, jnp.concatenate([low, high], axis=0)),
                dot_nn(high_scores[reached - half :, :], high),
            ]
            send_out(pair, slot, own_ref, sums)

    def send_out(pair, slot, own_ref, sums):
        columns = local_columns(pair)
        bounds = spans((0, half, reached, wide))

        def rows(start, stop):
            pieces = [
                term[max(start, first) - first : min(stop, last) - first]
                for term, (first, last) in zip(sums, bounds)
                if start < last and stop > first
            ]
            return jnp.concatenate(pieces, axis=0)

        own_ref[:, columns] = rows(rim, rim + points)
        near_low = rows(rim_width - near, rim_width).astype(jnp.bfloat16)
        near_high = rows(rim + points, rim + points + near).astype(jnp.bfloat16)
        to_partner_ref[slot, :, columns] = jnp.where(even, near_high, near_low)
        to_next_ref[slot, :, columns] = jnp.where(even, near_low, near_high)
        start = 0
        for at in range(far):
            to_far_refs[at][slot, :, columns] = rows(start, start + lengths[at]).astype(jnp.bfloat16)
            start += lengths[at]
        start = rim + points + near
        for at in range(far, 2 * far):
            size = lengths[at + 2]
            to_far_refs[at][slot, :, columns] = rows(start, start + size).astype(jnp.bfloat16)
            start += size

    def finish(pair):
        backward_outputs(pair)
        sent = [(att_ref, att_out)] + ([] if deferred else [(dq_ref, dq_out)])
        for at, (ref, out) in enumerate(sent):
            copy = pltpu.make_async_copy(ref.at[pair], out.at[:, columns_of(pair)], sems.at[at, pair])
            copy.start()
            copies.append(copy)

    units = [(pair, part) for pair in range(pairs) for part in range(2)]
    gather_keys(0)
    tops = {units[0]: forward_scores(*units[0])}
    for at, unit in enumerate(units):
        if at + 1 < len(units):
            following = units[at + 1]
            if following[1] == 0:
                gather_keys(following[0])
            tops[following] = forward_scores(*following)
        if unit[1] == 0 and unit[0] > 0:
            finish(unit[0] - 1)
        inverse = forward_probs(*unit, tops.pop(unit))
        delta = forward_outputs(*unit)
        backward_scores(*unit, inverse, delta)
    finish(units[-1][0])
    for copy in copies:
        copy.wait()


def query_kernel(points, low_pair, reached, carried, *refs):
    scores_ref, keys_ref = refs[:2]
    dq_out, dq_ref, sems = refs[2 + carried :]
    half = points // 2
    copies = []
    for pair in range(scores_ref.shape[0]):
        for part in range(2):
            span = slice(part * half, part * half + reached)
            dq_ref[pair, part * half : (part + 1) * half, :] = query_gradient(
                keys_ref[pair, :, span], scores_ref[pair, part], half
            )
        columns = slice((low_pair + pair) * PAIR, (low_pair + pair + 1) * PAIR)
        copies.append(pltpu.make_async_copy(dq_ref.at[pair], dq_out.at[:, columns], sems.at[pair]))
        copies[-1].start()
    for copy in copies:
        copy.wait()


def sum_kernel(far_lengths, points, low, high, carried, *refs):
    far = len(far_lengths) // 2
    own_refs, partner_ref, next_ref = refs[:2], refs[2], refs[3]
    far_refs = refs[4 : 4 + 2 * far]
    outs = refs[4 + 2 * far + carried :]
    total, low_ref, sems = outs[-3:]
    near = partner_ref.shape[1]
    first = pl.multiple_of(jnp.where(is_even(), points - near, 0), 8)
    starts = (first, points - near - first)
    copies = []
    for slot in range(2):
        total[...] = own_refs[slot][...]
        for at, ref in enumerate((partner_ref, next_ref)):
            rows = pl.ds(pl.multiple_of(starts[at], 8), near)
            total[rows, :] += ref[slot].astype(jnp.float32)
        for at, (ref, length) in enumerate(zip(far_refs, far_lengths)):
            rows = slice(points - length, points) if at < far else slice(0, length)
            total[rows, :] += ref[slot].astype(jnp.float32)
        low_ref[slot] = total[...].astype(jnp.bfloat16)
        copy = pltpu.make_async_copy(
            low_ref.at[slot], outs[slot].at[:, low * PAIR : high * PAIR], sems.at[slot]
        )
        copy.start()
        copies.append(copy)
    for copy in copies:
        copy.wait()


def chunk_call(kernel, args, carried, count, out_shape, vmem_bytes, **options):
    vmem = pl.BlockSpec(memory_space=pltpu.VMEM)
    anywhere = pl.BlockSpec(memory_space=pl.ANY)
    return pl.pallas_call(
        functools.partial(kernel, len(carried)),
        in_specs=[vmem] * len(args) + [anywhere] * len(carried),
        out_specs=[anywhere] * count + [vmem] * (len(out_shape) - count),
        out_shape=out_shape,
        input_output_aliases={len(args) + at: at for at in range(len(carried))},
        compiler_params=pltpu.CompilerParams(vmem_limit_bytes=vmem_bytes),
        **options,
    )(*args, *carried)


def per_device(queries, keys, values, grad_out, windows):
    points, width = queries.shape
    rim_width, reach = reach_sizes(points, lax.axis_size("band"))
    band = lax.axis_index("band")
    near = min(points, rim_width)
    far = [d for d in range(-reach, reach + 1) if abs(d) > 1]
    far_sizes = [min(points, rim_width - (abs(d) - 1) * points) for d in far]
    lows = len(far) // 2
    lengths = far_sizes[:lows] + [near, near] + far_sizes[lows:]
    wide = points + 2 * padded(rim_width)
    reached = points // 2 + 2 * padded(rim_width)
    relative = (windows - band * points).T

    to_next, from_next, from_partner = [], [], []
    ready = (keys, values)
    for chunk, (low, high) in enumerate(spans(NEXT_CHUNKS)):
        piece = pack(ready, near, low, high)
        to_next.append(piece)
        ready = lax.optimization_barrier((*ready, piece))[:2]
        if chunk > 1:
            piece = lax.optimization_barrier((piece, from_next[chunk - 2]))[0]
        from_next.append(swapped(piece, 1))
        if chunk == 0:
            from_partner = [swapped(field, 0) for field in ready]
        elif chunk == 1:
            ready = lax.optimization_barrier((*ready, *from_partner))[:2]
    from_far = []
    for d, size in zip(far, far_sizes):
        part = slice(points - size, points) if d < 0 else slice(0, size)
        from_far.append(passed_along(jnp.stack([keys[part], values[part]]), -d))

    whole = jax.ShapeDtypeStruct((points, width), jnp.bfloat16)
    outs, own_terms, back_partner, back_next, back_far = [], [], [], [], []
    for chunk, (low, high) in enumerate(spans(CHUNKS)):
        count = high - low
        chunk_width = count * PAIR
        kept_shapes = [
            jax.ShapeDtypeStruct((count, 2, reached, points), jnp.bfloat16),
            jax.ShapeDtypeStruct((count, PAIR, wide), jnp.bfloat16),
        ]
        parts = [
            (at, last - first)
            for at, (first, last) in enumerate(spans(NEXT_CHUNKS))
            if low <= first and last <= high
        ]
        next_pairs = [size for _, size in parts]
        assert sum(next_pairs) == count
        outs = chunk_call(
            functools.partial(
                attention_kernel, rim_width, lengths, points, low, next_pairs, chunk == 0
            ),
            [relative, queries, grad_out, keys, values, *from_partner]
            + [from_next[at] for at, _ in parts]
            + from_far,
            outs[:2],
            2,
            [whole] * 2
            + [jax.ShapeDtypeStruct((2, near, chunk_width), jnp.bfloat16)] * 2
            + [jax.ShapeDtypeStruct((points, chunk_width), jnp.float32)] * 2
            + [jax.ShapeDtypeStruct((2, size, chunk_width), jnp.bfloat16) for size in far_sizes]
            + (kept_shapes if chunk == 0 else []),
            48 * wide * points + 12 * 2**20,
            scratch_shapes=[
                pltpu.VMEM((2, reached, points), jnp.float32),
                pltpu.VMEM((2, 2, wide, PAIR), jnp.bfloat16),
                pltpu.VMEM((2, 2, PAIR, wide), jnp.bfloat16),
                pltpu.VMEM((2, 2, reached, points), jnp.float32),
                pltpu.VMEM((2, 2, reached, points), jnp.bfloat16),
                pltpu.VMEM((2, 2, reached, points), jnp.bfloat16),
                pltpu.VMEM((count, points, PAIR), jnp.bfloat16),
                pltpu.VMEM((count, points, PAIR), jnp.bfloat16),
                pltpu.SemaphoreType.DMA((2, count)),
            ],
            cost_estimate=pl.CostEstimate(
                flops=count * 120 * reached * points * PAIR,
                bytes_accessed=count * PAIR * (20 * points + 8 * wide),
                transcendentals=2 * count * points * reached,
            ),
            name=f"attention_{chunk}",
        )
        own_terms.append(outs[4:6])
        if chunk == 0:
            kept = outs[6 + len(far) :]
        back_partner.append(swapped(outs[2], 0))
        back_next.append(swapped(outs[3], 1))
        back_far.append([passed_along(term, d) for term, d in zip(outs[6 : 6 + len(far)], far)])

    first_pairs = CHUNKS[1]
    grad_q = chunk_call(
        functools.partial(query_kernel, points, 0, reached),
        kept,
        [outs[1]],
        1,
        [whole],
        16 * wide * points + 8 * 2**20,
        scratch_shapes=[
            pltpu.VMEM((first_pairs, points, PAIR), jnp.bfloat16),
            pltpu.SemaphoreType.DMA((first_pairs,)),
        ],
        cost_estimate=pl.CostEstimate(
            flops=first_pairs * 4 * reached * points * PAIR,
            bytes_accessed=first_pairs * 4 * reached * points,
            transcendentals=0,
        ),
        name="query_gradients",
    )[0]

    grads = []
    for chunk, (low, high) in enumerate(spans(CHUNKS)):
        chunk_width = (high - low) * PAIR
        grads = chunk_call(
            functools.partial(sum_kernel, far_sizes, points, low, high),
            [*own_terms[chunk], back_partner[chunk], back_next[chunk], *back_far[chunk]],
            grads,
            2,
            [whole] * 2,
            12 * 2**20,
            scratch_shapes=[
                pltpu.VMEM((points, chunk_width), jnp.float32),
                pltpu.VMEM((2, points, chunk_width), jnp.bfloat16),
                pltpu.SemaphoreType.DMA((2,)),
            ],
            cost_estimate=pl.CostEstimate(
                flops=6 * points * chunk_width,
                bytes_accessed=20 * points * chunk_width,
                transcendentals=0,
            ),
            name=f"gradient_sums_{chunk}",
        )
    return (outs[0], grad_q, grads[0], grads[1])


def solution(mesh):
    spread = P(("members", "band"), None)
    return jax.shard_map(
        per_device,
        mesh=mesh,
        in_specs=(spread, spread, spread, spread, P("band", None)),
        out_specs=(spread, spread, spread, spread),
        check_vma=False,
    )
```

```python
import functools
import math

import jax
import jax.numpy as jnp
from jax import lax
from jax.experimental import pallas as pl
from jax.experimental.pallas import tpu as pltpu
from jax.sharding import PartitionSpec as P

HEADS = 16
HEAD_DIM = 64
ROWMIN = 20
STEP = 4
PAIR = 2 * HEAD_DIM
PAIRS = HEADS // 2
SCALE = HEAD_DIM**-0.5
LOG2_E = math.log2(math.e)
BLOCK = 32
OUTSIDE = -1e30
CHUNKS = (0, 4, 8)
NEXT_CHUNKS = (0, 2, 4, 8)


def reach_sizes(points, count):
    area_rows = points * count // STEP
    root_bound = min(((area_rows + 2 * 4**power) // (3 * 2**power) for power in range(3, 9)))
    grow_rows = root_bound - ROWMIN // STEP - 6
    row_longest = ROWMIN + STEP * (grow_rows - 1)
    rim_width = 2 * row_longest
    return (rim_width, (rim_width + points - 1) // points)


def spans(bounds):
    return list(zip(bounds[:-1], bounds[1:]))


def passed_along(value, steps):
    count = lax.axis_size("band")
    initial, last = (max(0, -steps), min(count, count - steps))
    return lax.ppermute(value, "band", [(source, source + steps) for source in range(initial, last)])


def swapped(value, first):
    count = lax.axis_size("band")
    pairs = [(at, at + 1) for at in range(first, count - 1, 2)]
    return lax.ppermute(value, "band", pairs + [(high, low) for low, high in pairs])


def dot_nt(left, right):
    return lax.dot_general(
        left, right, (((1,), (1,)), ((), ())), preferred_element_type=jnp.float32
    )


def dot_nn(left, right):
    return jnp.dot(left, right, preferred_element_type=jnp.float32)


def head_masks():
    lanes = lax.broadcasted_iota(jnp.int32, (1, PAIR), 1)
    first = (lanes < HEAD_DIM).astype(jnp.float32)
    return (first.astype(jnp.bfloat16), (1.0 - first).astype(jnp.bfloat16))


def is_even():
    return lax.axis_index("band") % 2 == 0


def pack(sources, rows, low, high):
    points = sources[0].shape[0]
    columns = slice(low * PAIR, high * PAIR)
    first = jnp.stack([field[:rows, columns] for field in sources])
    last = jnp.stack([field[points - rows :, columns] for field in sources])
    return jnp.where(is_even(), first, last)


def padded(rows):
    return (rows + 15) // 16 * 16


def head_blocks(turned, half):
    return [turned[:HEAD_DIM, :half], turned[HEAD_DIM:, half:]]


def query_gradient(turned_keys, dscores, half):
    dq = head_blocks(dot_nn(turned_keys, dscores), half)
    return jnp.concatenate([(x * SCALE).astype(jnp.bfloat16) for x in dq], axis=0).T


def attention_kernel(rim_width, lengths, points, low_pair, next_pairs, deferred, carried, *refs):
    far = len(lengths) // 2 - 1
    near = lengths[far]
    half = points // 2
    rim = padded(rim_width)
    reached = half + 2 * rim
    wide = points + 2 * rim
    pairs = sum(next_pairs)
    win_ref, q_ref, g_ref, k_ref, v_ref, partner_k_ref, partner_v_ref = refs[:7]
    next_refs = refs[7 : 7 + len(next_pairs)]
    refs = refs[7 + len(next_pairs) :]
    far_refs = refs[: 2 * far]
    outs = refs[2 * far + carried :]
    att_out, dq_out, to_partner_ref, to_next_ref, dk_ref, dv_ref = outs[:6]
    to_far_refs = outs[6 : 6 + 2 * far]
    (bias_ref, keys_ref, turned_ref, exps_ref, probs_ref, dscores_ref, att_ref, dq_ref, sems) = outs[-9:]
    kept_scores, kept_keys = outs[6 + 2 * far : 8 + 2 * far] if deferred else (None, None)
    even = is_even()
    owns = [slice(part * half, (part + 1) * half) for part in range(2)]
    spans_of = [slice(part * half, part * half + reached) for part in range(2)]
    blocks = [slice(row, row + BLOCK) for row in range(0, reached, BLOCK)]
    masks = head_masks()

    for part, own in enumerate(owns):
        lower = jnp.concatenate([win_ref[0:1, own]] * 2, axis=1)
        upper = jnp.concatenate([win_ref[1:2, own]] * 2, axis=1)
        for block in blocks:
            keys = lax.broadcasted_iota(jnp.int32, (BLOCK, points), 0) + (part * half - rim + block.start)
            if rim > rim_width:
                below = jnp.where(keys < rim_width - rim, keys + (rim - rim_width), -wide)
                keys = jnp.where(keys < 0, below, jnp.where(keys < points + rim_width, keys, 2 * wide))
            inside = (keys >= lower) & (keys < upper)
            bias_ref[part, block, :] = jnp.where(inside, 0.0, OUTSIDE)

    if rim > rim_width:
        for gap in (slice(rim - 16, rim), slice(wide - 16, wide)):
            keys_ref[:, :, gap, :] = jnp.zeros((2, 2, 16, PAIR), jnp.bfloat16)

    where_next = [
        (chunk, at) for chunk, count in enumerate(next_pairs) for at in range(count)
    ]

    def columns_of(pair):
        return slice((low_pair + pair) * PAIR, (low_pair + pair + 1) * PAIR)

    def local_columns(pair):
        return slice(pair * PAIR, (pair + 1) * PAIR)

    def gather_keys(pair):
        columns = columns_of(pair)
        chunk, at = where_next[pair]
        next_columns = local_columns(at)
        into = keys_ref.at[pair % 2]
        for slot, (own_ref, partner_ref) in enumerate([(k_ref, partner_k_ref), (v_ref, partner_v_ref)]):
            start = 0
            for at in range(far):
                into[slot, start : start + lengths[at], :] = far_refs[at][slot, :, columns]
                start += lengths[at]
            into[slot, start : start + near, :] = jnp.where(
                even, next_refs[chunk][slot, :, next_columns], partner_ref[points - near :, columns]
            )
            into[slot, rim : rim + points, :] = own_ref[:, columns]
            start = rim + points
            into[slot, start : start + near, :] = jnp.where(
                even, partner_ref[:near, columns], next_refs[chunk][slot, :, next_columns]
            )
            start += near
            for at in range(far, 2 * far):
                into[slot, start : start + lengths[at + 2], :] = far_refs[at][slot, :, columns]
                start += lengths[at + 2]
            if deferred and slot == 0:
                kept_keys[pair] = into[slot].T
            else:
                turned_ref[pair % 2, slot] = into[slot].T

    def fold(op, total, block):
        for row in range(0, BLOCK, 8):
            total = op(total, block[row : row + 8])
        return total

    def both(turned):
        return head_blocks(turned, half)

    def dscores_of(pair, part):
        return kept_scores.at[pair, part] if deferred else dscores_ref.at[pair % 2, part]

    def probs_of(pair, part):
        return probs_ref.at[pair % 2, part]

    def q_both(pair, part):
        q = q_ref[owns[part], columns_of(pair)]
        return jnp.concatenate([q * (mask * SCALE) for mask in masks], axis=0)

    def g_both(pair, part):
        g = g_ref[owns[part], columns_of(pair)]
        return jnp.concatenate([g * mask for mask in masks], axis=0)

    def forward_scores(pair, part):
        exps = exps_ref.at[pair % 2, part]
        scores = dot_nt(keys_ref[pair % 2, 0, spans_of[part], :], q_both(pair, part))
        top = jnp.full((8, points), OUTSIDE, jnp.float32)
        for block in blocks:
            biased = scores[block] + bias_ref[part, block, :]
            exps[block, :] = biased
            top = fold(jnp.maximum, top, biased)
        return jnp.max(top, axis=0, keepdims=True)

    def forward_probs(pair, part, top):
        exps = exps_ref.at[pair % 2, part]
        total = jnp.zeros((8, points), jnp.float32)
        for block in blocks:
            values = jnp.exp2((exps[block, :] - top) * LOG2_E)
            exps[block, :] = values
            total = fold(jnp.add, total, values)
        inverse = 1.0 / jnp.sum(total, axis=0, keepdims=True)
        for block in blocks:
            probs_ref[pair % 2, part, block, :] = (exps[block, :] * inverse).astype(jnp.bfloat16)
        return inverse

    def forward_outputs(pair, part):
        own = owns[part]
        att = [
            x.astype(jnp.bfloat16)
            for x in both(
                dot_nn(turned_ref[pair % 2, 1, :, spans_of[part]], probs_ref[pair % 2, part])
            )
        ]
        att_ref[pair, own, :] = jnp.concatenate(att, axis=0).T
        g_turned = g_ref[own, columns_of(pair)].T
        return jnp.concatenate(
            [
                jnp.sum(
                    g_turned[head * HEAD_DIM : (head + 1) * HEAD_DIM].astype(jnp.float32)
                    * att[head].astype(jnp.float32),
                    axis=0,
                    keepdims=True,
                )
                for head in range(2)
            ],
            axis=1,
        )

    def backward_scores(pair, part, inverse, delta):
        dprobs = dot_nt(keys_ref[pair % 2, 1, spans_of[part], :], g_both(pair, part))
        for block in blocks:
            probs = exps_ref[pair % 2, part, block, :] * inverse
            dscores_of(pair, part)[block, :] = (probs * (dprobs[block] - delta)).astype(jnp.bfloat16)

    copies = []

    def backward_outputs(pair):
        for part in range(0 if deferred else 2):
            dq_ref[pair, owns[part], :] = query_gradient(
                turned_ref[pair % 2, 0, :, spans_of[part]], dscores_of(pair, part)[...], half
            )
        for slot, (scores_of, own_both, own_ref) in enumerate(
            [(dscores_of, q_both, dk_ref), (probs_of, g_both, dv_ref)]
        ):
            low_scores, high_scores = (scores_of(pair, part) for part in range(2))
            low, high = (own_both(pair, part) for part in range(2))
            shared = jnp.concatenate([low_scores[half:, :], high_scores[: reached - half, :]], axis=1)
            sums = [
                dot_nn(low_scores[:half, :], low),
                dot_nn(shared, jnp.concatenate([low, high], axis=0)),
                dot_nn(high_scores[reached - half :, :], high),
            ]
            send_out(pair, slot, own_ref, sums)

    def send_out(pair, slot, own_ref, sums):
        columns = local_columns(pair)
        bounds = spans((0, half, reached, wide))

        def rows(start, stop):
            pieces = [
                term[max(start, first) - first : min(stop, last) - first]
                for term, (first, last) in zip(sums, bounds)
                if start < last and stop > first
            ]
            return jnp.concatenate(pieces, axis=0)

        own_ref[:, columns] = rows(rim, rim + points)
        near_low = rows(rim_width - near, rim_width).astype(jnp.bfloat16)
        near_high = rows(rim + points, rim + points + near).astype(jnp.bfloat16)
        to_partner_ref[slot, :, columns] = jnp.where(even, near_high, near_low)
        to_next_ref[slot, :, columns] = jnp.where(even, near_low, near_high)
        start = 0
        for at in range(far):
            to_far_refs[at][slot, :, columns] = rows(start, start + lengths[at]).astype(jnp.bfloat16)
            start += lengths[at]
        start = rim + points + near
        for at in range(far, 2 * far):
            size = lengths[at + 2]
            to_far_refs[at][slot, :, columns] = rows(start, start + size).astype(jnp.bfloat16)
            start += size

    def finish(pair):
        backward_outputs(pair)
        sent = [(att_ref, att_out)] + ([] if deferred else [(dq_ref, dq_out)])
        for at, (ref, out) in enumerate(sent):
            copy = pltpu.make_async_copy(ref.at[pair], out.at[:, columns_of(pair)], sems.at[at, pair])
            copy.start()
            copies.append(copy)

    units = [(pair, part) for pair in range(pairs) for part in range(2)]
    gather_keys(0)
    tops = {units[0]: forward_scores(*units[0])}
    for at, unit in enumerate(units):
        if at + 1 < len(units):
            following = units[at + 1]
            if following[1] == 0:
                gather_keys(following[0])
            tops[following] = forward_scores(*following)
        if unit[1] == 0 and unit[0] > 0:
            finish(unit[0] - 1)
        inverse = forward_probs(*unit, tops.pop(unit))
        delta = forward_outputs(*unit)
        backward_scores(*unit, inverse, delta)
    finish(units[-1][0])
    for copy in copies:
        copy.wait()


def query_kernel(points, low_pair, reached, carried, *refs):
    scores_ref, keys_ref = refs[:2]
    dq_out, dq_ref, sems = refs[2 + carried :]
    half = points // 2
    copies = []
    for pair in range(scores_ref.shape[0]):
        for part in range(2):
            span = slice(part * half, part * half + reached)
            dq_ref[pair, part * half : (part + 1) * half, :] = query_gradient(
                keys_ref[pair, :, span], scores_ref[pair, part], half
            )
        columns = slice((low_pair + pair) * PAIR, (low_pair + pair + 1) * PAIR)
        copies.append(pltpu.make_async_copy(dq_ref.at[pair], dq_out.at[:, columns], sems.at[pair]))
        copies[-1].start()
    for copy in copies:
        copy.wait()


def sum_kernel(far_lengths, points, low, high, carried, *refs):
    far = len(far_lengths) // 2
    own_refs, partner_ref, next_ref = refs[:2], refs[2], refs[3]
    far_refs = refs[4 : 4 + 2 * far]
    outs = refs[4 + 2 * far + carried :]
    total, low_ref, sems = outs[-3:]
    near = partner_ref.shape[1]
    first = pl.multiple_of(jnp.where(is_even(), points - near, 0), 8)
    starts = (first, points - near - first)
    copies = []
    for slot in range(2):
        total[...] = own_refs[slot][...]
        for at, ref in enumerate((partner_ref, next_ref)):
            rows = pl.ds(pl.multiple_of(starts[at], 8), near)
            total[rows, :] += ref[slot].astype(jnp.float32)
        for at, (ref, length) in enumerate(zip(far_refs, far_lengths)):
            rows = slice(points - length, points) if at < far else slice(0, length)
            total[rows, :] += ref[slot].astype(jnp.float32)
        low_ref[slot] = total[...].astype(jnp.bfloat16)
        copy = pltpu.make_async_copy(
            low_ref.at[slot], outs[slot].at[:, low * PAIR : high * PAIR], sems.at[slot]
        )
        copy.start()
        copies.append(copy)
    for copy in copies:
        copy.wait()


def chunk_call(kernel, args, carried, count, out_shape, vmem_bytes, **options):
    vmem = pl.BlockSpec(memory_space=pltpu.VMEM)
    anywhere = pl.BlockSpec(memory_space=pl.ANY)
    return pl.pallas_call(
        functools.partial(kernel, len(carried)),
        in_specs=[vmem] * len(args) + [anywhere] * len(carried),
        out_specs=[anywhere] * count + [vmem] * (len(out_shape) - count),
        out_shape=out_shape,
        input_output_aliases={len(args) + at: at for at in range(len(carried))},
        compiler_params=pltpu.CompilerParams(vmem_limit_bytes=vmem_bytes),
        **options,
    )(*args, *carried)


def per_device(queries, keys, values, grad_out, windows):
    points, width = queries.shape
    rim_width, reach = reach_sizes(points, lax.axis_size("band"))
    band = lax.axis_index("band")
    near = min(points, rim_width)
    far = [d for d in range(-reach, reach + 1) if abs(d) > 1]
    far_sizes = [min(points, rim_width - (abs(d) - 1) * points) for d in far]
    lows = len(far) // 2
    lengths = far_sizes[:lows] + [near, near] + far_sizes[lows:]
    wide = points + 2 * padded(rim_width)
    reached = points // 2 + 2 * padded(rim_width)
    relative = (windows - band * points).T

    to_next, from_next, from_partner = [], [], []
    ready = (keys, values)
    for chunk, (low, high) in enumerate(spans(NEXT_CHUNKS)):
        piece = pack(ready, near, low, high)
        to_next.append(piece)
        ready = lax.optimization_barrier((*ready, piece))[:2]
        if chunk > 1:
            piece = lax.optimization_barrier((piece, from_next[chunk - 2]))[0]
        from_next.append(swapped(piece, 1))
        if chunk == 0:
            from_partner = [swapped(field, 0) for field in ready]
        elif chunk == 1:
            ready = lax.optimization_barrier((*ready, *from_partner))[:2]
    from_far = []
    for d, size in zip(far, far_sizes):
        part = slice(points - size, points) if d < 0 else slice(0, size)
        from_far.append(passed_along(jnp.stack([keys[part], values[part]]), -d))

    whole = jax.ShapeDtypeStruct((points, width), jnp.bfloat16)
    outs, own_terms, back_partner, back_next, back_far = [], [], [], [], []
    for chunk, (low, high) in enumerate(spans(CHUNKS)):
        count = high - low
        chunk_width = count * PAIR
        kept_shapes = [
            jax.ShapeDtypeStruct((count, 2, reached, points), jnp.bfloat16),
            jax.ShapeDtypeStruct((count, PAIR, wide), jnp.bfloat16),
        ]
        parts = [
            (at, last - first)
            for at, (first, last) in enumerate(spans(NEXT_CHUNKS))
            if low <= first and last <= high
        ]
        next_pairs = [size for _, size in parts]
        assert sum(next_pairs) == count
        outs = chunk_call(
            functools.partial(
                attention_kernel, rim_width, lengths, points, low, next_pairs, chunk == 0
            ),
            [relative, queries, grad_out, keys, values, *from_partner]
            + [from_next[at] for at, _ in parts]
            + from_far,
            outs[:2],
            2,
            [whole] * 2
            + [jax.ShapeDtypeStruct((2, near, chunk_width), jnp.bfloat16)] * 2
            + [jax.ShapeDtypeStruct((points, chunk_width), jnp.float32)] * 2
            + [jax.ShapeDtypeStruct((2, size, chunk_width), jnp.bfloat16) for size in far_sizes]
            + (kept_shapes if chunk == 0 else []),
            48 * wide * points + 5 * 2**20,
            scratch_shapes=[
                pltpu.VMEM((2, reached, points), jnp.float32),
                pltpu.VMEM((2, 2, wide, PAIR), jnp.bfloat16),
                pltpu.VMEM((2, 2, PAIR, wide), jnp.bfloat16),
                pltpu.VMEM((2, 2, reached, points), jnp.float32),
                pltpu.VMEM((2, 2, reached, points), jnp.bfloat16),
                pltpu.VMEM((2, 2, reached, points), jnp.bfloat16),
                pltpu.VMEM((count, points, PAIR), jnp.bfloat16),
                pltpu.VMEM((count, points, PAIR), jnp.bfloat16),
                pltpu.SemaphoreType.DMA((2, count)),
            ],
            cost_estimate=pl.CostEstimate(
                flops=count * 120 * reached * points * PAIR,
                bytes_accessed=count * PAIR * (20 * points + 8 * wide),
                transcendentals=2 * count * points * reached,
            ),
            name=f"attention_{chunk}",
        )
        own_terms.append(outs[4:6])
        if chunk == 0:
            kept = outs[6 + len(far) :]
        back_partner.append(swapped(outs[2], 0))
        back_next.append(swapped(outs[3], 1))
        back_far.append([passed_along(term, d) for term, d in zip(outs[6 : 6 + len(far)], far)])

    first_pairs = CHUNKS[1]
    grad_q = chunk_call(
        functools.partial(query_kernel, points, 0, reached),
        kept,
        [outs[1]],
        1,
        [whole],
        16 * wide * points + 3 * 2**20,
        scratch_shapes=[
            pltpu.VMEM((first_pairs, points, PAIR), jnp.bfloat16),
            pltpu.SemaphoreType.DMA((first_pairs,)),
        ],
        cost_estimate=pl.CostEstimate(
            flops=first_pairs * 4 * reached * points * PAIR,
            bytes_accessed=first_pairs * 4 * reached * points,
            transcendentals=0,
        ),
        name="query_gradients",
    )[0]

    grads = []
    for chunk, (low, high) in enumerate(spans(CHUNKS)):
        chunk_width = (high - low) * PAIR
        grads = chunk_call(
            functools.partial(sum_kernel, far_sizes, points, low, high),
            [*own_terms[chunk], back_partner[chunk], back_next[chunk], *back_far[chunk]],
            grads,
            2,
            [whole] * 2,
            7 * 2**20,
            scratch_shapes=[
                pltpu.VMEM((points, chunk_width), jnp.float32),
                pltpu.VMEM((2, points, chunk_width), jnp.bfloat16),
                pltpu.SemaphoreType.DMA((2,)),
            ],
            cost_estimate=pl.CostEstimate(
                flops=6 * points * chunk_width,
                bytes_accessed=20 * points * chunk_width,
                transcendentals=0,
            ),
            name=f"gradient_sums_{chunk}",
        )
    return (outs[0], grad_q, grads[0], grads[1])


def solution(mesh):
    spread = P(("members", "band"), None)
    return jax.shard_map(
        per_device,
        mesh=mesh,
        in_specs=(spread, spread, spread, spread, P("band", None)),
        out_specs=(spread, spread, spread, spread),
        check_vma=False,
    )
```

```python
import functools
import math

import jax
import jax.numpy as jnp
from jax import lax
from jax.experimental import pallas as pl
from jax.experimental.pallas import tpu as pltpu
from jax.sharding import PartitionSpec as P

HEADS = 16
HEAD_DIM = 64
ROWMIN = 20
STEP = 4
PAIR = 2 * HEAD_DIM
PAIRS = HEADS // 2
SCALE = HEAD_DIM**-0.5
LOG2_E = math.log2(math.e)
BLOCK = 32
OUTSIDE = -1e30
CHUNKS = (0, 4, 8)
NEXT_CHUNKS = (0, 2, 4, 8)


def reach_sizes(points, count):
    area_rows = points * count // STEP
    root_bound = min(((area_rows + 2 * 4**power) // (3 * 2**power) for power in range(3, 9)))
    grow_rows = root_bound - ROWMIN // STEP - 6
    row_longest = ROWMIN + STEP * (grow_rows - 1)
    rim_width = 2 * row_longest
    return (rim_width, (rim_width + points - 1) // points)


def spans(bounds):
    return list(zip(bounds[:-1], bounds[1:]))


def passed_along(value, steps):
    count = lax.axis_size("band")
    initial, last = (max(0, -steps), min(count, count - steps))
    return lax.ppermute(value, "band", [(source, source + steps) for source in range(initial, last)])


def swapped(value, first):
    count = lax.axis_size("band")
    pairs = [(at, at + 1) for at in range(first, count - 1, 2)]
    return lax.ppermute(value, "band", pairs + [(high, low) for low, high in pairs])


def dot_nt(left, right):
    return lax.dot_general(
        left, right, (((1,), (1,)), ((), ())), preferred_element_type=jnp.float32
    )


def dot_nn(left, right):
    return jnp.dot(left, right, preferred_element_type=jnp.float32)


def head_masks():
    lanes = lax.broadcasted_iota(jnp.int32, (1, PAIR), 1)
    first = (lanes < HEAD_DIM).astype(jnp.float32)
    return (first.astype(jnp.bfloat16), (1.0 - first).astype(jnp.bfloat16))


def is_even():
    return lax.axis_index("band") % 2 == 0


def pack(sources, rows, low, high):
    points = sources[0].shape[0]
    columns = slice(low * PAIR, high * PAIR)
    first = jnp.stack([field[:rows, columns] for field in sources])
    last = jnp.stack([field[points - rows :, columns] for field in sources])
    return jnp.where(is_even(), first, last)


def padded(rows):
    return (rows + 15) // 16 * 16


def attention_kernel(rim_width, lengths, points, low_pair, next_pairs, carried, *refs):
    far = len(lengths) // 2 - 1
    near = lengths[far]
    half = points // 2
    rim = padded(rim_width)
    reached = half + 2 * rim
    wide = points + 2 * rim
    pairs = sum(next_pairs)
    win_ref, q_ref, g_ref, k_ref, v_ref, partner_k_ref, partner_v_ref = refs[:7]
    next_refs = refs[7 : 7 + len(next_pairs)]
    refs = refs[7 + len(next_pairs) :]
    far_refs = refs[: 2 * far]
    outs = refs[2 * far + carried :]
    att_out, dq_out, to_partner_ref, to_next_ref, dk_ref, dv_ref = outs[:6]
    to_far_refs = outs[6 : 6 + 2 * far]
    (bias_ref, keys_ref, turned_ref, exps_ref, probs_ref, dscores_ref, att_ref, dq_ref, sems) = outs[-9:]
    even = is_even()
    owns = [slice(part * half, (part + 1) * half) for part in range(2)]
    spans_of = [slice(part * half, part * half + reached) for part in range(2)]
    blocks = [slice(row, row + BLOCK) for row in range(0, reached, BLOCK)]
    masks = head_masks()

    for part, own in enumerate(owns):
        lower = jnp.concatenate([win_ref[0:1, own]] * 2, axis=1)
        upper = jnp.concatenate([win_ref[1:2, own]] * 2, axis=1)
        for block in blocks:
            keys = lax.broadcasted_iota(jnp.int32, (BLOCK, points), 0) + (part * half - rim + block.start)
            if rim > rim_width:
                below = jnp.where(keys < rim_width - rim, keys + (rim - rim_width), -wide)
                keys = jnp.where(keys < 0, below, jnp.where(keys < points + rim_width, keys, 2 * wide))
            inside = (keys >= lower) & (keys < upper)
            bias_ref[part, block, :] = jnp.where(inside, 0.0, OUTSIDE)

    if rim > rim_width:
        for gap in (slice(rim - 16, rim), slice(wide - 16, wide)):
            keys_ref[:, :, gap, :] = jnp.zeros((2, 2, 16, PAIR), jnp.bfloat16)

    where_next = [
        (chunk, at) for chunk, count in enumerate(next_pairs) for at in range(count)
    ]

    def columns_of(pair):
        return slice((low_pair + pair) * PAIR, (low_pair + pair + 1) * PAIR)

    def local_columns(pair):
        return slice(pair * PAIR, (pair + 1) * PAIR)

    def gather_keys(pair):
        columns = columns_of(pair)
        chunk, at = where_next[pair]
        next_columns = local_columns(at)
        into = keys_ref.at[pair % 2]
        for slot, (own_ref, partner_ref) in enumerate([(k_ref, partner_k_ref), (v_ref, partner_v_ref)]):
            start = 0
            for at in range(far):
                into[slot, start : start + lengths[at], :] = far_refs[at][slot, :, columns]
                start += lengths[at]
            into[slot, start : start + near, :] = jnp.where(
                even, next_refs[chunk][slot, :, next_columns], partner_ref[points - near :, columns]
            )
            into[slot, rim : rim + points, :] = own_ref[:, columns]
            start = rim + points
            into[slot, start : start + near, :] = jnp.where(
                even, partner_ref[:near, columns], next_refs[chunk][slot, :, next_columns]
            )
            start += near
            for at in range(far, 2 * far):
                into[slot, start : start + lengths[at + 2], :] = far_refs[at][slot, :, columns]
                start += lengths[at + 2]
            turned_ref[pair % 2, slot] = into[slot].T

    def fold(op, total, block):
        for row in range(0, BLOCK, 8):
            total = op(total, block[row : row + 8])
        return total

    def both(turned):
        return [turned[:HEAD_DIM, :half], turned[HEAD_DIM:, half:]]

    def q_both(pair, part):
        q = q_ref[owns[part], columns_of(pair)]
        return jnp.concatenate([q * (mask * SCALE) for mask in masks], axis=0)

    def g_both(pair, part):
        g = g_ref[owns[part], columns_of(pair)]
        return jnp.concatenate([g * mask for mask in masks], axis=0)

    def forward_scores(pair, part):
        exps = exps_ref.at[pair % 2, part]
        scores = dot_nt(keys_ref[pair % 2, 0, spans_of[part], :], q_both(pair, part))
        top = jnp.full((8, points), OUTSIDE, jnp.float32)
        for block in blocks:
            biased = scores[block] + bias_ref[part, block, :]
            exps[block, :] = biased
            top = fold(jnp.maximum, top, biased)
        return jnp.max(top, axis=0, keepdims=True)

    def forward_probs(pair, part, top):
        exps = exps_ref.at[pair % 2, part]
        total = jnp.zeros((8, points), jnp.float32)
        for block in blocks:
            values = jnp.exp2((exps[block, :] - top) * LOG2_E)
            exps[block, :] = values
            total = fold(jnp.add, total, values)
        inverse = 1.0 / jnp.sum(total, axis=0, keepdims=True)
        for block in blocks:
            probs_ref[pair % 2, part, block, :] = (exps[block, :] * inverse).astype(jnp.bfloat16)
        return inverse

    def forward_outputs(pair, part):
        own = owns[part]
        att = [
            x.astype(jnp.bfloat16)
            for x in both(
                dot_nn(turned_ref[pair % 2, 1, :, spans_of[part]], probs_ref[pair % 2, part])
            )
        ]
        att_ref[pair, own, :] = jnp.concatenate(att, axis=0).T
        g_turned = g_ref[own, columns_of(pair)].T
        return jnp.concatenate(
            [
                jnp.sum(
                    g_turned[head * HEAD_DIM : (head + 1) * HEAD_DIM].astype(jnp.float32)
                    * att[head].astype(jnp.float32),
                    axis=0,
                    keepdims=True,
                )
                for head in range(2)
            ],
            axis=1,
        )

    def backward_scores(pair, part, inverse, delta):
        dprobs = dot_nt(keys_ref[pair % 2, 1, spans_of[part], :], g_both(pair, part))
        for block in blocks:
            probs = exps_ref[pair % 2, part, block, :] * inverse
            dscores_ref[pair % 2, part, block, :] = (probs * (dprobs[block] - delta)).astype(jnp.bfloat16)

    copies = []

    def backward_outputs(pair):
        for part in range(2):
            dq = both(dot_nn(turned_ref[pair % 2, 0, :, spans_of[part]], dscores_ref[pair % 2, part]))
            dq_ref[pair, owns[part], :] = jnp.concatenate(
                [(x * SCALE).astype(jnp.bfloat16) for x in dq], axis=0
            ).T
        for slot, (scores_ref, own_both, own_ref) in enumerate(
            [(dscores_ref, q_both, dk_ref), (probs_ref, g_both, dv_ref)]
        ):
            low_scores, high_scores = (scores_ref.at[pair % 2, part] for part in range(2))
            low, high = (own_both(pair, part) for part in range(2))
            shared = jnp.concatenate([low_scores[half:, :], high_scores[: reached - half, :]], axis=1)
            sums = [
                dot_nn(low_scores[:half, :], low),
                dot_nn(shared, jnp.concatenate([low, high], axis=0)),
                dot_nn(high_scores[reached - half :, :], high),
            ]
            send_out(pair, slot, own_ref, sums)

    def send_out(pair, slot, own_ref, sums):
        columns = local_columns(pair)
        bounds = spans((0, half, reached, wide))

        def rows(start, stop):
            pieces = [
                term[max(start, first) - first : min(stop, last) - first]
                for term, (first, last) in zip(sums, bounds)
                if start < last and stop > first
            ]
            return jnp.concatenate(pieces, axis=0)

        own_ref[:, columns] = rows(rim, rim + points)
        near_low = rows(rim_width - near, rim_width).astype(jnp.bfloat16)
        near_high = rows(rim + points, rim + points + near).astype(jnp.bfloat16)
        to_partner_ref[slot, :, columns] = jnp.where(even, near_high, near_low)
        to_next_ref[slot, :, columns] = jnp.where(even, near_low, near_high)
        start = 0
        for at in range(far):
            to_far_refs[at][slot, :, columns] = rows(start, start + lengths[at]).astype(jnp.bfloat16)
            start += lengths[at]
        start = rim + points + near
        for at in range(far, 2 * far):
            size = lengths[at + 2]
            to_far_refs[at][slot, :, columns] = rows(start, start + size).astype(jnp.bfloat16)
            start += size

    def finish(pair):
        backward_outputs(pair)
        for at, (ref, out) in enumerate([(att_ref, att_out), (dq_ref, dq_out)]):
            copy = pltpu.make_async_copy(ref.at[pair], out.at[:, columns_of(pair)], sems.at[at, pair])
            copy.start()
            copies.append(copy)

    units = [(pair, part) for pair in range(pairs) for part in range(2)]
    gather_keys(0)
    tops = {units[0]: forward_scores(*units[0])}
    for at, unit in enumerate(units):
        if unit[1] == 0 and unit[0] > 0:
            finish(unit[0] - 1)
        if at + 1 < len(units):
            following = units[at + 1]
            if following[1] == 0:
                gather_keys(following[0])
            tops[following] = forward_scores(*following)
        inverse = forward_probs(*unit, tops.pop(unit))
        delta = forward_outputs(*unit)
        backward_scores(*unit, inverse, delta)
    finish(units[-1][0])
    for copy in copies:
        copy.wait()


def sum_kernel(far_lengths, points, low, high, carried, *refs):
    far = len(far_lengths) // 2
    own_refs, partner_ref, next_ref = refs[:2], refs[2], refs[3]
    far_refs = refs[4 : 4 + 2 * far]
    outs = refs[4 + 2 * far + carried :]
    total, low_ref, sems = outs[-3:]
    near = partner_ref.shape[1]
    first = pl.multiple_of(jnp.where(is_even(), points - near, 0), 8)
    starts = (first, points - near - first)
    copies = []
    for slot in range(2):
        total[...] = own_refs[slot][...]
        for at, ref in enumerate((partner_ref, next_ref)):
            rows = pl.ds(pl.multiple_of(starts[at], 8), near)
            total[rows, :] += ref[slot].astype(jnp.float32)
        for at, (ref, length) in enumerate(zip(far_refs, far_lengths)):
            rows = slice(points - length, points) if at < far else slice(0, length)
            total[rows, :] += ref[slot].astype(jnp.float32)
        low_ref[slot] = total[...].astype(jnp.bfloat16)
        copy = pltpu.make_async_copy(
            low_ref.at[slot], outs[slot].at[:, low * PAIR : high * PAIR], sems.at[slot]
        )
        copy.start()
        copies.append(copy)
    for copy in copies:
        copy.wait()


def chunk_call(kernel, args, carried, count, out_shape, vmem_bytes, **options):
    vmem = pl.BlockSpec(memory_space=pltpu.VMEM)
    anywhere = pl.BlockSpec(memory_space=pl.ANY)
    return pl.pallas_call(
        functools.partial(kernel, len(carried)),
        in_specs=[vmem] * len(args) + [anywhere] * len(carried),
        out_specs=[anywhere] * count + [vmem] * (len(out_shape) - count),
        out_shape=out_shape,
        input_output_aliases={len(args) + at: at for at in range(len(carried))},
        compiler_params=pltpu.CompilerParams(vmem_limit_bytes=vmem_bytes),
        **options,
    )(*args, *carried)


def per_device(queries, keys, values, grad_out, windows):
    points, width = queries.shape
    rim_width, reach = reach_sizes(points, lax.axis_size("band"))
    band = lax.axis_index("band")
    near = min(points, rim_width)
    far = [d for d in range(-reach, reach + 1) if abs(d) > 1]
    far_sizes = [min(points, rim_width - (abs(d) - 1) * points) for d in far]
    lows = len(far) // 2
    lengths = far_sizes[:lows] + [near, near] + far_sizes[lows:]
    wide = points + 2 * padded(rim_width)
    reached = points // 2 + 2 * padded(rim_width)
    relative = (windows - band * points).T

    to_next, from_next, from_partner = [], [], []
    ready = (keys, values)
    for chunk, (low, high) in enumerate(spans(NEXT_CHUNKS)):
        piece = pack(ready, near, low, high)
        to_next.append(piece)
        ready = lax.optimization_barrier((*ready, piece))[:2]
        if chunk > 1:
            piece = lax.optimization_barrier((piece, from_next[chunk - 2]))[0]
        from_next.append(swapped(piece, 1))
        if chunk == 0:
            from_partner = [swapped(field, 0) for field in ready]
        elif chunk == 1:
            ready = lax.optimization_barrier((*ready, *from_partner))[:2]
    from_far = []
    for d, size in zip(far, far_sizes):
        part = slice(points - size, points) if d < 0 else slice(0, size)
        from_far.append(passed_along(jnp.stack([keys[part], values[part]]), -d))

    whole = jax.ShapeDtypeStruct((points, width), jnp.bfloat16)
    outs, own_terms, back_partner, back_next, back_far = [], [], [], [], []
    for chunk, (low, high) in enumerate(spans(CHUNKS)):
        count = high - low
        chunk_width = count * PAIR
        parts = [
            (at, last - first)
            for at, (first, last) in enumerate(spans(NEXT_CHUNKS))
            if low <= first and last <= high
        ]
        next_pairs = [size for _, size in parts]
        assert sum(next_pairs) == count
        outs = chunk_call(
            functools.partial(attention_kernel, rim_width, lengths, points, low, next_pairs),
            [relative, queries, grad_out, keys, values, *from_partner]
            + [from_next[at] for at, _ in parts]
            + from_far,
            outs[:2],
            2,
            [whole] * 2
            + [jax.ShapeDtypeStruct((2, near, chunk_width), jnp.bfloat16)] * 2
            + [jax.ShapeDtypeStruct((points, chunk_width), jnp.float32)] * 2
            + [jax.ShapeDtypeStruct((2, size, chunk_width), jnp.bfloat16) for size in far_sizes],
            48 * wide * points + 12 * 2**20,
            scratch_shapes=[
                pltpu.VMEM((2, reached, points), jnp.float32),
                pltpu.VMEM((2, 2, wide, PAIR), jnp.bfloat16),
                pltpu.VMEM((2, 2, PAIR, wide), jnp.bfloat16),
                pltpu.VMEM((2, 2, reached, points), jnp.float32),
                pltpu.VMEM((2, 2, reached, points), jnp.bfloat16),
                pltpu.VMEM((2, 2, reached, points), jnp.bfloat16),
                pltpu.VMEM((count, points, PAIR), jnp.bfloat16),
                pltpu.VMEM((count, points, PAIR), jnp.bfloat16),
                pltpu.SemaphoreType.DMA((2, count)),
            ],
            cost_estimate=pl.CostEstimate(
                flops=count * 120 * reached * points * PAIR,
                bytes_accessed=count * PAIR * (20 * points + 8 * wide),
                transcendentals=2 * count * points * reached,
            ),
            name=f"attention_{chunk}",
        )
        own_terms.append(outs[4:6])
        back_partner.append(swapped(outs[2], 0))
        back_next.append(swapped(outs[3], 1))
        back_far.append([passed_along(term, d) for term, d in zip(outs[6:], far)])

    grads = []
    for chunk, (low, high) in enumerate(spans(CHUNKS)):
        chunk_width = (high - low) * PAIR
        grads = chunk_call(
            functools.partial(sum_kernel, far_sizes, points, low, high),
            [*own_terms[chunk], back_partner[chunk], back_next[chunk], *back_far[chunk]],
            grads,
            2,
            [whole] * 2,
            12 * 2**20,
            scratch_shapes=[
                pltpu.VMEM((points, chunk_width), jnp.float32),
                pltpu.VMEM((2, points, chunk_width), jnp.bfloat16),
                pltpu.SemaphoreType.DMA((2,)),
            ],
            cost_estimate=pl.CostEstimate(
                flops=6 * points * chunk_width,
                bytes_accessed=20 * points * chunk_width,
                transcendentals=0,
            ),
            name=f"gradient_sums_{chunk}",
        )
    return (outs[0], outs[1], grads[0], grads[1])


def solution(mesh):
    spread = P(("members", "band"), None)
    return jax.shard_map(
        per_device,
        mesh=mesh,
        in_specs=(spread, spread, spread, spread, P("band", None)),
        out_specs=(spread, spread, spread, spread),
        check_vma=False,
    )
```
